32 devices in a mesh: fsdp: 2 (over x), ctx: 4 (over z), tp: 4 (over y, core).
Axes of the slice: x: 2, y: 2, z: 4, core: 2. Of those that a mesh axis runs over, the one named last changes fastest.
Arguments:
- tokens: bfloat16 [3, 2, 1024, 768], P(None, 'fsdp', ('ctx', 'tp')), may hold values from -6 to 6
- positions: int32 [3, 2, 1024], P(None, 'fsdp', 'ctx'), may hold values from 0 to 1535, as said below
- w_query: bfloat16 [768, 768], P('fsdp', 'tp'), may hold values from -0.109375 to 0.109375
- w_key: bfloat16 [768, 768], P('fsdp', 'tp'), may hold values from -0.109375 to 0.109375
- w_value: bfloat16 [768, 768], P('fsdp', 'tp'), may hold values from -0.21875 to 0.21875
- w_out: bfloat16 [768, 768], P('tp', 'fsdp'), may hold values from -1.75 to 1.75
- w_in: bfloat16 [768, 3072], P('fsdp', 'tp'), may hold values from -0.21875 to 0.21875
- w_back: bfloat16 [3072, 768], P('tp', 'fsdp'), may hold values from -0.109375 to 0.109375
- gain_one: bfloat16 [768], P('fsdp'), may hold values from 0.5 to 1.5
- gain_two: bfloat16 [768], P('fsdp'), may hold values from 0.5 to 1.5
- bias_table: bfloat16 [32, 12], P('fsdp', 'tp'), may hold values from -4 to 4
- cotangent: bfloat16 [3, 2, 1024, 768], P(None, 'fsdp', ('ctx', 'tp')), may hold values from -6 to 6
Outputs:
- output: bfloat16 [3, 2, 1024, 768], P(None, 'fsdp', ('ctx', 'tp'))
- input_grad: bfloat16 [3, 2, 1024, 768], P(None, 'fsdp', ('ctx', 'tp'))
- gain_one_grad: float32 [768], P('fsdp')
- gain_two_grad: float32 [768], P('fsdp')
- query_grad: float32 [768, 768], P('fsdp', 'tp')
- key_grad: float32 [768, 768], P('fsdp', 'tp')
- value_grad: float32 [768, 768], P('fsdp', 'tp')
- out_grad: float32 [768, 768], P('tp', 'fsdp')
- in_grad: float32 [768, 3072], P('fsdp', 'tp')
- back_grad: float32 [3072, 768], P('tp', 'fsdp')
- table_grad: float32 [32, 12], P('fsdp', 'tp')
The draws below stay inside these ranges and needn't reach their ends.
Inputs may be any that keep to these rules, and one draw needn't show every extreme that they name: Within each sequence the positions start at 0 and rise by 1 or 2 from one token to the next; exactly 512 of the steps rise by 2, so the last position is 1535.
All inputs are finite; a program needn't handle non-finite values.
Results may differ from the reference program's by a relative error of at most 0.02.
Values may be sent and summed in bfloat16 or wider, within the bound.
A program may use at most 128 MiB of HBM per device.

```python
import math
import jax
import jax.numpy as jnp
from jax import lax

D = 768
HEADS = 12
HDIM = 64
FF = 3072
BUCKETS = 32
MICRO = 3
LEN = 1024
SEQS = 2


def draw_positions(key, part):
    order_rows = jnp.broadcast_to(jnp.arange(LEN - 1, dtype=jnp.int32), (MICRO, SEQS, LEN - 1))
    shuffled = jax.random.permutation(key, order_rows, axis=-1, independent=True)
    increments = 1 + (shuffled < LEN // 2).astype(jnp.int32)
    starting = jnp.zeros((MICRO, SEQS, 1), jnp.int32)
    return jnp.concatenate([starting, jnp.cumsum(increments, axis=-1).astype(jnp.int32)], axis=-1).astype(jnp.int32)


def levels(rng, shape, split, smallest, largest):
    def one(axis_at, parts):
        draws = jax.random.uniform(jax.random.fold_in(jax.random.fold_in(rng, 6), axis_at), (parts,), jnp.float32, smallest / len(split), largest / len(split))
        return jnp.repeat(jnp.exp(draws), shape[axis_at] // parts).reshape((-1,) + (1,) * (len(shape) - axis_at - 1))

    loudness = one(*split[0])
    for cut in split[1:]:
        loudness = loudness * one(*cut)
    return loudness


def gaussian(key, dims, spread, limit, shards=(), held_as=jnp.bfloat16):
    level = levels(key, dims, shards, -0.22, 0.18) if shards else 1.0
    array = jax.random.normal(key, dims, jnp.float32) * spread * level
    return jnp.minimum(jnp.maximum(array, -limit), limit).astype(held_as)


def setup_inputs(seed: int = 0) -> dict:
    keys = jax.random.split(jax.random.key(seed), 13)
    tokens = gaussian(keys[0], (MICRO, SEQS, LEN, D), 1.0, 6.0, ((1, 2), (2, 16)))
    positions = draw_positions(jax.random.fold_in(keys[12], 71), 0)
    w_query = gaussian(keys[2], (D, HEADS * HDIM), (4 * D) ** -0.5, 0.109375, ((0, 2), (1, 4)))
    w_key = gaussian(keys[3], (D, HEADS * HDIM), (4 * D) ** -0.5, 0.109375, ((0, 2), (1, 4)))
    w_value = gaussian(keys[4], (D, HEADS * HDIM), D ** -0.5, 0.21875, ((0, 2), (1, 4)))
    w_out = gaussian(keys[5], (HEADS * HDIM, D), (max(1, D // max(1, LEN // 16))) ** -0.5, 1.75, ((0, 4), (1, 2)))
    w_in = gaussian(keys[6], (D, FF), D ** -0.5, 0.21875, ((0, 2), (1, 4)))
    w_back = gaussian(keys[7], (FF, D), FF ** -0.5, 0.109375, ((0, 4), (1, 2)))
    gain_one = jnp.clip(1.0 + 0.1 * jax.random.normal(keys[8], (D,), jnp.float32), 0.5, 1.5).astype(jnp.bfloat16)
    gain_two = jnp.clip(1.0 + 0.1 * jax.random.normal(keys[9], (D,), jnp.float32), 0.5, 1.5).astype(jnp.bfloat16)
    bias_table = gaussian(keys[10], (BUCKETS, HEADS), 1.0, 4.0, ((0, 2), (1, 4)))
    cotangent = gaussian(keys[11], (MICRO, SEQS, LEN, D), 1.0, 6.0, ((1, 2), (2, 16)))
    return dict(tokens=tokens, positions=positions, w_query=w_query, w_key=w_key, w_value=w_value, w_out=w_out, w_in=w_in, w_back=w_back, gain_one=gain_one, gain_two=gain_two, bias_table=bias_table, cotangent=cotangent)


@jax.custom_vjp
def low(v):
    return lax.optimization_barrier(v.astype(jnp.bfloat16)).astype(jnp.float32)

@jax.custom_vjp
def low_back(v):
    return v

def low_keep(v):
    return (low(v), None)

def low_pass(kept, grad):
    return (grad,)

def back_keep(v):
    return (v, None)

def back_low(kept, grad):
    return (low(grad),)
low.defvjp(low_keep, low_pass)
low_back.defvjp(back_keep, back_low)
epsilon = 1e-06
bucket_edges = (12, 16, 23, 32, 46, 64, 91)
highest = lax.Precision.HIGHEST

def low_both(value_in):
    return low(low_back(value_in))

def bucket_of(query_pos, key_pos):
    relative = (key_pos[None, :] - query_pos[:, None]).astype(jnp.int32)
    magnitude = jnp.abs(relative)
    bucket = jnp.minimum(magnitude, 8)
    for edge_value in bucket_edges:
        bucket = bucket + (magnitude >= edge_value).astype(jnp.int32)
    return (bucket + 16 * (relative > 0).astype(jnp.int32)).astype(jnp.int32)

def inverse_rms(token_rows):
    return lax.rsqrt(lax.optimization_barrier(jnp.mean(token_rows * token_rows, axis=-1, keepdims=True)) + epsilon)

def matmul(left, right):
    return jnp.dot(left, right, precision=highest, preferred_element_type=jnp.float32)

def sequence_layer(params, token_rows, seq_pos):
    w_query, w_key, w_value, w_out, w_in, w_back, gain_one, gain_two, bias_rows = params
    seq_len = token_rows.shape[0]
    normed_one = low(token_rows * inverse_rms(token_rows) * gain_one)
    queries = low_both(matmul(normed_one, w_query)).reshape(seq_len, HEADS, HDIM)
    keys_all = low_both(matmul(normed_one, w_key)).reshape(seq_len, HEADS, HDIM)
    values_all = low_both(matmul(normed_one, w_value)).reshape(seq_len, HEADS, HDIM)
    block_rows = math.gcd(seq_len, 512)

    def attend_block(first_row):
        query_block = lax.dynamic_slice_in_dim(queries, first_row, block_rows, 0)
        pos_block = lax.dynamic_slice_in_dim(seq_pos, first_row, block_rows, 0)
        scores = low_back(jnp.einsum('qhd,khd->hqk', query_block, keys_all, precision=highest))
        scores = scores + jnp.transpose(bias_rows[bucket_of(pos_block, seq_pos)], (2, 0, 1))
        row_peak = lax.optimization_barrier(jnp.max(scores, axis=-1, keepdims=True))
        log_total = row_peak + jnp.log(lax.optimization_barrier(jnp.sum(jnp.exp(scores - row_peak), axis=-1, keepdims=True)))
        probability = low(jnp.exp(scores - log_total))
        return jnp.einsum('hqk,khd->qhd', probability, values_all, precision=highest)
    first_rows = jnp.arange(0, seq_len, block_rows, dtype=jnp.int32)
    attended = lax.map(jax.checkpoint(attend_block), first_rows).reshape(seq_len, HEADS * HDIM)
    attended = low_both(attended)
    middle = token_rows + low_back(matmul(attended, w_out))
    normed_two = low(middle * inverse_rms(middle) * gain_two)
    hidden_pre = low_back(matmul(normed_two, w_in))
    hidden = low(jax.nn.gelu(hidden_pre, approximate=False))
    return middle + matmul(hidden, w_back)

def reference(tokens, positions, w_query, w_key, w_value, w_out, w_in, w_back, gain_one, gain_two, bias_table, cotangent):
    params = tuple((weight_in.astype(jnp.float32) for weight_in in (w_query, w_key, w_value, w_out, w_in, w_back, gain_one, gain_two, bias_table)))
    flat_tokens = tokens.astype(jnp.float32).reshape(MICRO * SEQS, LEN, D)
    flat_pos = positions.reshape(MICRO * SEQS, LEN).astype(jnp.int32)

    def layer(param_set, token_set):

        def one_sequence(pair_items):
            return sequence_layer(param_set, pair_items[0], pair_items[1])
        return lax.map(one_sequence, (token_set, flat_pos))
    output, pullback = jax.vjp(layer, params, flat_tokens)
    param_grads, token_grads = pullback(cotangent.astype(jnp.float32).reshape(MICRO * SEQS, LEN, D))
    full_shape = tokens.shape
    return (output.reshape(full_shape).astype(jnp.bfloat16), token_grads.reshape(full_shape).astype(jnp.bfloat16), param_grads[6], param_grads[7], param_grads[0], param_grads[1], param_grads[2], param_grads[3], param_grads[4], param_grads[5], param_grads[8])
```

```python
import functools
import math

import jax
import jax.numpy as jnp
from jax import lax
from jax.experimental import pallas as pl
from jax.experimental.pallas import tpu as pltpu
from jax.sharding import PartitionSpec as P

D = 768
HDIM = 64


epsilon = 1e-06
bucket_edges = (12, 16, 23, 32, 46, 64, 91)


def bucket_of(query_pos, key_pos):
    relative = (key_pos[None, :] - query_pos[:, None]).astype(jnp.int32)
    magnitude = jnp.abs(relative)
    bucket = jnp.minimum(magnitude, 8)
    for edge_value in bucket_edges:
        bucket = bucket + (magnitude >= edge_value).astype(jnp.int32)
    return bucket + 16 * (relative > 0).astype(jnp.int32)


def table_bias(bucket, bias_rows):
    slot_ids = jnp.arange(bias_rows.shape[0], dtype=jnp.int32)
    matches = bucket[None, :, :, None] == slot_ids[None, None, None, :]
    return jnp.sum(jnp.where(matches, bias_rows.T[:, None, None, :], 0.0), axis=-1)


def table_grad(bucket, grad_scores, bucket_count):
    slot_ids = jnp.arange(bucket_count, dtype=jnp.int32)
    matches = bucket[None, None, :, :] == slot_ids[:, None, None, None]
    return jnp.sum(jnp.where(matches, grad_scores[None], 0.0), axis=(2, 3))


def inverse_rms(token_rows):
    return lax.rsqrt(jnp.mean(token_rows * token_rows, axis=-1, keepdims=True) + epsilon)


def norm_back(token_rows, scale_rows, gain_full, grad_normed):
    weighted = gain_full * grad_normed
    grad_rows = scale_rows * weighted - token_rows * scale_rows**3 * jnp.mean(
        token_rows * weighted, axis=-1, keepdims=True
    )
    return (grad_rows, jnp.sum(grad_normed * token_rows * scale_rows, axis=0))


def gelu_slope(values_in):
    return (
        0.5 * (1.0 + jax.scipy.special.erf(values_in * 0.7071067811865476))
        + values_in * jnp.exp(-0.5 * values_in * values_in) * 0.3989422804014327
    )


def left_product(left, right):
    return jnp.einsum("ra,rb->ab", left, right, preferred_element_type=jnp.float32)


def right_product(left, right):
    return jnp.einsum("ra,ba->rb", left, right, preferred_element_type=jnp.float32)


def spread_rows(local_rows):
    return lax.all_gather(local_rows, "tp", axis=0, tiled=True)


def collect_rows(partial_rows):
    return lax.psum_scatter(
        partial_rows.astype(jnp.bfloat16), "tp", scatter_dimension=0, tiled=True
    ).astype(jnp.float32)


def pair_terms(
    query_block,
    query_pos,
    key_block,
    key_pos,
    value_block,
    grad_att,
    log_total,
    row_delta,
    bias_rows,
):
    bucket = bucket_of(query_pos, key_pos)
    scores = jnp.einsum("qhd,khd->hqk", query_block, key_block, preferred_element_type=jnp.float32)
    scores = scores + table_bias(bucket, bias_rows)
    probability = jnp.exp(scores - log_total[:, :, None])
    grad_prob = jnp.einsum(
        "qhd,khd->hqk", grad_att, value_block, preferred_element_type=jnp.float32
    )
    grad_scores = probability * (grad_prob - row_delta[:, :, None])
    return (bucket, probability, grad_scores)


def make_fold(queries, query_pos, bias_rows, key_rows):
    head_count = queries.shape[1]

    def fold_keys(state_carry, shard_piece, first_row):
        keys_part, values_part, pos_part = shard_piece
        block_count = keys_part.shape[0] // key_rows
        key_blocks = keys_part.reshape(block_count, key_rows, head_count, HDIM)
        value_blocks = values_part.reshape(block_count, key_rows, head_count, HDIM)
        pos_blocks = pos_part.reshape(block_count, key_rows)

        def fold_one_block(inner, block_item):
            run_peak, run_total, run_acc = inner
            key_block, value_block, pos_block = block_item
            scores = jnp.einsum(
                "qhd,khd->hqk", queries, key_block, preferred_element_type=jnp.float32
            )
            scores = scores + table_bias(bucket_of(query_pos, pos_block), bias_rows)
            new_peak = jnp.maximum(run_peak, jnp.max(scores, axis=-1))
            factor = jnp.exp(run_peak - new_peak)
            weights_exp = jnp.exp(scores - new_peak[:, :, None])
            run_total = run_total * factor + jnp.sum(weights_exp, axis=-1)
            run_acc = run_acc * factor[:, :, None] + jnp.einsum(
                "hqk,khd->hqd",
                weights_exp.astype(jnp.bfloat16),
                value_block,
                preferred_element_type=jnp.float32,
            )
            return ((new_peak, run_total, run_acc), None)

        result, unused = lax.scan(
            fold_one_block, state_carry, (key_blocks, value_blocks, pos_blocks)
        )
        return result

    return fold_keys


def attend_back(
    queries,
    query_pos,
    bias_rows,
    keys_all,
    values_all,
    pos_all,
    grad_att,
    log_total,
    row_delta,
    key_rows,
):
    local_len, head_count = (queries.shape[0], queries.shape[1])
    bucket_count = bias_rows.shape[0]
    block_count = keys_all.shape[0] // key_rows
    key_blocks = keys_all.reshape(block_count, key_rows, head_count, HDIM)
    value_blocks = values_all.reshape(block_count, key_rows, head_count, HDIM)
    pos_blocks = pos_all.reshape(block_count, key_rows)

    def attend_one_block(inner, block_item):
        grad_query, grad_bias = inner
        key_block, value_block, pos_block = block_item
        bucket, probability, grad_scores = pair_terms(
            queries,
            query_pos,
            key_block,
            pos_block,
            value_block,
            grad_att,
            log_total,
            row_delta,
            bias_rows,
        )
        grad_bias = grad_bias + table_grad(bucket, grad_scores, bucket_count)
        scores_low = grad_scores.astype(jnp.bfloat16)
        grad_query = grad_query + jnp.einsum(
            "hqk,khd->qhd", scores_low, key_block, preferred_element_type=jnp.float32
        )
        grad_value = jnp.einsum(
            "hqk,qhd->khd",
            probability.astype(jnp.bfloat16),
            grad_att,
            preferred_element_type=jnp.float32,
        )
        grad_key = jnp.einsum(
            "hqk,qhd->khd", scores_low, queries, preferred_element_type=jnp.float32
        )
        return ((grad_query, grad_bias), (grad_key, grad_value))

    start_state = (
        jnp.zeros((local_len, head_count, HDIM), jnp.float32),
        jnp.zeros((bucket_count, head_count), jnp.float32),
    )
    final_state, stacked = lax.scan(
        attend_one_block, start_state, (key_blocks, value_blocks, pos_blocks)
    )
    total_keys = keys_all.shape[0]
    return (
        final_state[0],
        final_state[1],
        stacked[0].reshape(total_keys, head_count * HDIM),
        stacked[1].reshape(total_keys, head_count * HDIM),
    )


def own_share(grad_term, grad_dim):
    share_len = grad_term.shape[grad_dim] // lax.axis_size("fsdp")
    return lax.dynamic_slice_in_dim(
        grad_term, lax.axis_index("fsdp") * share_len, share_len, grad_dim
    )


def per_device_plain(
    tokens,
    positions,
    w_query,
    w_key,
    w_value,
    w_out,
    w_in,
    w_back,
    gain_one,
    gain_two,
    bias_table,
    cotangent,
):
    micro_count = tokens.shape[0]
    head_count = w_query.shape[1] // HDIM
    head_cols = head_count * HDIM
    hidden_cols = w_in.shape[1]
    bucket_count = bias_table.shape[0] * lax.axis_size("fsdp")
    grad_wq = jnp.zeros((D, head_cols), jnp.float32)
    grad_wk = jnp.zeros((D, head_cols), jnp.float32)
    grad_wv = jnp.zeros((D, head_cols), jnp.float32)
    grad_wo = jnp.zeros((head_cols, D), jnp.float32)
    grad_wi = jnp.zeros((D, hidden_cols), jnp.float32)
    grad_wb = jnp.zeros((hidden_cols, D), jnp.float32)
    grad_table = jnp.zeros((bucket_count, head_count), jnp.float32)
    grad_gain_one = jnp.zeros((D,), jnp.float32)
    grad_gain_two = jnp.zeros((D,), jnp.float32)
    outputs = []
    input_grads = []
    for micro_step in range(micro_count):
        full_wq, full_wk, full_wv, full_wo, full_wi, full_wb, full_g1, full_g2, full_table = (
            lax.all_gather(w_query, "fsdp", axis=0, tiled=True),
            lax.all_gather(w_key, "fsdp", axis=0, tiled=True),
            lax.all_gather(w_value, "fsdp", axis=0, tiled=True),
            lax.all_gather(w_out, "fsdp", axis=1, tiled=True),
            lax.all_gather(w_in, "fsdp", axis=0, tiled=True),
            lax.all_gather(w_back, "fsdp", axis=1, tiled=True),
            lax.all_gather(gain_one, "fsdp", axis=0, tiled=True),
            lax.all_gather(gain_two, "fsdp", axis=0, tiled=True),
            lax.all_gather(bias_table, "fsdp", axis=0, tiled=True),
        )
        gain_first = full_g1.astype(jnp.float32)
        gain_second = full_g2.astype(jnp.float32)
        bias_rows = full_table.astype(jnp.float32)
        token_rows = tokens[micro_step, 0].astype(jnp.float32)
        query_pos = positions[micro_step, 0]
        scale_one = inverse_rms(token_rows)
        normed = spread_rows((token_rows * scale_one * gain_first).astype(jnp.bfloat16))
        local_len = normed.shape[0]
        key_rows = math.gcd(local_len, 256)
        queries_low = jnp.dot(normed, full_wq, preferred_element_type=jnp.float32).astype(
            jnp.bfloat16
        )
        keys_low = jnp.dot(normed, full_wk, preferred_element_type=jnp.float32).astype(jnp.bfloat16)
        values_low = jnp.dot(normed, full_wv, preferred_element_type=jnp.float32).astype(
            jnp.bfloat16
        )
        queries = queries_low.reshape(local_len, head_count, HDIM)
        start_state = (
            jnp.full((head_count, local_len), -1e30, jnp.float32),
            jnp.zeros((head_count, local_len), jnp.float32),
            jnp.zeros((head_count, local_len, HDIM), jnp.float32),
        )
        fold_keys = make_fold(queries, query_pos, bias_rows, key_rows)
        run_peak, run_total, run_acc = fold_keys(
            start_state,
            (
                lax.all_gather(keys_low, "ctx", axis=0, tiled=True),
                lax.all_gather(values_low, "ctx", axis=0, tiled=True),
                lax.all_gather(query_pos, "ctx", axis=0, tiled=True),
            ),
            jnp.int32(0),
        )
        log_total = run_peak + jnp.log(run_total)
        attended_f = jnp.transpose(run_acc / run_total[:, :, None], (1, 0, 2)).reshape(
            local_len, head_cols
        )
        attended = attended_f.astype(jnp.bfloat16)
        middle = token_rows + collect_rows(
            jnp.dot(attended, full_wo, preferred_element_type=jnp.float32)
        )
        scale_two = inverse_rms(middle)
        normed_two = spread_rows((middle * scale_two * gain_second).astype(jnp.bfloat16))
        hidden_pre = jnp.dot(normed_two, full_wi, preferred_element_type=jnp.float32)
        hidden = jax.nn.gelu(hidden_pre, approximate=False).astype(jnp.bfloat16)
        output_rows = middle + collect_rows(
            jnp.dot(hidden, full_wb, preferred_element_type=jnp.float32)
        )
        outputs.append(output_rows.astype(jnp.bfloat16))
        grad_local = cotangent[micro_step, 0]
        grad_full = spread_rows(grad_local)
        grad_wb = grad_wb + left_product(hidden, grad_full)
        grad_hidden = right_product(grad_full, full_wb)
        grad_pre = (grad_hidden * gelu_slope(hidden_pre)).astype(jnp.bfloat16)
        grad_wi = grad_wi + left_product(normed_two, grad_pre)
        grad_normed_two = collect_rows(right_product(grad_pre, full_wi))
        grad_middle, gain_part_two = norm_back(middle, scale_two, gain_second, grad_normed_two)
        grad_middle = grad_middle + grad_local.astype(jnp.float32)
        grad_gain_two = grad_gain_two + gain_part_two
        grad_mixed = spread_rows(grad_middle.astype(jnp.bfloat16))
        grad_wo = grad_wo + left_product(attended, grad_mixed)
        grad_attended = right_product(grad_mixed, full_wo).astype(jnp.bfloat16)
        row_delta = jnp.sum(
            (grad_attended.astype(jnp.float32) * attended_f).reshape(local_len, head_count, HDIM),
            axis=-1,
        ).T
        back_keys, back_values, back_pos = (
            lax.all_gather(keys_low, "ctx", axis=0, tiled=True),
            lax.all_gather(values_low, "ctx", axis=0, tiled=True),
            lax.all_gather(query_pos, "ctx", axis=0, tiled=True),
        )
        grad_att_heads = grad_attended.reshape(local_len, head_count, HDIM)
        grad_queries, table_part, grad_keys_all, grad_values_all = attend_back(
            queries,
            query_pos,
            bias_rows,
            back_keys,
            back_values,
            back_pos,
            grad_att_heads,
            log_total,
            row_delta,
            key_rows,
        )
        grad_keys, grad_values = (
            lax.psum_scatter(
                grad_keys_all.astype(jnp.bfloat16), "ctx", scatter_dimension=0, tiled=True
            ).astype(jnp.float32),
            lax.psum_scatter(
                grad_values_all.astype(jnp.bfloat16), "ctx", scatter_dimension=0, tiled=True
            ).astype(jnp.float32),
        )
        grad_table = grad_table + table_part
        grad_q_low = grad_queries.reshape(local_len, head_cols).astype(jnp.bfloat16)
        grad_k_low = grad_keys.astype(jnp.bfloat16)
        grad_v_low = grad_values.astype(jnp.bfloat16)
        grad_wq = grad_wq + left_product(normed, grad_q_low)
        grad_wk = grad_wk + left_product(normed, grad_k_low)
        grad_wv = grad_wv + left_product(normed, grad_v_low)
        grad_normed = collect_rows(
            right_product(grad_q_low, full_wq)
            + right_product(grad_k_low, full_wk)
            + right_product(grad_v_low, full_wv)
        )
        grad_input, gain_part_one = norm_back(token_rows, scale_one, gain_first, grad_normed)
        grad_gain_one = grad_gain_one + gain_part_one
        input_grads.append((grad_input + grad_middle).astype(jnp.bfloat16))
    gain_total_one, gain_total_two = lax.psum((grad_gain_one, grad_gain_two), ("fsdp", "ctx", "tp"))
    sum_wq, sum_wk, sum_wv, sum_wo, sum_wi, sum_wb, sum_table = lax.psum(
        (grad_wq, grad_wk, grad_wv, grad_wo, grad_wi, grad_wb, grad_table), ("fsdp", "ctx")
    )
    share_wq = own_share(sum_wq, 0)
    share_wk = own_share(sum_wk, 0)
    share_wv = own_share(sum_wv, 0)
    share_wo = own_share(sum_wo, 1)
    share_wi = own_share(sum_wi, 0)
    share_wb = own_share(sum_wb, 1)
    share_table = own_share(sum_table, 0)
    return (
        jnp.stack(outputs)[:, None],
        jnp.stack(input_grads)[:, None],
        own_share(gain_total_one, 0),
        own_share(gain_total_two, 0),
        share_wq,
        share_wk,
        share_wv,
        share_wo,
        share_wi,
        share_wb,
        share_table,
    )


MESH = pl.DeviceIdType.MESH
F32 = jnp.float32
BF16 = jnp.bfloat16
HEADS_HERE = 3
BLK = 128
VALUE_ROWS = (128, 192, 64)


def nn(left, right):
    return lax.dot_general(left, right, (((1,), (0,)), ((), ())), preferred_element_type=F32)


def nt(left, right):
    return lax.dot_general(left, right, (((1,), (1,)), ((), ())), preferred_element_type=F32)


def tn(left, right):
    return lax.dot_general(left, right, (((0,), (0,)), ((), ())), preferred_element_type=F32)


def at_rows(offset, size, unit):
    return pl.ds(pl.multiple_of(offset, unit), size)


def fold_rows(block):
    return jnp.sum(block.reshape(block.shape[0] // 8, 8, block.shape[1]), axis=0)


class Sems:
    def __init__(self):
        self.numbers = {}

    def __call__(self, *name):
        return self.numbers.setdefault(name, len(self.numbers))


def grad_chunks(share, hidden):
    half = hidden // 2
    chunks, row = [], 0
    for name, rows, cols in (
        ("back0", half, share),
        ("back1", half, share),
        ("in0", share, half),
        ("in1", share, half),
        ("out", HEADS_HERE * HDIM, share),
        ("kv", share, 384),
        ("q", share, 256),
    ):
        chunks.append((name, row, rows, cols))
        row += rows
    return chunks, row


def layer_kernel(
    nf, nc, micro, rows_own, share, hidden, n_sems, sems,
    tok, pos_in, cot, wqkv_loc, wo_loc, wi_loc, wb_loc, small_loc,
    out, grad_in, grads_out, small_out,
    wqkv, wo, wi, wb, small_rx, smallf, n1, g, posb, bkt, bias, qm, kv, e_t, s_t, ds_t, att_t,
    inv, att, scr, keep, keep6, send1, send2, recv1, recv2, zsend, zrecv, gz, n2, hid, gp, gm,
    mid_f, gmid, dq, dom, nds, tacc, facc, gain2, xs, xr, zr1, zr2, tot, sm, smr,
    ssem, rsem, lsem,
):
    f, c, t = lax.axis_index("fsdp"), lax.axis_index("ctx"), lax.axis_index("tp")
    nt_ = 4
    T = rows_own
    R = nt_ * T
    L = nc * R
    NB = L // BLK
    t1 = t + 1 - 2 * lax.rem(t, 2)
    t2 = lax.rem(t + 2, 4)
    t3 = lax.rem(t1 + 2, 4)
    sib, ypeer = (f, c, t1), (f, c, t2)
    xpeers = [(lax.rem(f + j, nf), c, t) for j in range(1, nf)]
    zpeers = [(f, lax.rem(c + k, nc), t) for k in range(1, nc)]
    half_c = nc // 2
    low_side = c < half_c
    inward = jnp.where(low_side, c + 1, c - 1)
    outward = jnp.clip(jnp.where(low_side, c - 1, c + 1), 0, nc - 1)
    is_mid = (c == half_c - 1) | (c == half_c)
    has_out = (c > 0) & (c < nc - 1)
    if nc == 2:
        has_out = c < 0
    chunks, chunk_rows = grad_chunks(share, hidden)
    pending = []
    zs = xs.at[0]

    def send(src, dst, name_s, name_r, dev, when=None):
        copy = pltpu.make_async_remote_copy(
            src, dst, ssem.at[sems(*name_s)], rsem.at[sems(*name_r)], device_id=dev, device_id_type=MESH
        )
        if when is None:
            copy.start()
        else:
            pl.when(when)(copy.start)
        pending.append((name_s, copy, when))

    def sent(*name_s):
        for at, (name, copy, when) in enumerate(pending):
            if name == name_s:
                if when is None:
                    copy.wait_send()
                else:
                    pl.when(when)(copy.wait_send)
                del pending[at]
                return

    def arrived(dst, *name_r):
        pltpu.make_async_remote_copy(
            dst, dst, ssem.at[sems(*name_r)], rsem.at[sems(*name_r)], device_id=sib, device_id_type=MESH
        ).wait_recv()

    def rms(rows):
        return lax.rsqrt(jnp.mean(rows * rows, axis=-1, keepdims=True) + epsilon)

    def piece(buf, m, block, t_of):
        return buf.at[m, at_rows(block * R + t_of * T, T, T)]

    for m in range(micro):
        rows = tok[m].astype(F32)
        n1[m, at_rows(c * R + t * T, T, T)] = (rows * rms(rows)).astype(BF16)
    dom[...] = jnp.zeros_like(dom)
    tacc[...] = jnp.zeros_like(tacc)
    facc[...] = jnp.zeros_like(facc)
    posb[0] = jnp.zeros_like(posb[0])
    posb[2] = jnp.zeros_like(posb[2])
    posb[1] = pos_in[...]
    local = []

    def local_copy(src, dst, i):
        copy = pltpu.make_async_copy(src, dst, lsem.at[i])
        copy.start()
        local.append(copy)

    share_cols = at_rows(f * share, share, BLK)
    share_rows = at_rows(f * share, share, BLK)
    own_rows = at_rows(t * T, T, T)
    local_copy(wo_loc.at[pl.ds(0, 128)], wo.at[pl.ds(128, 128), share_cols], 0)
    local_copy(wo_loc.at[pl.ds(128, 64)], wo.at[pl.ds(64, 64), share_cols], 1)
    local_copy(wi_loc, wi.at[share_rows], 2)
    local_copy(wb_loc, wb.at[:, share_cols], 3)
    for m in range(micro):
        local_copy(cot.at[m], g.at[m, own_rows], 4 + m)
    wo[pl.ds(0, 64)] = jnp.zeros((64, D), BF16)

    barrier = pltpu.get_barrier_semaphore()
    peers = [sib, ypeer] + xpeers + zpeers
    for dev in peers:
        pl.semaphore_signal(barrier, inc=1, device_id=dev, device_id_type=MESH)
    pl.semaphore_wait(barrier, len(peers))

    def spread_first(m):
        mine = piece(n1, m, c, t)
        send(mine, mine, ("ny", m, 0), ("ny", m, 0), ypeer)
        for k in range(1, nc):
            send(mine, mine, ("nz", m, k), ("nz", m, nc - k), zpeers[k - 1])
        send(mine, mine, ("ns", m, 0), ("ns", m, 0), sib)

    spread_first(0)
    for j, dev in enumerate(xpeers):
        send(wqkv_loc, wqkv.at[share_rows], ("wqkv", j), ("wqkv", nf - 2 - j), dev)
        send(small_loc, small_rx.at[f], ("small", j), ("small", nf - 2 - j), dev)
    send(pos_in, posb.at[0], ("posu",), ("posu",), (f, jnp.minimum(c + 1, nc - 1), t), c < nc - 1)
    send(pos_in, posb.at[2], ("posd",), ("posd",), (f, jnp.maximum(c - 1, 0), t), c > 0)
    for m in range(1, micro):
        spread_first(m)
    for j, dev in enumerate(xpeers):
        send(wo_loc.at[pl.ds(0, 128)], wo.at[pl.ds(128, 128), share_cols], ("woa", j), ("woa", nf - 2 - j), dev)
        send(wo_loc.at[pl.ds(128, 64)], wo.at[pl.ds(64, 64), share_cols], ("wob", j), ("wob", nf - 2 - j), dev)
        send(wi_loc, wi.at[share_rows], ("wi", j), ("wi", nf - 2 - j), dev)
        send(wb_loc, wb.at[:, share_cols], ("wb", j), ("wb", nf - 2 - j), dev)
    wqkv[share_rows] = wqkv_loc[...]
    small_rx[f] = small_loc[...]

    def spread_own(name, buf, m):
        mine = buf.at[m, own_rows]
        send(mine, mine, (name, "y", m), (name, "y", m), ypeer)
        send(mine, mine, (name, "s", m), (name, "s", m), sib)

    def spread_on(name, buf, m):
        there = buf.at[m, at_rows(t2 * T, T, T)]
        arrived(there, name, "y", m)
        send(there, there, (name, "f", m), (name, "f", m), sib)

    def spread_end(name, buf, m):
        arrived(buf.at[m, at_rows(t1 * T, T, T)], name, "s", m)
        arrived(buf.at[m, at_rows(t3 * T, T, T)], name, "f", m)

    def gather_z(m, k):
        z = lax.rem(c + k, nc)
        there = piece(n1, m, z, t)
        arrived(there, "nz", m, k)
        send(there, there, ("ny", m, k), ("ny", m, k), ypeer)
        send(there, there, ("ns", m, k), ("ns", m, k), sib)

    def gather_y(m, k):
        z = lax.rem(c + k, nc)
        there = piece(n1, m, z, t2)
        arrived(there, "ny", m, k)
        send(there, there, ("nf", m, k), ("nf", m, k), sib)

    order = [k for pair in zip(range(1, nc), range(nc - 1, 0, -1)) for k in pair]
    order = list(dict.fromkeys(order))

    def gather(m):
        gather_y(m, 0)
        for at, k in enumerate(order):
            gather_z(m, k)
            if at >= 1:
                gather_y(m, order[at - 1])
        gather_y(m, order[-1])

    def gather_end(m):
        for k in range(nc):
            z = lax.rem(c + k, nc)
            arrived(piece(n1, m, z, t1), "ns", m, k)
            arrived(piece(n1, m, z, t3), "nf", m, k)

    def take_small():
        for j in range(nf - 1):
            arrived(small_rx.at[lax.rem(f + 1 + j, nf)], "small", j)
        total = small_rx[0]
        for j in range(1, nf):
            total = total + small_rx[j]
        smallf[...] = total

    def positions_and_bias():
        @pl.when(c > 0)
        def _():
            arrived(posb.at[0], "posu")

        @pl.when(c < nc - 1)
        def _():
            arrived(posb.at[2], "posd")

        def one(m, unused):
            for qb in range(2):
                query_row = posb[1, m, qb : qb + 1, :]
                for d in (-1, 0, 1):
                    slot, row = ((0, 1), (1, 0), (1, 1), (2, 0))[qb + d + 1]
                    key_row = posb[slot, m, row : row + 1, :]
                    key_col = jnp.transpose(jnp.broadcast_to(key_row, (BLK, BLK)))
                    relative = key_col - query_row
                    size = jnp.abs(relative)
                    bucket = jnp.minimum(size, 8)
                    for edge_value in bucket_edges:
                        bucket = bucket + (size >= edge_value).astype(jnp.int32)
                    bucket = bucket + 16 * (relative > 0).astype(jnp.int32)
                    sub = qb * 3 + d + 1
                    bkt[m, sub] = bucket
                    for h in range(HEADS_HERE):
                        row_of = jnp.broadcast_to(smallf[h : h + 1, pl.ds(D, 128)], (BLK, BLK))
                        bias[m, sub, h] = jnp.take_along_axis(row_of, bucket, axis=1).astype(BF16)
            return unused

        lax.fori_loop(0, micro, one, 0)

    def fold_gain():
        for j in range(nf - 1):
            peer = lax.rem(f + 1 + j, nf)
            arrived(wqkv.at[at_rows(peer * share, share, BLK)], "wqkv", j)

        def one(i, unused):
            r = at_rows(i * BLK, BLK, BLK)
            col = jnp.transpose(jnp.broadcast_to(smallf[0:1, r], (BLK, BLK)))
            for j in range(5):
                cols = pl.ds(j * BLK, BLK)
                wqkv[r, cols] = (wqkv[r, cols].astype(F32) * col).astype(BF16)
            return unused

        lax.fori_loop(0, D // BLK, one, 0)

    def reduce_start(slot, rid, kept, value, previous):
        scr[...] = value
        if previous is not None:
            sent("r1", previous)
        send1[slot, 0] = scr[at_rows(t1 * T, T, T)].astype(BF16)
        send1[slot, 1] = scr[at_rows(t3 * T, T, T)].astype(BF16)
        send(send1.at[slot], recv1.at[rid], ("r1", rid), ("r1", rid), sib)
        kept[0] = scr[own_rows].astype(kept.dtype)
        kept[1] = scr[at_rows(t2 * T, T, T)].astype(kept.dtype)

    def reduce_mid(slot, rid, kept, previous):
        arrived(recv1.at[rid], "r1", rid)
        if previous is not None:
            sent("r2", previous)
        send2[slot] = (kept[1].astype(F32) + recv1[rid, 1].astype(F32)).astype(BF16)
        send(send2.at[slot], recv2.at[rid], ("r2", rid), ("r2", rid), ypeer)
        kept[0] = (kept[0].astype(F32) + recv1[rid, 0].astype(F32)).astype(kept.dtype)

    def reduce_end(rid, kept):
        arrived(recv2.at[rid], "r2", rid)
        return kept[0].astype(F32) + recv2[rid].astype(F32)

    def phase(p, m):
        rid = p * micro + m
        return p, rid, keep.at[rid], (rid - 1 if m > 0 else None)

    def start_phase(p, m, value):
        slot, rid, kept, previous = phase(p, m)
        reduce_start(slot, rid, kept, value, previous)

    def mid_phase(p, m):
        slot, rid, kept, previous = phase(p, m)
        reduce_mid(slot, rid, kept, previous)

    def end_phase(p, m):
        slot, rid, kept, previous = phase(p, m)
        return reduce_end(rid, kept)

    def attend(m):
        own = at_rows(c * R, R, R)
        queries = nn(n1[m, own], wqkv[:, 0:256])
        lane = lax.broadcasted_iota(jnp.int32, (R, 256), 1)
        for h in range(HEADS_HERE):
            keep_it = (lane >= h * HDIM) & (lane < (h + 1) * HDIM)
            qm[m, pl.ds(h * R, R)] = jnp.where(keep_it, queries, 0.0).astype(BF16)

        def one_block(z, unused):
            r = at_rows(z * R, R, R)
            kv[m, r] = nn(n1[m, r], wqkv[:, 256:640]).astype(BF16)
            return unused

        lax.fori_loop(0, nc, one_block, 0)
        for h in range(HEADS_HERE):
            cols = pl.ds(h * R, R)
            below = smallf[h : h + 1, pl.ds(D, 128)][:, 15:16]
            above = smallf[h : h + 1, pl.ds(D, 128)][:, 31:32]

            def scores(kb, unused):
                r = at_rows(kb * BLK, BLK, BLK)
                block = nt(kv[m, r, 0:256], qm[m, cols])
                for qb in range(2):
                    d = kb - 2 * c - qb
                    far = jnp.where(d < -1, below, jnp.where(d > 1, above, 0.0))
                    s_t[r, pl.ds(qb * BLK, BLK)] = block[:, qb * BLK : (qb + 1) * BLK] + far
                return unused

            lax.fori_loop(0, NB, scores, 0)
            for qb in range(2):
                for d in (-1, 0, 1):
                    kb = 2 * c + qb + d

                    def near(kb=kb, qb=qb, d=d):
                        r = at_rows(kb * BLK, BLK, BLK)
                        q = pl.ds(qb * BLK, BLK)
                        s_t[r, q] = s_t[r, q] + bias[m, qb * 3 + d + 1, h].astype(F32)

                    if qb + d in (0, 1):
                        near()
                    else:
                        pl.when((kb >= 0) & (kb < NB))(near)

            def peak(kb, top):
                block = s_t[at_rows(kb * BLK, BLK, BLK)]
                return jnp.maximum(top, jnp.max(block.reshape(BLK // 8, 8, R), axis=0))

            top = lax.fori_loop(0, NB, peak, jnp.full((8, R), -jnp.inf, F32))
            top = jnp.max(top, axis=0, keepdims=True)

            def expo(kb, total):
                r = at_rows(kb * BLK, BLK, BLK)
                weights = jnp.exp(s_t[r] - top)
                e_t[m, r, cols] = weights.astype(BF16)
                return total + fold_rows(weights)

            total = lax.fori_loop(0, NB, expo, jnp.zeros((8, R), F32))
            over = 1.0 / jnp.sum(total, axis=0, keepdims=True)
            inv[m * HEADS_HERE + h] = jnp.broadcast_to(over, (8, R))
            mixed = tn(kv[m, :, 128:384], e_t[m, :, cols])
            v0 = VALUE_ROWS[h]
            att_t[m, pl.ds(v0, HDIM)] = mixed[v0 : v0 + HDIM] * over
        att_t[m, pl.ds(0, HDIM)] = jnp.zeros((HDIM, R), F32)
        attended = jnp.transpose(att_t[m]).astype(BF16)
        att[pl.ds(m * R, R)] = attended
        return attended

    def attend_and_mix(m):
        attended = attend(m)
        start_phase(0, m, nn(attended, wo[...]))

    def take_wo():
        local[0].wait()
        local[1].wait()
        for j in range(nf - 1):
            cols = at_rows(lax.rem(f + 1 + j, nf) * share, share, BLK)
            arrived(wo.at[pl.ds(128, 128), cols], "woa", j)
            arrived(wo.at[pl.ds(64, 64), cols], "wob", j)

    def take_ff():
        local[2].wait()
        local[3].wait()
        for j in range(nf - 1):
            peer = at_rows(lax.rem(f + 1 + j, nf) * share, share, BLK)
            arrived(wi.at[peer], "wi", j)
            arrived(wb.at[:, peer], "wb", j)

    def norm_two(m):
        middle = tok[m].astype(F32) + end_phase(0, m)
        mid_f[m] = middle
        n2[m, own_rows] = (middle * rms(middle) * smallf[1:2, 0:D]).astype(BF16)
        spread_own("n2", n2, m)

    def feed(m):
        spread_end("n2", n2, m)
        rows = n2[m]

        def one(i, unused):
            cols = at_rows(i * 256, 256, 256)
            pre = nn(rows, wi[:, cols])
            slope = nt(g[m], wb[cols])
            bell = 0.5 * (1.0 + lax.erf(pre * 0.7071067811865476))
            hid[m, :, cols] = (pre * bell).astype(BF16)
            bell = bell + pre * jnp.exp(-0.5 * pre * pre) * 0.3989422804014327
            gp[m, :, cols] = (slope * bell).astype(BF16)
            return unused

        lax.fori_loop(0, hidden // 256, one, 0)
        start_phase(1, m, nt(gp[m], wi[...]))
        start_phase(2, m, nn(hid[m], wb[...]))

    def output_rows(m):
        out[m] = (mid_f[m] + end_phase(2, m)).astype(BF16)

    def back_two(m):
        grad_normed = end_phase(1, m)
        middle = mid_f[m]
        scale = rms(middle)
        unit = middle * scale
        part = fold_rows(grad_normed * unit)
        gain2[...] = part if m == 0 else gain2[...] + part
        weighted = smallf[1:2, 0:D] * grad_normed
        grad = scale * (weighted - unit * jnp.mean(unit * weighted, axis=-1, keepdims=True))
        grad = grad + g[m, own_rows].astype(F32)
        gmid[m] = grad
        gm[m, own_rows] = grad.astype(BF16)
        spread_own("gm", gm, m)

    def attend_back(m):
        spread_end("gm", gm, m)
        grad_att = nt(wo[...], gm[m]).astype(BF16).astype(F32)
        deltas = []
        for h in range(HEADS_HERE):
            v0 = VALUE_ROWS[h]
            scaled = (grad_att[v0 : v0 + HDIM] * inv[m * HEADS_HERE + h, 0:1, :]).astype(BF16)
            dom[pl.ds(v0, HDIM), pl.ds(h * R, R)] = scaled
            deltas.append(jnp.sum(scaled.astype(F32) * att_t[m, pl.ds(v0, HDIM)], axis=0, keepdims=True))

        def one_block(kb, unused):
            r = at_rows(kb * BLK, BLK, BLK)
            for h in range(HEADS_HERE):
                cols = pl.ds(h * R, R)
                grad_prob = nn(kv[m, r, 128:384], dom[:, cols])
                grad = e_t[m, r, cols].astype(F32) * (grad_prob - deltas[h])
                ds_t[r, cols] = grad.astype(BF16)
                part = fold_rows(grad)
                rel = kb - 2 * c + 1
                low, high = part[:, 0:BLK], part[:, BLK:]
                facc[h, 0] += jnp.where(rel < 0, low, 0.0) + jnp.where(rel < 1, high, 0.0)
                facc[h, 1] += jnp.where(rel > 2, low, 0.0) + jnp.where(rel > 3, high, 0.0)

                @pl.when((rel >= 0) & (rel < 4))
                def _():
                    nds[jnp.clip(rel, 0, 3), :, cols] = grad

            return unused

        lax.fori_loop(0, NB, one_block, 0)
        columns = []
        for h in range(HEADS_HERE):
            grad_q = tn(kv[m, :, 0:256], ds_t[:, pl.ds(h * R, R)])
            columns.append(grad_q[h * HDIM : (h + 1) * HDIM])
        columns.append(jnp.zeros((HDIM, R), F32))
        dq[m] = jnp.transpose(jnp.concatenate(columns, axis=0)).astype(BF16)

        def one_grad(z, unused):
            r = at_rows(z * R, R, R)
            grad_k = nn(ds_t[r], qm[m])
            grad_v = nt(e_t[m, r], dom[...])
            kv[m, r, 0:128] = grad_k[:, 0:128].astype(BF16)
            kv[m, r, 128:256] = (grad_k[:, 128:256] + grad_v[:, 0:128]).astype(BF16)
            kv[m, r, 256:384] = grad_v[:, 128:256].astype(BF16)
            return unused

        lax.fori_loop(0, nc, one_grad, 0)

    def bin_table(m):
        for qb in range(2):
            for d in (-1, 0, 1):
                rel = qb + d + 1
                sub = qb * 3 + d + 1

                def one(b, unused, rel=rel, sub=sub, qb=qb):
                    same = bkt[m, sub] == b
                    for h in range(HEADS_HERE):
                        block = nds[rel, :, pl.ds(h * R + qb * BLK, BLK)]
                        tacc[h, b] += fold_rows(jnp.where(same, block, 0.0))
                    return unused

                first, last = {-1: (1, 16), 0: (0, 32), 1: (17, 32)}[d]

                def run(first=first, last=last, one=one):
                    lax.fori_loop(first, last, one, 0)

                if rel in (1, 2):
                    run()
                else:
                    pl.when((2 * c + rel - 1 >= 0) & (2 * c + rel - 1 < NB))(run)

    def six(m, k):
        return 3 + k, 3 * micro + m * nc + k, keep6.at[m * nc + k], (3 * micro + (m - 1) * nc + k if m > 0 else None)

    def back_start(m, k):
        r = at_rows(lax.rem(c + k, nc) * R, R, R)
        value = nt(kv[m, r], wqkv[:, 256:640])
        if k == 0:
            value = value + nt(dq[m], wqkv[:, 0:256])
        slot, rid, kept, previous = six(m, k)
        reduce_start(slot, rid, kept, value, previous)

    def back_mid(m, k):
        slot, rid, kept, previous = six(m, k)
        reduce_mid(slot, rid, kept, previous)

    def back_out(m, k):
        slot, rid, kept, previous = six(m, k)
        total = reduce_end(rid, kept)
        if k == 0:
            gz[m] = total
        else:
            zsend[m, k - 1] = total.astype(BF16)
            send(zsend.at[m, k - 1], zrecv.at[m, nc - k - 1], ("gz", m, k), ("gz", m, nc - k), zpeers[k - 1])

    def back_one(m):
        weighted = gz[m]
        for k in range(1, nc):
            arrived(zrecv.at[m, k - 1], "gz", m, k)
            weighted = weighted + zrecv[m, k - 1].astype(F32)
        rows = tok[m].astype(F32)
        scale = rms(rows)
        unit = rows * scale
        grad = scale * (weighted - unit * jnp.mean(unit * weighted, axis=-1, keepdims=True))
        grad_in[m] = (gmid[m] + grad).astype(BF16)

    all_rows = micro * R

    def grad_of(name, part, i):
        r = at_rows(i * BLK, BLK, BLK)
        share_at = at_rows(part, share, BLK)
        if name in ("back0", "back1"):
            at = at_rows(int(name[-1]) * (hidden // 2) + i * BLK, BLK, BLK)
            return sum(tn(hid[m, :, at], g[m, :, share_at]) for m in range(micro))
        if name in ("in0", "in1"):
            at = at_rows(part + i * BLK, BLK, BLK)
            cols = pl.ds(int(name[-1]) * (hidden // 2), hidden // 2)
            return sum(tn(n2[m, :, at], gp[m, :, cols]) for m in range(micro))
        at = at_rows(part + i * BLK, BLK, BLK)
        if name == "kv":
            return sum(tn(n1[m, :, at], kv[m]) for m in range(micro))
        own = at_rows(c * R, R, R)
        return sum(tn(n1[m, own, at], dq[m]) for m in range(micro))

    def out_grad(part):
        share_at = at_rows(part, share, BLK)
        return [
            sum(
                tn(att[pl.ds(m * R, R), pl.ds(at, size)], gm[m, :, share_at]) for m in range(micro)
            )
            for at, size in ((128, 128), (64, 64))
        ]

    def each_part(chunk, part, use):
        name, row, rows, cols = chunk
        if name == "out":
            first, second = out_grad(part)
            use(row, 128, first)
            use(row + 128, 64, second)
            return

        def one(i, unused):
            use(pl.multiple_of(row + i * BLK, 64), BLK, grad_of(name, part, i))
            return unused

        lax.fori_loop(0, rows // BLK, one, 0)

    def share_out(q):
        chunk = chunks[q]
        name, row, rows, cols = chunk
        for j, dev in enumerate(xpeers):
            part = lax.rem(f + 1 + j, nf) * share

            def use(at, size, value, j=j):
                xs[j, pl.ds(at, size), 0:cols] = value.astype(BF16)

            each_part(chunk, part, use)
            src = xs.at[j, pl.ds(row, rows), pl.ds(0, cols)]
            dst = xr.at[nf - 2 - j, pl.ds(row, rows), pl.ds(0, cols)]
            send(src, dst, ("x", q, j), ("x", q, nf - 2 - j), dev)

    def own_share(q):
        chunk = chunks[q]
        name, row, rows, cols = chunk
        for j in range(nf - 1):
            arrived(xr.at[j, pl.ds(row, rows), pl.ds(0, cols)], "x", q, j)
        sent("x", q, 0)

        def use(at, size, value):
            for j in range(nf - 1):
                value = value + xr[j, pl.ds(at, size), 0:cols].astype(F32)
            zs[pl.ds(at, size), 0:cols] = value.astype(BF16)
            if name in ("q", "kv"):
                i = pl.multiple_of(at - row, BLK)
                first = 0 if name == "q" else 256
                weight = wqkv_loc[pl.ds(i, BLK), pl.ds(first, cols)].astype(F32)
                column = jnp.sum(weight * value, axis=1, keepdims=True)
                line = jnp.transpose(jnp.broadcast_to(column, (BLK, BLK)))[0:1, :]
                sm[0, 0:1, at_rows(f * share + i, BLK, BLK)] += line

        each_part(chunk, f * share, use)

    def ends_inward(q):
        name, row, rows, cols = chunks[q]
        at = (pl.ds(row, rows), pl.ds(0, cols))

        @pl.when(has_out)
        def _():
            arrived(zr1.at[at], "zi", q)
            zs[at] = (zs[at].astype(F32) + zr1[at].astype(F32)).astype(BF16)

    def first_inward(q):
        own_share(q)
        name, row, rows, cols = chunks[q]
        at = (pl.ds(row, rows), pl.ds(0, cols))
        end = jnp.logical_not(has_out)
        dev = (f, inward, t)
        if nc == 2:
            send(zs.at[at], zr2.at[at], ("ze", q), ("zx", q), dev)
        else:
            send(zs.at[at], zr1.at[at], ("ze", q), ("zi", q), dev, end)

    def then_inward(q):
        if nc == 2:
            return
        name, row, rows, cols = chunks[q]
        at = (pl.ds(row, rows), pl.ds(0, cols))
        ends_inward(q)
        dev = (f, inward, t)
        send(zs.at[at], zr2.at[at], ("zm", q), ("zx", q), dev, is_mid)
        if nc > 4:
            send(zs.at[at], zr1.at[at], ("zn", q), ("zi", q), dev, has_out & jnp.logical_not(is_mid))

    def then_outward(q):
        name, row, rows, cols = chunks[q]
        at = (pl.ds(row, rows), pl.ds(0, cols))

        @pl.when(is_mid)
        def _():
            arrived(zr2.at[at], "zx", q)
            tot[at] = (zs[at].astype(F32) + zr2[at].astype(F32)).astype(BF16)

        @pl.when(jnp.logical_not(is_mid))
        def _():
            arrived(tot.at[at], "zo", q)

        if nc > 2:
            send(tot.at[at], tot.at[at], ("zo", q), ("zo", q), (f, outward, t), has_out)
        local_copy(tot.at[at], grads_out.at[at], 4 + micro + q)

    def small_start():
        g2 = jnp.sum(gain2[...], axis=0, keepdims=True)
        sm[0, 1:2, 0:D] = g2
        for h in range(HEADS_HERE):
            below = jnp.sum(facc[h, 0])
            above = jnp.sum(facc[h, 1])
            per = jnp.sum(tacc[h], axis=1)
            per = jnp.sum(jnp.concatenate([per, jnp.zeros((96, 128), F32)], axis=0), axis=1, keepdims=True)
            line = jnp.transpose(jnp.broadcast_to(per, (128, 128)))[0:1, :]
            lane = lax.broadcasted_iota(jnp.int32, (1, 128), 1)
            line = line + jnp.where(lane == 15, below, 0.0) + jnp.where(lane == 31, above, 0.0)
            sm[0, h : h + 1, pl.ds(D, 128)] = line

    def small_send(step):
        if step == 0:
            send(sm.at[0], smr.at[0], ("m", 0), ("m", 0), sib)
        elif step == 1:
            send(sm.at[1], smr.at[1], ("m", 1), ("m", 1), ypeer)
        elif step == 2:
            for j, dev in enumerate(xpeers):
                send(sm.at[2], smr.at[2 + nf - 2 - j], ("mx", j), ("mx", nf - 2 - j), dev)
        else:
            for k in range(1, nc):
                send(sm.at[3], smr.at[1 + nf + nc - k - 1], ("mz", k), ("mz", nc - k), zpeers[k - 1])

    def small_take(step):
        if step < 2:
            arrived(smr.at[step], "m", step)
            lanes = lax.broadcasted_iota(jnp.int32, (8, D + 128), 1)
            sm[step + 1] = sm[step] + jnp.where(lanes < D, smr[step], 0.0)
        elif step == 2:
            total = sm[2]
            for j in range(nf - 1):
                arrived(smr.at[2 + j], "mx", j)
                total = total + smr[2 + j]
            sm[3] = total
        else:
            total = sm[3]
            for k in range(1, nc):
                arrived(smr.at[1 + nf + k - 1], "mz", k)
                total = total + smr[1 + nf + k - 1]
            small_out[...] = total

    sm[0] = jnp.zeros((8, D + 128), F32)
    take_small()
    positions_and_bias()
    gather(0)
    fold_gain()
    gather_end(0)
    take_wo()
    for m in range(micro):
        local[4 + m].wait()
        spread_own("g", g, m)
    attend_and_mix(0)
    gather(1)
    mid_phase(0, 0)
    gather_end(1)
    attend_and_mix(1)
    norm_two(0)
    gather(2)
    mid_phase(0, 1)
    spread_on("n2", n2, 0)
    gather_end(2)
    attend_and_mix(2)
    norm_two(1)
    for m in range(micro):
        spread_on("g", g, m)
    for m in range(micro):
        spread_end("g", g, m)
    take_ff()
    feed(0)
    mid_phase(0, 2)
    spread_on("n2", n2, 1)
    mid_phase(1, 0)
    mid_phase(2, 0)
    norm_two(2)
    feed(1)
    back_two(0)
    spread_on("n2", n2, 2)
    mid_phase(1, 1)
    mid_phase(2, 1)
    output_rows(0)
    spread_on("gm", gm, 0)
    feed(2)
    back_two(1)
    mid_phase(1, 2)
    mid_phase(2, 2)
    output_rows(1)
    spread_on("gm", gm, 1)
    attend_back(0)
    back_two(2)
    for k in range(nc):
        back_start(0, k)
    share_out(0)
    spread_on("gm", gm, 2)
    for k in range(nc):
        back_mid(0, k)
    bin_table(0)
    output_rows(2)
    attend_back(1)
    for k in range(nc):
        back_out(0, k)
    for k in range(nc):
        back_start(1, k)
    share_out(1)
    share_out(2)
    for k in range(nc):
        back_mid(1, k)
    bin_table(1)
    first_inward(0)
    attend_back(2)
    for k in range(nc):
        back_out(1, k)
    for k in range(nc):
        back_start(2, k)
    share_out(5)
    share_out(6)
    for k in range(nc):
        back_mid(2, k)
    back_one(0)
    share_out(3)
    share_out(4)
    bin_table(2)
    small_start()
    for k in range(nc):
        back_out(2, k)
    first_inward(5)
    first_inward(6)
    small_send(0)
    back_one(1)
    then_inward(0)
    first_inward(1)
    first_inward(2)
    small_take(0)
    small_send(1)
    first_inward(3)
    first_inward(4)
    then_inward(5)
    then_inward(6)
    small_take(1)
    small_send(2)
    back_one(2)
    then_outward(0)
    then_inward(1)
    small_take(2)
    small_send(3)
    then_inward(2)
    then_inward(3)
    then_inward(4)
    then_outward(5)
    then_outward(6)
    then_outward(1)
    then_outward(2)
    then_outward(3)
    then_outward(4)
    small_take(3)
    for copy in local[4 + micro :]:
        copy.wait()
    for name, copy, when in pending:
        if when is None:
            copy.wait_send()
        else:
            pl.when(when)(copy.wait_send)
    assert len(sems.numbers) <= n_sems, len(sems.numbers)


def kernel_scratch(nf, nc, micro, T, share, hidden, n_sems):
    R = 4 * T
    L = nc * R
    vm = lambda shape, kind=BF16: pltpu.VMEM(shape, kind)
    rids = 3 * micro + nc * micro
    chunks, chunk_rows = grad_chunks(share, hidden)
    wide = max(384, share)
    return [
        vm((D, 640)), vm((256, D)), vm((D, hidden)), vm((hidden, D)),
        vm((nf, 8, D + 128), F32), vm((8, D + 128), F32),
        vm((micro, L, D)), vm((micro, R, D)),
        vm((3, micro, 8, 128), jnp.int32), vm((micro, 6, BLK, BLK), jnp.int32),
        vm((micro, 6, HEADS_HERE, BLK, BLK)),
        vm((micro, HEADS_HERE * R, 256)), vm((micro, L, 384)),
        vm((micro, L, HEADS_HERE * R)), vm((L, R), F32), vm((L, HEADS_HERE * R)),
        vm((micro, 256, R), F32), vm((micro * HEADS_HERE, 8, R), F32), vm((micro * R, 256)),
        vm((R, D), F32), vm((3 * micro, 2, T, D), F32), vm((nc * micro, 2, T, D)),
        vm((3 + nc, 2, T, D)), vm((3 + nc, T, D)), vm((rids, 2, T, D)), vm((rids, T, D)),
        vm((micro, nc - 1, T, D)), vm((micro, nc - 1, T, D)), vm((micro, T, D), F32),
        vm((micro, R, D)), vm((micro, R, hidden)), vm((micro, R, hidden)), vm((micro, R, D)),
        vm((micro, T, D), F32), vm((micro, T, D), F32), vm((micro, R, 256)),
        vm((256, HEADS_HERE * R)), vm((4, BLK, HEADS_HERE * R), F32),
        vm((HEADS_HERE, 32, 8, 128), F32), vm((HEADS_HERE, 2, 8, 128), F32), vm((8, D), F32),
        vm((nf - 1, chunk_rows, wide)), vm((nf - 1, chunk_rows, wide)),
        vm((chunk_rows, wide)), vm((chunk_rows, wide)), vm((chunk_rows, wide)),
        vm((4, 8, D + 128), F32), vm((1 + nf + nc - 1, 8, D + 128), F32),
        pltpu.SemaphoreType.DMA((n_sems,)), pltpu.SemaphoreType.DMA((n_sems,)),
        pltpu.SemaphoreType.DMA((4 + micro + len(chunks),)),
    ]


def per_device(
    nf, nc,
    tokens, positions, w_query, w_key, w_value, w_out, w_in, w_back, gain_one, gain_two, bias_table, cotangent,
):
    micro, T = tokens.shape[0], tokens.shape[2]
    share, hidden = w_in.shape
    R = 4 * T
    buckets_here = bias_table.shape[0]
    f = lax.axis_index("fsdp")
    wqkv = jnp.concatenate(
        [w_query, jnp.zeros((share, 64), BF16), w_key, w_value[:, 128:], w_value[:, :128]], axis=1
    )
    pos = jnp.pad(positions.reshape(micro, R // 128, 128), ((0, 0), (0, 8 - R // 128), (0, 0)))
    small = jnp.zeros((8, D + 128), F32)
    gains = jnp.stack([gain_one, gain_two]).astype(F32)
    small = lax.dynamic_update_slice(small, gains, (0, f * share))
    small = lax.dynamic_update_slice(small, bias_table.astype(F32).T, (0, D + f * buckets_here))
    chunks, chunk_rows = grad_chunks(share, hidden)
    wide = max(384, share)
    n_sems = 320
    sems = Sems()
    vmem, anywhere = pl.BlockSpec(memory_space=pltpu.VMEM), pl.BlockSpec(memory_space=pl.ANY)
    out, grad_in, grads, sums = pl.pallas_call(
        functools.partial(layer_kernel, nf, nc, micro, T, share, hidden, n_sems, sems),
        out_shape=[
            jax.ShapeDtypeStruct((micro, T, D), BF16),
            jax.ShapeDtypeStruct((micro, T, D), BF16),
            jax.ShapeDtypeStruct((chunk_rows, wide), BF16),
            jax.ShapeDtypeStruct((8, D + 128), F32),
        ],
        in_specs=[vmem, vmem, anywhere, vmem, anywhere, anywhere, anywhere, vmem],
        out_specs=[vmem, vmem, anywhere, vmem],
        scratch_shapes=kernel_scratch(nf, nc, micro, T, share, hidden, n_sems),
        compiler_params=pltpu.CompilerParams(
            collective_id=0, has_side_effects=True, vmem_limit_bytes=61800 * 1024
        ),
    )(tokens[:, 0], pos, cotangent[:, 0], wqkv, w_out, w_in, w_back, small)
    named = {name: grads[row : row + rows, :cols].astype(F32) for name, row, rows, cols in chunks}
    scale = gain_one.astype(F32)[:, None]
    grad_kv = named["kv"] * scale
    grad_q = named["q"][:, :192] * scale
    gain_rows = lax.dynamic_slice(sums, (0, f * share), (2, share))
    grad_table = lax.dynamic_slice(sums, (0, D + f * buckets_here), (HEADS_HERE, buckets_here)).T
    return (
        out[:, None],
        grad_in[:, None],
        gain_rows[0],
        gain_rows[1],
        grad_q,
        grad_kv[:, :192],
        jnp.concatenate([grad_kv[:, 256:384], grad_kv[:, 192:256]], axis=1),
        named["out"],
        jnp.concatenate([named["in0"], named["in1"]], axis=1),
        jnp.concatenate([named["back0"], named["back1"]], axis=0),
        grad_table,
    )


def solution(mesh):
    nf, nc = mesh.shape["fsdp"], mesh.shape["ctx"]
    fits = D // nf % BLK == 0 and nc <= 4 and nc % 2 == 0 and mesh.shape["tp"] == 4
    return jax.shard_map(
        functools.partial(per_device, nf, nc) if fits else per_device_plain,
        mesh=mesh,
        in_specs=(
            P(None, "fsdp", ("ctx", "tp"), None),
            P(None, "fsdp", "ctx"),
            P("fsdp", "tp"),
            P("fsdp", "tp"),
            P("fsdp", "tp"),
            P("tp", "fsdp"),
            P("fsdp", "tp"),
            P("tp", "fsdp"),
            P("fsdp"),
            P("fsdp"),
            P("fsdp", "tp"),
            P(None, "fsdp", ("ctx", "tp"), None),
        ),
        out_specs=(
            P(None, "fsdp", ("ctx", "tp"), None),
            P(None, "fsdp", ("ctx", "tp"), None),
            P("fsdp"),
            P("fsdp"),
            P("fsdp", "tp"),
            P("fsdp", "tp"),
            P("fsdp", "tp"),
            P("tp", "fsdp"),
            P("fsdp", "tp"),
            P("tp", "fsdp"),
            P("fsdp", "tp"),
        ),
        check_vma=False,
    )
```

```python
import functools
import math

import jax
import jax.numpy as jnp
from jax import lax
from jax.experimental import pallas as pl
from jax.experimental.pallas import tpu as pltpu
from jax.sharding import PartitionSpec as P

D = 768
HDIM = 64


epsilon = 1e-06
bucket_edges = (12, 16, 23, 32, 46, 64, 91)


def bucket_of(query_pos, key_pos):
    relative = (key_pos[None, :] - query_pos[:, None]).astype(jnp.int32)
    magnitude = jnp.abs(relative)
    bucket = jnp.minimum(magnitude, 8)
    for edge_value in bucket_edges:
        bucket = bucket + (magnitude >= edge_value).astype(jnp.int32)
    return bucket + 16 * (relative > 0).astype(jnp.int32)


def table_bias(bucket, bias_rows):
    slot_ids = jnp.arange(bias_rows.shape[0], dtype=jnp.int32)
    matches = bucket[None, :, :, None] == slot_ids[None, None, None, :]
    return jnp.sum(jnp.where(matches, bias_rows.T[:, None, None, :], 0.0), axis=-1)


def table_grad(bucket, grad_scores, bucket_count):
    slot_ids = jnp.arange(bucket_count, dtype=jnp.int32)
    matches = bucket[None, None, :, :] == slot_ids[:, None, None, None]
    return jnp.sum(jnp.where(matches, grad_scores[None], 0.0), axis=(2, 3))


def inverse_rms(token_rows):
    return lax.rsqrt(jnp.mean(token_rows * token_rows, axis=-1, keepdims=True) + epsilon)


def norm_back(token_rows, scale_rows, gain_full, grad_normed):
    weighted = gain_full * grad_normed
    grad_rows = scale_rows * weighted - token_rows * scale_rows**3 * jnp.mean(
        token_rows * weighted, axis=-1, keepdims=True
    )
    return (grad_rows, jnp.sum(grad_normed * token_rows * scale_rows, axis=0))


def gelu_slope(values_in):
    return (
        0.5 * (1.0 + jax.scipy.special.erf(values_in * 0.7071067811865476))
        + values_in * jnp.exp(-0.5 * values_in * values_in) * 0.3989422804014327
    )


def left_product(left, right):
    return jnp.einsum("ra,rb->ab", left, right, preferred_element_type=jnp.float32)


def right_product(left, right):
    return jnp.einsum("ra,ba->rb", left, right, preferred_element_type=jnp.float32)


def spread_rows(local_rows):
    return lax.all_gather(local_rows, "tp", axis=0, tiled=True)


def collect_rows(partial_rows):
    return lax.psum_scatter(
        partial_rows.astype(jnp.bfloat16), "tp", scatter_dimension=0, tiled=True
    ).astype(jnp.float32)


def pair_terms(
    query_block,
    query_pos,
    key_block,
    key_pos,
    value_block,
    grad_att,
    log_total,
    row_delta,
    bias_rows,
):
    bucket = bucket_of(query_pos, key_pos)
    scores = jnp.einsum("qhd,khd->hqk", query_block, key_block, preferred_element_type=jnp.float32)
    scores = scores + table_bias(bucket, bias_rows)
    probability = jnp.exp(scores - log_total[:, :, None])
    grad_prob = jnp.einsum(
        "qhd,khd->hqk", grad_att, value_block, preferred_element_type=jnp.float32
    )
    grad_scores = probability * (grad_prob - row_delta[:, :, None])
    return (bucket, probability, grad_scores)


def make_fold(queries, query_pos, bias_rows, key_rows):
    head_count = queries.shape[1]

    def fold_keys(state_carry, shard_piece, first_row):
        keys_part, values_part, pos_part = shard_piece
        block_count = keys_part.shape[0] // key_rows
        key_blocks = keys_part.reshape(block_count, key_rows, head_count, HDIM)
        value_blocks = values_part.reshape(block_count, key_rows, head_count, HDIM)
        pos_blocks = pos_part.reshape(block_count, key_rows)

        def fold_one_block(inner, block_item):
            run_peak, run_total, run_acc = inner
            key_block, value_block, pos_block = block_item
            scores = jnp.einsum(
                "qhd,khd->hqk", queries, key_block, preferred_element_type=jnp.float32
            )
            scores = scores + table_bias(bucket_of(query_pos, pos_block), bias_rows)
            new_peak = jnp.maximum(run_peak, jnp.max(scores, axis=-1))
            factor = jnp.exp(run_peak - new_peak)
            weights_exp = jnp.exp(scores - new_peak[:, :, None])
            run_total = run_total * factor + jnp.sum(weights_exp, axis=-1)
            run_acc = run_acc * factor[:, :, None] + jnp.einsum(
                "hqk,khd->hqd",
                weights_exp.astype(jnp.bfloat16),
                value_block,
                preferred_element_type=jnp.float32,
            )
            return ((new_peak, run_total, run_acc), None)

        result, unused = lax.scan(
            fold_one_block, state_carry, (key_blocks, value_blocks, pos_blocks)
        )
        return result

    return fold_keys


def attend_back(
    queries,
    query_pos,
    bias_rows,
    keys_all,
    values_all,
    pos_all,
    grad_att,
    log_total,
    row_delta,
    key_rows,
):
    local_len, head_count = (queries.shape[0], queries.shape[1])
    bucket_count = bias_rows.shape[0]
    block_count = keys_all.shape[0] // key_rows
    key_blocks = keys_all.reshape(block_count, key_rows, head_count, HDIM)
    value_blocks = values_all.reshape(block_count, key_rows, head_count, HDIM)
    pos_blocks = pos_all.reshape(block_count, key_rows)

    def attend_one_block(inner, block_item):
        grad_query, grad_bias = inner
        key_block, value_block, pos_block = block_item
        bucket, probability, grad_scores = pair_terms(
            queries,
            query_pos,
            key_block,
            pos_block,
            value_block,
            grad_att,
            log_total,
            row_delta,
            bias_rows,
        )
        grad_bias = grad_bias + table_grad(bucket, grad_scores, bucket_count)
        scores_low = grad_scores.astype(jnp.bfloat16)
        grad_query = grad_query + jnp.einsum(
            "hqk,khd->qhd", scores_low, key_block, preferred_element_type=jnp.float32
        )
        grad_value = jnp.einsum(
            "hqk,qhd->khd",
            probability.astype(jnp.bfloat16),
            grad_att,
            preferred_element_type=jnp.float32,
        )
        grad_key = jnp.einsum(
            "hqk,qhd->khd", scores_low, queries, preferred_element_type=jnp.float32
        )
        return ((grad_query, grad_bias), (grad_key, grad_value))

    start_state = (
        jnp.zeros((local_len, head_count, HDIM), jnp.float32),
        jnp.zeros((bucket_count, head_count), jnp.float32),
    )
    final_state, stacked = lax.scan(
        attend_one_block, start_state, (key_blocks, value_blocks, pos_blocks)
    )
    total_keys = keys_all.shape[0]
    return (
        final_state[0],
        final_state[1],
        stacked[0].reshape(total_keys, head_count * HDIM),
        stacked[1].reshape(total_keys, head_count * HDIM),
    )


def own_share(grad_term, grad_dim):
    share_len = grad_term.shape[grad_dim] // lax.axis_size("fsdp")
    return lax.dynamic_slice_in_dim(
        grad_term, lax.axis_index("fsdp") * share_len, share_len, grad_dim
    )


def per_device_plain(
    tokens,
    positions,
    w_query,
    w_key,
    w_value,
    w_out,
    w_in,
    w_back,
    gain_one,
    gain_two,
    bias_table,
    cotangent,
):
    micro_count = tokens.shape[0]
    head_count = w_query.shape[1] // HDIM
    head_cols = head_count * HDIM
    hidden_cols = w_in.shape[1]
    bucket_count = bias_table.shape[0] * lax.axis_size("fsdp")
    grad_wq = jnp.zeros((D, head_cols), jnp.float32)
    grad_wk = jnp.zeros((D, head_cols), jnp.float32)
    grad_wv = jnp.zeros((D, head_cols), jnp.float32)
    grad_wo = jnp.zeros((head_cols, D), jnp.float32)
    grad_wi = jnp.zeros((D, hidden_cols), jnp.float32)
    grad_wb = jnp.zeros((hidden_cols, D), jnp.float32)
    grad_table = jnp.zeros((bucket_count, head_count), jnp.float32)
    grad_gain_one = jnp.zeros((D,), jnp.float32)
    grad_gain_two = jnp.zeros((D,), jnp.float32)
    outputs = []
    input_grads = []
    for micro_step in range(micro_count):
        full_wq, full_wk, full_wv, full_wo, full_wi, full_wb, full_g1, full_g2, full_table = (
            lax.all_gather(w_query, "fsdp", axis=0, tiled=True),
            lax.all_gather(w_key, "fsdp", axis=0, tiled=True),
            lax.all_gather(w_value, "fsdp", axis=0, tiled=True),
            lax.all_gather(w_out, "fsdp", axis=1, tiled=True),
            lax.all_gather(w_in, "fsdp", axis=0, tiled=True),
            lax.all_gather(w_back, "fsdp", axis=1, tiled=True),
            lax.all_gather(gain_one, "fsdp", axis=0, tiled=True),
            lax.all_gather(gain_two, "fsdp", axis=0, tiled=True),
            lax.all_gather(bias_table, "fsdp", axis=0, tiled=True),
        )
        gain_first = full_g1.astype(jnp.float32)
        gain_second = full_g2.astype(jnp.float32)
        bias_rows = full_table.astype(jnp.float32)
        token_rows = tokens[micro_step, 0].astype(jnp.float32)
        query_pos = positions[micro_step, 0]
        scale_one = inverse_rms(token_rows)
        normed = spread_rows((token_rows * scale_one * gain_first).astype(jnp.bfloat16))
        local_len = normed.shape[0]
        key_rows = math.gcd(local_len, 256)
        queries_low = jnp.dot(normed, full_wq, preferred_element_type=jnp.float32).astype(
            jnp.bfloat16
        )
        keys_low = jnp.dot(normed, full_wk, preferred_element_type=jnp.float32).astype(jnp.bfloat16)
        values_low = jnp.dot(normed, full_wv, preferred_element_type=jnp.float32).astype(
            jnp.bfloat16
        )
        queries = queries_low.reshape(local_len, head_count, HDIM)
        start_state = (
            jnp.full((head_count, local_len), -1e30, jnp.float32),
            jnp.zeros((head_count, local_len), jnp.float32),
            jnp.zeros((head_count, local_len, HDIM), jnp.float32),
        )
        fold_keys = make_fold(queries, query_pos, bias_rows, key_rows)
        run_peak, run_total, run_acc = fold_keys(
            start_state,
            (
                lax.all_gather(keys_low, "ctx", axis=0, tiled=True),
                lax.all_gather(values_low, "ctx", axis=0, tiled=True),
                lax.all_gather(query_pos, "ctx", axis=0, tiled=True),
            ),
            jnp.int32(0),
        )
        log_total = run_peak + jnp.log(run_total)
        attended_f = jnp.transpose(run_acc / run_total[:, :, None], (1, 0, 2)).reshape(
            local_len, head_cols
        )
        attended = attended_f.astype(jnp.bfloat16)
        middle = token_rows + collect_rows(
            jnp.dot(attended, full_wo, preferred_element_type=jnp.float32)
        )
        scale_two = inverse_rms(middle)
        normed_two = spread_rows((middle * scale_two * gain_second).astype(jnp.bfloat16))
        hidden_pre = jnp.dot(normed_two, full_wi, preferred_element_type=jnp.float32)
        hidden = jax.nn.gelu(hidden_pre, approximate=False).astype(jnp.bfloat16)
        output_rows = middle + collect_rows(
            jnp.dot(hidden, full_wb, preferred_element_type=jnp.float32)
        )
        outputs.append(output_rows.astype(jnp.bfloat16))
        grad_local = cotangent[micro_step, 0]
        grad_full = spread_rows(grad_local)
        grad_wb = grad_wb + left_product(hidden, grad_full)
        grad_hidden = right_product(grad_full, full_wb)
        grad_pre = (grad_hidden * gelu_slope(hidden_pre)).astype(jnp.bfloat16)
        grad_wi = grad_wi + left_product(normed_two, grad_pre)
        grad_normed_two = collect_rows(right_product(grad_pre, full_wi))
        grad_middle, gain_part_two = norm_back(middle, scale_two, gain_second, grad_normed_two)
        grad_middle = grad_middle + grad_local.astype(jnp.float32)
        grad_gain_two = grad_gain_two + gain_part_two
        grad_mixed = spread_rows(grad_middle.astype(jnp.bfloat16))
        grad_wo = grad_wo + left_product(attended, grad_mixed)
        grad_attended = right_product(grad_mixed, full_wo).astype(jnp.bfloat16)
        row_delta = jnp.sum(
            (grad_attended.astype(jnp.float32) * attended_f).reshape(local_len, head_count, HDIM),
            axis=-1,
        ).T
        back_keys, back_values, back_pos = (
            lax.all_gather(keys_low, "ctx", axis=0, tiled=True),
            lax.all_gather(values_low, "ctx", axis=0, tiled=True),
            lax.all_gather(query_pos, "ctx", axis=0, tiled=True),
        )
        grad_att_heads = grad_attended.reshape(local_len, head_count, HDIM)
        grad_queries, table_part, grad_keys_all, grad_values_all = attend_back(
            queries,
            query_pos,
            bias_rows,
            back_keys,
            back_values,
            back_pos,
            grad_att_heads,
            log_total,
            row_delta,
            key_rows,
        )
        grad_keys, grad_values = (
            lax.psum_scatter(
                grad_keys_all.astype(jnp.bfloat16), "ctx", scatter_dimension=0, tiled=True
            ).astype(jnp.float32),
            lax.psum_scatter(
                grad_values_all.astype(jnp.bfloat16), "ctx", scatter_dimension=0, tiled=True
            ).astype(jnp.float32),
        )
        grad_table = grad_table + table_part
        grad_q_low = grad_queries.reshape(local_len, head_cols).astype(jnp.bfloat16)
        grad_k_low = grad_keys.astype(jnp.bfloat16)
        grad_v_low = grad_values.astype(jnp.bfloat16)
        grad_wq = grad_wq + left_product(normed, grad_q_low)
        grad_wk = grad_wk + left_product(normed, grad_k_low)
        grad_wv = grad_wv + left_product(normed, grad_v_low)
        grad_normed = collect_rows(
            right_product(grad_q_low, full_wq)
            + right_product(grad_k_low, full_wk)
            + right_product(grad_v_low, full_wv)
        )
        grad_input, gain_part_one = norm_back(token_rows, scale_one, gain_first, grad_normed)
        grad_gain_one = grad_gain_one + gain_part_one
        input_grads.append((grad_input + grad_middle).astype(jnp.bfloat16))
    gain_total_one, gain_total_two = lax.psum((grad_gain_one, grad_gain_two), ("fsdp", "ctx", "tp"))
    sum_wq, sum_wk, sum_wv, sum_wo, sum_wi, sum_wb, sum_table = lax.psum(
        (grad_wq, grad_wk, grad_wv, grad_wo, grad_wi, grad_wb, grad_table), ("fsdp", "ctx")
    )
    share_wq = own_share(sum_wq, 0)
    share_wk = own_share(sum_wk, 0)
    share_wv = own_share(sum_wv, 0)
    share_wo = own_share(sum_wo, 1)
    share_wi = own_share(sum_wi, 0)
    share_wb = own_share(sum_wb, 1)
    share_table = own_share(sum_table, 0)
    return (
        jnp.stack(outputs)[:, None],
        jnp.stack(input_grads)[:, None],
        own_share(gain_total_one, 0),
        own_share(gain_total_two, 0),
        share_wq,
        share_wk,
        share_wv,
        share_wo,
        share_wi,
        share_wb,
        share_table,
    )


MESH = pl.DeviceIdType.MESH
F32 = jnp.float32
BF16 = jnp.bfloat16
HEADS_HERE = 3
BLK = 128
VALUE_ROWS = (128, 192, 64)


def nn(left, right):
    return lax.dot_general(left, right, (((1,), (0,)), ((), ())), preferred_element_type=F32)


def nt(left, right):
    return lax.dot_general(left, right, (((1,), (1,)), ((), ())), preferred_element_type=F32)


def tn(left, right):
    return lax.dot_general(left, right, (((0,), (0,)), ((), ())), preferred_element_type=F32)


def at_rows(offset, size, unit):
    return pl.ds(pl.multiple_of(offset, unit), size)


def fold_rows(block):
    return jnp.sum(block.reshape(block.shape[0] // 8, 8, block.shape[1]), axis=0)


class Sems:
    def __init__(self):
        self.numbers = {}

    def __call__(self, *name):
        return self.numbers.setdefault(name, len(self.numbers))


PART = 256
REACH = (0, 1, 2, 3, 4, 5, 6, 7, 11, 15, 22, 31, 45, 63, 90, 127)


def grad_chunks(share, hidden):
    head_cols = HEADS_HERE * HDIM
    names = [(f"back{i}", PART, share) for i in range(hidden // PART)]
    names += [(f"in{i}", share, PART) for i in range(hidden // PART)]
    names += [(name, head_cols, share) for name in ("out", "key", "value", "query")]
    chunks, row = [], 0
    for name, rows, cols in names:
        chunks.append((name, row, rows, cols))
        row += rows
    return chunks, row


def layer_kernel(
    nf, nc, micro, rows_own, share, hidden, n_sems, sems,
    tok, pos_in, wq_in, wk_in, wv_in, wo_loc, wi_loc, wb_loc, g1_in, g2_in, table_in, cot,
    out, grad_in, grads_out, small_out,
    w_loc, small_loc, wqkv, wo, wi, wb, small_rx, smallf, n1, g, posb, bkt, bias, qm, kv, e_t, s_t, ds_t, att_t,
    inv, att, scr, keep, keep6, send1, send2, recv1, recv2, zsend, zrecv, gz, n2, hid, gp, gm,
    mid_f, gmid, dq, dom, nds, gacc, tacc, facc, gain2, xs, xr, zr1, zr2, sm, smr,
    ssem, rsem, lsem,
):
    f, c, t = lax.axis_index("fsdp"), lax.axis_index("ctx"), lax.axis_index("tp")
    nt_ = 4
    T = rows_own
    R = nt_ * T
    L = nc * R
    NB = L // BLK
    t1 = t + 1 - 2 * lax.rem(t, 2)
    t2 = lax.rem(t + 2, 4)
    t3 = lax.rem(t1 + 2, 4)
    sib, ypeer = (f, c, t1), (f, c, t2)
    xpeers = [(lax.rem(f + j, nf), c, t) for j in range(1, nf)]
    zpeers = [(f, lax.rem(c + k, nc), t) for k in range(1, nc)]
    half_c = nc // 2
    low_side = c < half_c
    inward = jnp.where(low_side, c + 1, c - 1)
    outward = jnp.clip(jnp.where(low_side, c - 1, c + 1), 0, nc - 1)
    is_mid = (c == half_c - 1) | (c == half_c)
    has_out = (c > 0) & (c < nc - 1)
    if nc == 2:
        has_out = c < 0
    chunks, chunk_rows = grad_chunks(share, hidden)
    pending = []
    zs = xs.at[0]

    def send(src, dst, name_s, name_r, dev, when=None):
        copy = pltpu.make_async_remote_copy(
            src, dst, ssem.at[sems(*name_s)], rsem.at[sems(*name_r)], device_id=dev, device_id_type=MESH
        )
        if when is None:
            copy.start()
        else:
            pl.when(when)(copy.start)
        pending.append((name_s, copy, when))

    def sent(*name_s):
        for at, (name, copy, when) in enumerate(pending):
            if name == name_s:
                if when is None:
                    copy.wait_send()
                else:
                    pl.when(when)(copy.wait_send)
                del pending[at]
                return

    def arrived(dst, *name_r):
        pltpu.make_async_remote_copy(
            dst, dst, ssem.at[sems(*name_r)], rsem.at[sems(*name_r)], device_id=sib, device_id_type=MESH
        ).wait_recv()

    def rms(rows):
        return lax.rsqrt(jnp.mean(rows * rows, axis=-1, keepdims=True) + epsilon)

    def piece(m, block, t_of):
        return n1.at[at_rows(m * L + block * R + t_of * T, T, T)]

    def rows_of(m, t_of):
        return at_rows(m * R + t_of * T, T, T)

    posb[0] = jnp.zeros_like(posb[0])
    posb[2] = jnp.zeros_like(posb[2])
    barrier = pltpu.get_barrier_semaphore()
    peers = [sib, ypeer] + xpeers + zpeers
    for dev in peers:
        pl.semaphore_signal(barrier, inc=1, device_id=dev, device_id_type=MESH)
    for m in range(micro):
        rows = tok[m].astype(F32)
        n1[at_rows(m * L + c * R + t * T, T, T)] = (rows * rms(rows)).astype(BF16)
    posb[1] = pos_in[...]
    local = {}

    def local_copy(src, dst, i):
        copy = pltpu.make_async_copy(src, dst, lsem.at[i])
        copy.start()
        local[i] = copy

    share_cols = at_rows(f * share, share, BLK)
    share_rows = at_rows(f * share, share, BLK)
    own_rows = at_rows(t * T, T, T)
    qkv_parts = (
        (wq_in, 0, 0, 192), (wk_in, 0, 256, 192), (wv_in, 128, 448, 64), (wv_in, 0, 512, 128),
    )
    for i, (src, row, at, size) in enumerate(qkv_parts):
        local_copy(src.at[pl.ds(row, size)], w_loc.at[pl.ds(at, size)], 4 + micro + len(chunks) + i)
    local_copy(wo_loc.at[pl.ds(0, 128)], wo.at[pl.ds(128, 128), share_cols], 0)
    local_copy(wo_loc.at[pl.ds(128, 64)], wo.at[pl.ds(64, 64), share_cols], 1)
    local_copy(wi_loc, wi.at[share_rows], 2)
    local_copy(wb_loc, wb.at[:, share_cols], 3)
    for m in range(micro):
        local_copy(cot.at[m], g.at[rows_of(m, t)], 4 + m)
    small_loc[...] = jnp.zeros_like(small_loc)
    small_loc[0:1, share_cols] = g1_in[...].astype(F32).reshape(1, share)
    small_loc[1:2, share_cols] = g2_in[...].astype(F32).reshape(1, share)
    buckets_here = table_in.shape[1]
    spot = lax.broadcasted_iota(jnp.int32, (buckets_here, 128), 1) - f * buckets_here
    spot = spot == lax.broadcasted_iota(jnp.int32, (buckets_here, 128), 0)
    small_loc[0:HEADS_HERE, pl.ds(D, 128)] = nn(table_in[...], jnp.where(spot, 1.0, 0.0).astype(BF16))

    small_rx[f] = small_loc[...]
    pl.semaphore_wait(barrier, len(peers))

    def spread_first(m):
        mine = piece(m, c, t)
        send(mine, mine, ("ny", m, 0), ("ny", m, 0), ypeer)
        for k in range(1, nc):
            send(mine, mine, ("nz", m, k), ("nz", m, nc - k), zpeers[k - 1])
        send(mine, mine, ("ns", m, 0), ("ns", m, 0), sib)

    def send_small():
        for j, dev in enumerate(xpeers):
            send(small_loc, small_rx.at[f], ("small", j), ("small", nf - 2 - j), dev)
        send(pos_in, posb.at[0], ("posu",), ("posu",), (f, jnp.minimum(c + 1, nc - 1), t), c < nc - 1)
        send(pos_in, posb.at[2], ("posd",), ("posd",), (f, jnp.maximum(c - 1, 0), t), c > 0)

    def send_qkv():
        for j, dev in enumerate(xpeers):
            for i, (src, row, at, size) in enumerate(qkv_parts):
                dst = wqkv.at[pl.ds(at, size), share_cols]
                send(src.at[pl.ds(row, size)], dst, ("wqkv", i, j), ("wqkv", i, nf - 2 - j), dev)

    def send_wo():
        for j, dev in enumerate(xpeers):
            send(wo_loc.at[pl.ds(0, 128)], wo.at[pl.ds(128, 128), share_cols], ("woa", j), ("woa", nf - 2 - j), dev)
            send(wo_loc.at[pl.ds(128, 64)], wo.at[pl.ds(64, 64), share_cols], ("wob", j), ("wob", nf - 2 - j), dev)

    def send_wi():
        for j, dev in enumerate(xpeers):
            send(wi_loc, wi.at[share_rows], ("wi", j), ("wi", nf - 2 - j), dev)

    def send_wb():
        for j, dev in enumerate(xpeers):
            send(wb_loc, wb.at[:, share_cols], ("wb", j), ("wb", nf - 2 - j), dev)

    def share_g(m):
        local[4 + m].wait()
        spread_own("g", g, m)

    def clear():
        w_loc[192:256] = jnp.zeros((64, share), BF16)
        wqkv[192:256] = jnp.zeros((64, D), BF16)
        wo[pl.ds(0, 64)] = jnp.zeros((64, D), BF16)
        dom[...] = jnp.zeros_like(dom)
        tacc[...] = jnp.zeros_like(tacc)
        facc[...] = jnp.zeros_like(facc)
        sm[0] = jnp.zeros((8, D + 128), F32)

    def spread_own(name, buf, m):
        mine = buf.at[rows_of(m, t)]
        send(mine, mine, (name, "y", m), (name, "y", m), ypeer)
        send(mine, mine, (name, "s", m), (name, "s", m), sib)

    def spread_on(name, buf, m):
        there = buf.at[rows_of(m, t2)]
        arrived(there, name, "y", m)
        send(there, there, (name, "f", m), (name, "f", m), sib)

    def spread_end(name, buf, m):
        arrived(buf.at[rows_of(m, t1)], name, "s", m)
        arrived(buf.at[rows_of(m, t3)], name, "f", m)

    def gather_z(m, k):
        z = lax.rem(c + k, nc)
        there = piece(m, z, t)
        arrived(there, "nz", m, k)
        send(there, there, ("ny", m, k), ("ny", m, k), ypeer)
        send(there, there, ("ns", m, k), ("ns", m, k), sib)

    def gather_y(m, k):
        z = lax.rem(c + k, nc)
        there = piece(m, z, t2)
        arrived(there, "ny", m, k)
        send(there, there, ("nf", m, k), ("nf", m, k), sib)

    order = [k for pair in zip(range(1, nc), range(nc - 1, 0, -1)) for k in pair]
    order = list(dict.fromkeys(order))

    def gather(m):
        gather_y(m, 0)
        for at, k in enumerate(order):
            gather_z(m, k)
            if at >= 1:
                gather_y(m, order[at - 1])
        gather_y(m, order[-1])

    def gather_end(m):
        for k in range(nc):
            z = lax.rem(c + k, nc)
            arrived(piece(m, z, t1), "ns", m, k)
            arrived(piece(m, z, t3), "nf", m, k)

    def take_small():
        for j in range(nf - 1):
            arrived(small_rx.at[lax.rem(f + 1 + j, nf)], "small", j)
        total = small_rx[0]
        for j in range(1, nf):
            total = total + small_rx[j]
        smallf[...] = total

    def take_positions():
        @pl.when(c > 0)
        def _():
            arrived(posb.at[0], "posu")

        @pl.when(c < nc - 1)
        def _():
            arrived(posb.at[2], "posd")

    def bias_of(m):
        for qb in range(2):
            query_row = posb[1, m, :, pl.ds(qb * BLK, BLK)]
            for d in (-1, 0, 1):
                slot, row = ((0, 1), (1, 0), (1, 1), (2, 0))[qb + d + 1]
                key_row = posb[slot, m, :, pl.ds(row * BLK, BLK)]
                key_col = jnp.transpose(jnp.broadcast_to(key_row, (BLK, BLK)))
                relative = key_col - query_row
                size = jnp.abs(relative)
                bucket = jnp.minimum(size, 8)
                for edge_value in bucket_edges:
                    bucket = bucket + (size >= edge_value).astype(jnp.int32)
                bucket = bucket + 16 * (relative > 0).astype(jnp.int32)
                sub = qb * 3 + d + 1
                bkt[m, sub] = bucket
                for h in range(HEADS_HERE):
                    row_of = jnp.broadcast_to(smallf[h : h + 1, pl.ds(D, 128)], (BLK, BLK))
                    bias[m, sub, h] = jnp.take_along_axis(row_of, bucket, axis=1).astype(BF16)

    def fold_gain():
        for i in range(len(qkv_parts)):
            local[4 + micro + len(chunks) + i].wait()
        wqkv[:, share_cols] = w_loc[...]
        for j in range(nf - 1):
            cols = at_rows(lax.rem(f + 1 + j, nf) * share, share, BLK)
            for i, (src, row, at, size) in enumerate(qkv_parts):
                arrived(wqkv.at[pl.ds(at, size), cols], "wqkv", i, j)
        wqkv[...] = (wqkv[...].astype(F32) * smallf[0:1, 0:D]).astype(BF16)

    def reduce_start(slot, rid, kept, value, previous):
        scr[...] = value
        if previous is not None:
            sent("r1", previous)
        send1[slot, 0] = scr[at_rows(t1 * T, T, T)].astype(BF16)
        send1[slot, 1] = scr[at_rows(t3 * T, T, T)].astype(BF16)
        send(send1.at[slot], recv1.at[rid], ("r1", rid), ("r1", rid), sib)
        kept[0] = scr[own_rows].astype(kept.dtype)
        kept[1] = scr[at_rows(t2 * T, T, T)].astype(kept.dtype)

    def reduce_mid(slot, rid, kept, previous):
        arrived(recv1.at[rid], "r1", rid)
        if previous is not None:
            sent("r2", previous)
        send2[slot] = (kept[1].astype(F32) + recv1[rid, 1].astype(F32)).astype(BF16)
        send(send2.at[slot], recv2.at[rid], ("r2", rid), ("r2", rid), ypeer)
        kept[0] = (kept[0].astype(F32) + recv1[rid, 0].astype(F32)).astype(kept.dtype)

    def reduce_end(rid, kept):
        arrived(recv2.at[rid], "r2", rid)
        return kept[0].astype(F32) + recv2[rid].astype(F32)

    def phase(p, m):
        rid = p * micro + m
        return p, rid, keep.at[2 * p + m % 2], (rid - 1 if m > 0 else None)

    def start_phase(p, m, value):
        slot, rid, kept, previous = phase(p, m)
        reduce_start(slot, rid, kept, value, previous)

    def mid_phase(p, m):
        slot, rid, kept, previous = phase(p, m)
        reduce_mid(slot, rid, kept, previous)

    def end_phase(p, m):
        slot, rid, kept, previous = phase(p, m)
        return reduce_end(rid, kept)

    wide_cols = HEADS_HERE * R

    def far_row(kb, below, above):
        parts = []
        for h in range(HEADS_HERE):
            for qb in range(2):
                d = kb - 2 * c - qb
                parts.append(jnp.where(d < -1, below[h], jnp.where(d > 1, above[h], 0.0)))
        return jnp.concatenate(parts, axis=1)

    def near_blocks(use):
        for qb in range(2):
            for d in (-1, 0, 1):
                kb = 2 * c + qb + d
                if qb + d in (0, 1):
                    use(qb, d, kb)
                else:
                    pl.when((kb >= 0) & (kb < NB))(functools.partial(use, qb, d, kb))

    def project(m):
        own = at_rows(m * L + c * R, R, R)
        queries = nt(n1[own], wqkv[0:256])
        lane = lax.broadcasted_iota(jnp.int32, (R, 256), 1)
        for h in range(HEADS_HERE):
            keep_it = (lane >= h * HDIM) & (lane < (h + 1) * HDIM)
            qm[m, pl.ds(h * R, R)] = jnp.where(keep_it, queries, 0.0).astype(BF16)
        kv[pl.ds(m * L, L)] = nt(n1[pl.ds(m * L, L)], wqkv[256:640]).astype(BF16)

    def attend(m):
        first = m * L
        every = pl.ds(first, L)
        s_t[...] = nt(kv[every, 0:256], qm[m])
        tables = [smallf[h : h + 1, pl.ds(D, 128)] for h in range(HEADS_HERE)]
        below = [jnp.broadcast_to(tab[:, 15:16], (1, BLK)) for tab in tables]
        above = [jnp.broadcast_to(tab[:, 31:32], (1, BLK)) for tab in tables]

        def near(qb, d, kb):
            r = at_rows(kb * BLK, BLK, BLK)
            for h in range(HEADS_HERE):
                q = pl.ds(h * R + qb * BLK, BLK)
                s_t[r, q] = s_t[r, q] + bias[m, qb * 3 + d + 1, h].astype(F32)

        near_blocks(near)

        def peak(kb, top):
            block = s_t[at_rows(kb * BLK, BLK, BLK)]
            block = jnp.max(block.reshape(BLK // 8, 8, wide_cols), axis=0)
            return jnp.maximum(top, block + far_row(kb, below, above))

        top = lax.fori_loop(0, NB, peak, jnp.full((8, wide_cols), -jnp.inf, F32))
        top = jnp.max(top, axis=0, keepdims=True)

        def expo(kb, total):
            weights = jnp.exp(s_t[at_rows(kb * BLK, BLK, BLK)] - (top - far_row(kb, below, above)))
            e_t[at_rows(first + kb * BLK, BLK, BLK)] = weights.astype(BF16)
            return total + fold_rows(weights)

        total = lax.fori_loop(0, NB, expo, jnp.zeros((8, wide_cols), F32))
        over = 1.0 / jnp.sum(total, axis=0, keepdims=True)
        inv[m] = jnp.broadcast_to(over, (8, wide_cols))
        mixed = tn(kv[every, 128:384], e_t[every])
        for h in range(HEADS_HERE):
            v0 = VALUE_ROWS[h]
            cols = slice(h * R, (h + 1) * R)
            att_t[m, pl.ds(v0, HDIM)] = mixed[v0 : v0 + HDIM, cols] * over[:, cols]
        att_t[m, pl.ds(0, HDIM)] = jnp.zeros((HDIM, R), F32)
        attended = jnp.transpose(att_t[m]).astype(BF16)
        att[pl.ds(m * R, R)] = attended

    def mix(m):
        start_phase(0, m, nn(att[pl.ds(m * R, R)], wo[...]))

    def take_wo():
        local[0].wait()
        local[1].wait()
        for j in range(nf - 1):
            cols = at_rows(lax.rem(f + 1 + j, nf) * share, share, BLK)
            arrived(wo.at[pl.ds(128, 128), cols], "woa", j)
            arrived(wo.at[pl.ds(64, 64), cols], "wob", j)

    def take_wi():
        local[2].wait()
        for j in range(nf - 1):
            arrived(wi.at[at_rows(lax.rem(f + 1 + j, nf) * share, share, BLK)], "wi", j)

    def take_wb():
        local[3].wait()
        for j in range(nf - 1):
            arrived(wb.at[:, at_rows(lax.rem(f + 1 + j, nf) * share, share, BLK)], "wb", j)

    def norm_two(m):
        middle = tok[m].astype(F32) + end_phase(0, m)
        mid_f[m] = middle
        n2[rows_of(m, t)] = (middle * rms(middle) * smallf[1:2, 0:D]).astype(BF16)
        spread_own("n2", n2, m)

    def feed(m):
        spread_end("n2", n2, m)
        here = pl.ds(m * R, R)
        rows = n2[here]

        def one(i, unused):
            cols = at_rows(i * 256, 256, 256)
            pre = nn(rows, wi[:, cols])
            slope = nt(g[here], wb[cols])
            bell = 0.5 * (1.0 + lax.erf(pre * 0.7071067811865476))
            hid[here, cols] = (pre * bell).astype(BF16)
            bell = bell + pre * jnp.exp(-0.5 * pre * pre) * 0.3989422804014327
            gp[here, cols] = (slope * bell).astype(BF16)
            return unused

        lax.fori_loop(0, hidden // 256, one, 0)
        start_phase(1, m, nt(gp[here], wi[...]))
        start_phase(2, m, nn(hid[here], wb[...]))

    def output_rows(m):
        out[m] = (mid_f[m] + end_phase(2, m)).astype(BF16)

    def back_two(m):
        grad_normed = end_phase(1, m)
        middle = mid_f[m]
        scale = rms(middle)
        unit = middle * scale
        part = fold_rows(grad_normed * unit)
        gain2[...] = part if m == 0 else gain2[...] + part
        weighted = smallf[1:2, 0:D] * grad_normed
        grad = scale * (weighted - unit * jnp.mean(unit * weighted, axis=-1, keepdims=True))
        grad = grad + g[rows_of(m, t)].astype(F32)
        gmid[m] = grad
        gm[rows_of(m, t)] = grad.astype(BF16)
        spread_own("gm", gm, m)

    def attend_back(m):
        first = m * L
        every = pl.ds(first, L)
        grad_att = nt(wo[...], gm[pl.ds(m * R, R)]).astype(BF16).astype(F32)
        deltas = []
        for h in range(HEADS_HERE):
            v0 = VALUE_ROWS[h]
            scaled = (grad_att[v0 : v0 + HDIM] * inv[m, 0:1, pl.ds(h * R, R)]).astype(BF16)
            dom[pl.ds(v0, HDIM), pl.ds(h * R, R)] = scaled
            deltas.append(jnp.sum(scaled.astype(F32) * att_t[m, pl.ds(v0, HDIM)], axis=0, keepdims=True))
        delta = jnp.concatenate(deltas, axis=1)
        s_t[...] = nn(kv[every, 128:384], dom[...])
        half = lax.rem(lax.broadcasted_iota(jnp.int32, (8, wide_cols), 1) // BLK, 2)

        def one_block(kb, sums):
            r = at_rows(kb * BLK, BLK, BLK)
            grad = e_t[at_rows(first + kb * BLK, BLK, BLK)].astype(F32) * (s_t[r] - delta)
            ds_t[r] = grad.astype(BF16)
            part = fold_rows(grad)
            d = kb - 2 * c - half
            return sums[0] + jnp.where(d < -1, part, 0.0), sums[1] + jnp.where(d > 1, part, 0.0)

        zero = jnp.zeros((8, wide_cols), F32)
        low, high = lax.fori_loop(0, NB, one_block, (zero, zero))
        facc[0] += low
        facc[1] += high

        def save(qb, d, kb):
            r = at_rows(kb * BLK, BLK, BLK)
            for h in range(HEADS_HERE):
                nds[m, qb * 3 + d + 1, h] = ds_t[r, pl.ds(h * R + qb * BLK, BLK)]

        near_blocks(save)
        grad_q = tn(kv[every, 0:256], ds_t[...])
        columns = [grad_q[h * HDIM : (h + 1) * HDIM, h * R : (h + 1) * R] for h in range(HEADS_HERE)]
        columns.append(jnp.zeros((HDIM, R), F32))
        dq[pl.ds(m * R, R)] = jnp.transpose(jnp.concatenate(columns, axis=0)).astype(BF16)
        grad_k = nn(ds_t[...], qm[m])
        grad_v = nt(e_t[every], dom[...])
        kv[every, 0:128] = grad_k[:, 0:128].astype(BF16)
        kv[every, 128:256] = (grad_k[:, 128:256] + grad_v[:, 0:128]).astype(BF16)
        kv[every, 256:384] = grad_v[:, 128:256].astype(BF16)

    def merged(block, spots):
        where_at, parts = spots
        size = BLK // parts
        out_block = block[(parts - 1) * size :]
        for i in range(parts - 2, -1, -1):
            out_block = jnp.where(where_at == i, block[i * size : (i + 1) * size], out_block)
        return out_block

    def spots_of(parts):
        size = BLK // parts
        lane = lax.broadcasted_iota(jnp.int32, (size, BLK), 1)
        tile = lax.broadcasted_iota(jnp.int32, (size, BLK), 0) // 8
        away = lane - 8 * tile - 4 + size // 2
        spot = jnp.zeros((size, BLK), jnp.int32)
        for i in range(1, parts):
            spot = spot + (away >= i * size).astype(jnp.int32)
        return spot, parts

    def bin_table(m):
        def use(qb, d, kb):
            sub = qb * 3 + d + 1

            def bins(names, ids, blocks):
                for b in names:
                    same = ids == b
                    for h in range(HEADS_HERE):
                        tacc[h, b] += fold_rows(jnp.where(same, blocks[h], 0.0))

            if d == 0:
                ids = bkt[m, sub]
                blocks = [nds[m, sub, h].astype(F32) for h in range(HEADS_HERE)]
                for parts, sizes in ((4, range(0, 9)), (2, range(9, 11))):
                    spots = spots_of(parts)
                    both = [b for b in sizes] + [16 + b for b in sizes if b > 0]
                    bins(both, merged(ids, spots), [merged(block, spots) for block in blocks])
                bins([b + s for b in range(11, 16) for s in (0, 16)], ids, blocks)
            else:
                for size in range(1, 16):
                    rows = min(BLK, (REACH[size] + 7) // 8 * 8)
                    low = (rows + 15) // 16 * 16
                    r = pl.ds(BLK - rows if d < 0 else 0, rows)
                    part = slice(low - rows, low) if d < 0 else slice(0, rows)
                    low = pl.ds(BLK - low if d < 0 else 0, low)
                    blocks = [nds[m, sub, h, low].astype(F32)[part] for h in range(HEADS_HERE)]
                    bins([size if d < 0 else 16 + size], bkt[m, sub, r], blocks)

        near_blocks(use)

    def six(m, k):
        return 3 + k, 3 * micro + m * nc + k, keep6.at[k], (3 * micro + (m - 1) * nc + k if m > 0 else None)

    def back_start(m, k):
        r = at_rows(m * L + lax.rem(c + k, nc) * R, R, R)
        value = nn(kv[r], wqkv[256:640])
        if k == 0:
            value = value + nn(dq[pl.ds(m * R, R)], wqkv[0:256])
        slot, rid, kept, previous = six(m, k)
        reduce_start(slot, rid, kept, value, previous)

    def back_mid(m, k):
        slot, rid, kept, previous = six(m, k)
        reduce_mid(slot, rid, kept, previous)

    def back_out(m, k):
        slot, rid, kept, previous = six(m, k)
        total = reduce_end(rid, kept)
        if k == 0:
            gz[m] = total
        else:
            if m > 0:
                sent("gz", m - 1, k)
            zsend[k - 1] = total.astype(BF16)
            send(zsend.at[k - 1], zrecv.at[m, nc - k - 1], ("gz", m, k), ("gz", m, nc - k), zpeers[k - 1])

    def back_one(m):
        weighted = gz[m]
        for k in range(1, nc):
            arrived(zrecv.at[m, k - 1], "gz", m, k)
            weighted = weighted + zrecv[m, k - 1].astype(F32)
        rows = tok[m].astype(F32)
        scale = rms(rows)
        unit = rows * scale
        grad = scale * (weighted - unit * jnp.mean(unit * weighted, axis=-1, keepdims=True))
        grad_in[m] = (gmid[m] + grad).astype(BF16)

    def gather_grads(m):
        own = at_rows(m * L + c * R, R, R)
        every = pl.ds(m * L, L)
        for rows, value in (
            (pl.ds(0, 256), tn(dq[pl.ds(m * R, R)], n1[own])),
            (pl.ds(256, 384), tn(kv[every], n1[every])),
        ):
            gacc[rows] = value if m == 0 else gacc[rows] + value

    def each_part(chunk, part, use):
        name, row, rows, cols = chunk
        share_at = at_rows(part, share, BLK)
        if name.startswith("back"):
            use(row, rows, tn(hid[:, pl.ds(int(name[4:]) * PART, PART)], g[:, share_at]), None)
        elif name.startswith("in"):
            use(row, rows, tn(n2[:, share_at], gp[:, pl.ds(int(name[2:]) * PART, PART)]), None)
        elif name == "out":
            value = tn(att[...], gm[:, share_at])
            use(row, 128, value[128:], None)
            use(row + 128, 64, value[64:128], None)
        elif name == "value":
            use(row, 128, gacc[pl.ds(512, 128), share_at], 512)
            use(row + 128, 64, gacc[pl.ds(448, 64), share_at], 448)
        else:
            first = 0 if name == "query" else 256
            use(row, rows, gacc[pl.ds(first, rows), share_at], first)

    def share_out(q):
        chunk = chunks[q]
        name, row, rows, cols = chunk
        for j, dev in enumerate(xpeers):
            part = lax.rem(f + 1 + j, nf) * share

            def use(at, size, value, first, j=j):
                xs[j, pl.ds(at, size), 0:cols] = value.astype(BF16)

            each_part(chunk, part, use)
            src = xs.at[j, pl.ds(row, rows), pl.ds(0, cols)]
            dst = xr.at[nf - 2 - j, pl.ds(row, rows), pl.ds(0, cols)]
            send(src, dst, ("x", q, j), ("x", q, nf - 2 - j), dev)

    def own_share(q):
        chunk = chunks[q]
        name, row, rows, cols = chunk
        for j in range(nf - 1):
            arrived(xr.at[j, pl.ds(row, rows), pl.ds(0, cols)], "x", q, j)
        sent("x", q, 0)

        def use(at, size, value, first):
            for j in range(nf - 1):
                value = value + xr[j, pl.ds(at, size), 0:cols].astype(F32)
            if first is not None:
                weight = w_loc[pl.ds(first, size)].astype(F32)
                sm[0, 0:1, share_cols] += jnp.sum(weight * value, axis=0, keepdims=True)
                value = value * smallf[0:1, share_cols]
            zs[pl.ds(at, size), 0:cols] = value.astype(BF16)

        each_part(chunk, f * share, use)

    def first_inward(q):
        own_share(q)
        name, row, rows, cols = chunks[q]
        at = (pl.ds(row, rows), pl.ds(0, cols))
        dev = (f, inward, t)
        if nc == 2:
            send(zs.at[at], zr2.at[at], ("ze", q), ("zx", q), dev)
        else:
            send(zs.at[at], zr1.at[at], ("ze", q), ("zi", q), dev, jnp.logical_not(has_out))

    def then_inward(q):
        if nc == 2:
            return
        name, row, rows, cols = chunks[q]
        at = (pl.ds(row, rows), pl.ds(0, cols))

        @pl.when(has_out)
        def _():
            arrived(zr1.at[at], "zi", q)
            zs[at] = (zs[at].astype(F32) + zr1[at].astype(F32)).astype(BF16)

        send(zs.at[at], zr2.at[at], ("zm", q), ("zx", q), (f, inward, t), is_mid)

    def then_outward(q):
        name, row, rows, cols = chunks[q]
        at = (pl.ds(row, rows), pl.ds(0, cols))

        @pl.when(is_mid)
        def _():
            arrived(zr2.at[at], "zx", q)
            zr2[at] = (zs[at].astype(F32) + zr2[at].astype(F32)).astype(BF16)

        if nc > 2:
            send(zr2.at[at], zr2.at[at], ("zo", q), ("zo", q), (f, outward, t), has_out)

    def last_outward(q):
        name, row, rows, cols = chunks[q]
        at = (pl.ds(row, rows), pl.ds(0, cols))

        @pl.when(jnp.logical_not(is_mid))
        def _():
            arrived(zr2.at[at], "zo", q)

        local_copy(zr2.at[at], grads_out.at[at], 4 + micro + q)

    def small_start():
        g2 = jnp.sum(gain2[...], axis=0, keepdims=True)
        sm[0, 1:2, 0:D] = g2
        for h in range(HEADS_HERE):
            below = jnp.sum(jnp.sum(facc[0, :, pl.ds(h * R, R)], axis=0, keepdims=True), axis=1, keepdims=True)
            above = jnp.sum(jnp.sum(facc[1, :, pl.ds(h * R, R)], axis=0, keepdims=True), axis=1, keepdims=True)
            per = jnp.sum(tacc[h], axis=1)
            per = jnp.sum(jnp.concatenate([per, jnp.zeros((96, 128), F32)], axis=0), axis=1, keepdims=True)
            line = jnp.transpose(jnp.broadcast_to(per, (128, 128)))[0:1, :]
            lane = lax.broadcasted_iota(jnp.int32, (1, 128), 1)
            line = line + jnp.where(lane == 15, below, 0.0) + jnp.where(lane == 31, above, 0.0)
            sm[0, h : h + 1, pl.ds(D, 128)] = line

    def small_send(step):
        if step == 0:
            send(sm.at[0], smr.at[0], ("m", 0), ("m", 0), sib)
        elif step == 1:
            send(sm.at[1], smr.at[1], ("m", 1), ("m", 1), ypeer)
        elif step == 2:
            for j, dev in enumerate(xpeers):
                send(sm.at[2], smr.at[2 + nf - 2 - j], ("mx", j), ("mx", nf - 2 - j), dev)
        else:
            for k in range(1, nc):
                send(sm.at[3], smr.at[1 + nf + nc - k - 1], ("mz", k), ("mz", nc - k), zpeers[k - 1])

    def small_take(step):
        if step < 2:
            arrived(smr.at[step], "m", step)
            lanes = lax.broadcasted_iota(jnp.int32, (8, D + 128), 1)
            sm[step + 1] = sm[step] + jnp.where(lanes < D, smr[step], 0.0)
        elif step == 2:
            total = sm[2]
            for j in range(nf - 1):
                arrived(smr.at[2 + j], "mx", j)
                total = total + smr[2 + j]
            sm[3] = total
        else:
            total = sm[3]
            for k in range(1, nc):
                arrived(smr.at[1 + nf + k - 1], "mz", k)
                total = total + smr[1 + nf + k - 1]
            small_out[...] = total
            smr[0] = total
            for i in range(2):
                small_out[i : i + 1, 0:share] = smr[0, i : i + 1, share_cols]

    spread_first(0)
    share_g(0)
    send_small()
    share_g(2)
    share_g(1)
    spread_first(1)
    spread_first(2)
    send_qkv()
    send_wo()
    send_wi()
    send_wb()
    clear()
    take_small()
    take_positions()
    bias_of(0)
    bias_of(1)
    bias_of(2)
    spread_on("g", g, 0)
    gather_y(0, 0)
    spread_end("g", g, 0)
    spread_on("g", g, 2)
    gather_z(0, 1)
    spread_end("g", g, 2)
    spread_on("g", g, 1)
    spread_end("g", g, 1)
    gather_y(1, 0)
    fold_gain()
    gather_z(0, 2)
    gather_y(2, 0)
    gather_z(0, 3)
    take_wo()
    gather_y(0, 1)
    gather_z(1, 1)
    gather_y(0, 2)
    gather_y(0, 3)
    gather_z(1, 2)
    gather_end(0)
    project(0)
    attend(0)
    gather_z(1, 3)
    gather_z(2, 1)
    gather_y(1, 2)
    gather_y(1, 1)
    mix(0)
    mid_phase(0, 0)
    take_wi()
    gather_y(1, 3)
    gather_z(2, 2)
    gather_end(1)
    project(1)
    gather_y(2, 1)
    gather_z(2, 3)
    attend(1)
    mix(1)
    norm_two(0)
    gather_y(2, 2)
    mid_phase(0, 1)
    gather_y(2, 3)
    gather_end(2)
    project(2)
    attend(2)
    mix(2)
    spread_on("n2", n2, 0)
    norm_two(1)
    take_wb()
    mid_phase(0, 2)
    feed(0)
    spread_on("n2", n2, 1)
    mid_phase(1, 0)
    mid_phase(2, 0)
    feed(1)
    norm_two(2)
    back_two(0)
    mid_phase(1, 1)
    mid_phase(2, 1)
    output_rows(0)
    spread_on("n2", n2, 2)
    feed(2)
    share_out(4)
    mid_phase(1, 2)
    spread_on("gm", gm, 0)
    share_out(1)
    back_two(1)
    spread_end("gm", gm, 0)
    attend_back(0)
    back_start(0, 1)
    back_start(0, 2)
    first_inward(4)
    spread_on("gm", gm, 1)
    back_mid(0, 2)
    back_start(0, 3)
    spread_end("gm", gm, 1)
    attend_back(1)
    back_out(0, 2)
    first_inward(1)
    back_start(1, 2)
    then_inward(4)
    back_mid(0, 1)
    back_two(2)
    back_mid(0, 3)
    share_out(3)
    mid_phase(2, 2)
    back_mid(1, 2)
    share_out(5)
    back_start(0, 0)
    bin_table(0)
    back_out(0, 1)
    back_start(1, 1)
    back_mid(0, 0)
    bin_table(1)
    back_mid(1, 1)
    spread_on("gm", gm, 2)
    then_inward(1)
    first_inward(3)
    then_outward(4)
    spread_end("gm", gm, 2)
    attend_back(2)
    back_out(1, 2)
    first_inward(5)
    then_inward(3)
    bin_table(2)
    back_out(0, 0)
    back_start(1, 0)
    then_outward(1)
    back_out(1, 1)
    back_out(0, 3)
    back_start(1, 3)
    back_mid(1, 0)
    back_start(2, 2)
    last_outward(4)
    share_out(2)
    back_mid(1, 3)
    back_mid(2, 2)
    output_rows(1)
    share_out(0)
    back_start(2, 1)
    then_inward(5)
    output_rows(2)
    gather_grads(0)
    back_mid(2, 1)
    back_out(1, 0)
    back_start(2, 0)
    share_out(6)
    then_outward(3)
    last_outward(1)
    back_out(1, 3)
    back_start(2, 3)
    first_inward(2)
    back_mid(2, 0)
    back_out(2, 2)
    gather_grads(1)
    gather_grads(2)
    share_out(8)
    share_out(9)
    back_out(2, 1)
    back_one(0)
    first_inward(0)
    share_out(7)
    back_out(2, 0)
    back_mid(2, 3)
    then_outward(5)
    then_inward(2)
    first_inward(6)
    last_outward(3)
    back_one(1)
    back_out(2, 3)
    first_inward(8)
    first_inward(9)
    then_inward(0)
    first_inward(7)
    small_start()
    small_send(0)
    then_inward(6)
    then_outward(2)
    last_outward(5)
    small_take(0)
    small_send(1)
    back_one(2)
    small_take(1)
    small_send(2)
    then_inward(8)
    small_take(2)
    then_outward(0)
    last_outward(2)
    small_send(3)
    then_inward(9)
    then_outward(6)
    then_inward(7)
    then_outward(8)
    last_outward(0)
    small_take(3)
    last_outward(6)
    then_outward(9)
    last_outward(8)
    then_outward(7)
    last_outward(9)
    last_outward(7)
    for q in range(len(chunks)):
        local[4 + micro + q].wait()
    for name, copy, when in pending:
        if when is None:
            copy.wait_send()
        else:
            pl.when(when)(copy.wait_send)
    assert len(sems.numbers) <= n_sems, len(sems.numbers)


def kernel_scratch(nf, nc, micro, T, share, hidden, n_sems):
    R = 4 * T
    L = nc * R
    vm = lambda shape, kind=BF16: pltpu.VMEM(shape, kind)
    rids = 3 * micro + nc * micro
    chunks, chunk_rows = grad_chunks(share, hidden)
    wide = max(384, share)
    return [
        vm((640, share)), vm((8, D + 128), F32),
        vm((640, D)), vm((256, D)), vm((D, hidden)), vm((hidden, D)),
        vm((nf, 8, D + 128), F32), vm((8, D + 128), F32),
        vm((micro * L, D)), vm((micro * R, D)),
        vm((3, micro, 1, R), jnp.int32), vm((micro, 6, BLK, BLK), jnp.int32),
        vm((micro, 6, HEADS_HERE, BLK, BLK)),
        vm((micro, HEADS_HERE * R, 256)), vm((micro * L, 384)),
        vm((micro * L, HEADS_HERE * R)), vm((L, HEADS_HERE * R), F32), vm((L, HEADS_HERE * R)),
        vm((micro, 256, R), F32), vm((micro, 8, HEADS_HERE * R), F32), vm((micro * R, 256)),
        vm((R, D), F32), vm((6, 2, T, D), F32), vm((nc, 2, T, D)),
        vm((3 + nc, 2, T, D)), vm((3 + nc, T, D)), vm((rids, 2, T, D)), vm((rids, T, D)),
        vm((nc - 1, T, D)), vm((micro, nc - 1, T, D)), vm((micro, T, D), F32),
        vm((micro * R, D)), vm((micro * R, hidden)), vm((micro * R, hidden)), vm((micro * R, D)),
        vm((micro, T, D), F32), vm((micro, T, D), F32), vm((micro * R, 256)),
        vm((256, HEADS_HERE * R)), vm((micro, 6, HEADS_HERE, BLK, BLK)), vm((640, D), F32),
        vm((HEADS_HERE, 32, 8, 128), F32), vm((2, 8, HEADS_HERE * R), F32), vm((8, D), F32),
        vm((nf - 1, chunk_rows, wide)), vm((nf - 1, chunk_rows, wide)),
        vm((chunk_rows, wide)), vm((chunk_rows, wide)),
        vm((4, 8, D + 128), F32), vm((1 + nf + nc - 1, 8, D + 128), F32),
        pltpu.SemaphoreType.DMA((n_sems,)), pltpu.SemaphoreType.DMA((n_sems,)),
        pltpu.SemaphoreType.DMA((8 + micro + len(chunks),)),
    ]


def finish_kernel(
    share, hidden, out_low, in_low, grads, sums,
    out, grad_in, gain_one, gain_two, grad_q, grad_k, grad_v, grad_o, grad_i, grad_b, grad_t, turned,
):
    out[:, 0] = out_low[...]
    grad_in[:, 0] = in_low[...]
    gain_one[...] = sums[0:1, 0:share].reshape(share)
    gain_two[...] = sums[1:2, 0:share].reshape(share)
    turned[...] = jnp.transpose(
        jnp.concatenate([sums[:, pl.ds(D, 128)], jnp.zeros((120, 128), F32)], axis=0)
    )
    here = grad_t.shape[1]
    part = turned[pl.ds(pl.multiple_of(lax.axis_index("fsdp") * here, here), here)]
    part = jnp.transpose(jnp.concatenate([part, jnp.zeros((128 - here, 128), F32)], axis=0))
    grad_t[...] = part[0:HEADS_HERE, 0:here]
    chunks, unused = grad_chunks(share, hidden)
    for name, row, rows, cols in chunks:
        value = grads[pl.ds(row, rows), 0:cols].astype(F32)
        if name.startswith("back"):
            grad_b[pl.ds(int(name[4:]) * PART, PART)] = value
        elif name.startswith("in"):
            grad_i[:, pl.ds(int(name[2:]) * PART, PART)] = value
        else:
            {"query": grad_q, "key": grad_k, "value": grad_v, "out": grad_o}[name][...] = value


def per_device(
    nf, nc,
    tokens, positions, w_query, w_key, w_value, w_out, w_in, w_back, gain_one, gain_two, bias_table, cotangent,
):
    micro, T = tokens.shape[0], tokens.shape[2]
    share, hidden = w_in.shape
    chunks, chunk_rows = grad_chunks(share, hidden)
    wide = max(384, share)
    n_sems = 320
    sems = Sems()
    vmem, anywhere = pl.BlockSpec(memory_space=pltpu.VMEM), pl.BlockSpec(memory_space=pl.ANY)
    low = pl.pallas_call(
        functools.partial(layer_kernel, nf, nc, micro, T, share, hidden, n_sems, sems),
        out_shape=[
            jax.ShapeDtypeStruct((micro, T, D), BF16),
            jax.ShapeDtypeStruct((micro, T, D), BF16),
            jax.ShapeDtypeStruct((chunk_rows, wide), BF16),
            jax.ShapeDtypeStruct((8, D + 128), F32),
        ],
        in_specs=[vmem] * 2 + [anywhere] * 6 + [vmem] * 3 + [anywhere],
        out_specs=[vmem, vmem, anywhere, vmem],
        scratch_shapes=kernel_scratch(nf, nc, micro, T, share, hidden, n_sems),
        compiler_params=pltpu.CompilerParams(
            collective_id=0, has_side_effects=True, vmem_limit_bytes=61800 * 1024
        ),
    )(
        tokens[:, 0], positions, w_query.T, w_key.T, w_value.T, w_out, w_in, w_back,
        gain_one, gain_two, bias_table.T, cotangent[:, 0],
    )
    shapes = [
        (tokens.shape, BF16), (tokens.shape, BF16), (gain_one.shape, F32), (gain_two.shape, F32),
        (w_query.T.shape, F32), (w_key.T.shape, F32), (w_value.T.shape, F32), (w_out.shape, F32),
        (w_in.shape, F32), (w_back.shape, F32), (bias_table.T.shape, F32),
    ]
    done = pl.pallas_call(
        functools.partial(finish_kernel, share, hidden),
        out_shape=[jax.ShapeDtypeStruct(shape, kind) for shape, kind in shapes],
        in_specs=[vmem] * 4,
        out_specs=[vmem] * len(shapes),
        scratch_shapes=[pltpu.VMEM((128, 128), F32)],
        compiler_params=pltpu.CompilerParams(vmem_limit_bytes=61800 * 1024),
    )(*low)
    return tuple(x.T if i in (4, 5, 6, 10) else x for i, x in enumerate(done))


def solution(mesh):
    nf, nc = mesh.shape["fsdp"], mesh.shape["ctx"]
    fits = D // nf % BLK == 0 and nc <= 4 and nc % 2 == 0 and mesh.shape["tp"] == 4
    return jax.shard_map(
        functools.partial(per_device, nf, nc) if fits else per_device_plain,
        mesh=mesh,
        in_specs=(
            P(None, "fsdp", ("ctx", "tp"), None),
            P(None, "fsdp", "ctx"),
            P("fsdp", "tp"),
            P("fsdp", "tp"),
            P("fsdp", "tp"),
            P("tp", "fsdp"),
            P("fsdp", "tp"),
            P("tp", "fsdp"),
            P("fsdp"),
            P("fsdp"),
            P("fsdp", "tp"),
            P(None, "fsdp", ("ctx", "tp"), None),
        ),
        out_specs=(
            P(None, "fsdp", ("ctx", "tp"), None),
            P(None, "fsdp", ("ctx", "tp"), None),
            P("fsdp"),
            P("fsdp"),
            P("fsdp", "tp"),
            P("fsdp", "tp"),
            P("fsdp", "tp"),
            P("tp", "fsdp"),
            P("fsdp", "tp"),
            P("tp", "fsdp"),
            P("fsdp", "tp"),
        ),
        check_vma=False,
    )
```

```python
import functools
import math

import jax
import jax.numpy as jnp
from jax import lax
from jax.experimental import pallas as pl
from jax.experimental.pallas import tpu as pltpu
from jax.sharding import PartitionSpec as P

D = 768
HDIM = 64


epsilon = 1e-06
bucket_edges = (12, 16, 23, 32, 46, 64, 91)


def bucket_of(query_pos, key_pos):
    relative = (key_pos[None, :] - query_pos[:, None]).astype(jnp.int32)
    magnitude = jnp.abs(relative)
    bucket = jnp.minimum(magnitude, 8)
    for edge_value in bucket_edges:
        bucket = bucket + (magnitude >= edge_value).astype(jnp.int32)
    return bucket + 16 * (relative > 0).astype(jnp.int32)


def table_bias(bucket, bias_rows):
    slot_ids = jnp.arange(bias_rows.shape[0], dtype=jnp.int32)
    matches = bucket[None, :, :, None] == slot_ids[None, None, None, :]
    return jnp.sum(jnp.where(matches, bias_rows.T[:, None, None, :], 0.0), axis=-1)


def table_grad(bucket, grad_scores, bucket_count):
    slot_ids = jnp.arange(bucket_count, dtype=jnp.int32)
    matches = bucket[None, None, :, :] == slot_ids[:, None, None, None]
    return jnp.sum(jnp.where(matches, grad_scores[None], 0.0), axis=(2, 3))


def inverse_rms(token_rows):
    return lax.rsqrt(jnp.mean(token_rows * token_rows, axis=-1, keepdims=True) + epsilon)


def norm_back(token_rows, scale_rows, gain_full, grad_normed):
    weighted = gain_full * grad_normed
    grad_rows = scale_rows * weighted - token_rows * scale_rows**3 * jnp.mean(
        token_rows * weighted, axis=-1, keepdims=True
    )
    return (grad_rows, jnp.sum(grad_normed * token_rows * scale_rows, axis=0))


def gelu_slope(values_in):
    return (
        0.5 * (1.0 + jax.scipy.special.erf(values_in * 0.7071067811865476))
        + values_in * jnp.exp(-0.5 * values_in * values_in) * 0.3989422804014327
    )


def left_product(left, right):
    return jnp.einsum("ra,rb->ab", left, right, preferred_element_type=jnp.float32)


def right_product(left, right):
    return jnp.einsum("ra,ba->rb", left, right, preferred_element_type=jnp.float32)


def spread_rows(local_rows):
    return lax.all_gather(local_rows, "tp", axis=0, tiled=True)


def collect_rows(partial_rows):
    return lax.psum_scatter(
        partial_rows.astype(jnp.bfloat16), "tp", scatter_dimension=0, tiled=True
    ).astype(jnp.float32)


def pair_terms(
    query_block,
    query_pos,
    key_block,
    key_pos,
    value_block,
    grad_att,
    log_total,
    row_delta,
    bias_rows,
):
    bucket = bucket_of(query_pos, key_pos)
    scores = jnp.einsum("qhd,khd->hqk", query_block, key_block, preferred_element_type=jnp.float32)
    scores = scores + table_bias(bucket, bias_rows)
    probability = jnp.exp(scores - log_total[:, :, None])
    grad_prob = jnp.einsum(
        "qhd,khd->hqk", grad_att, value_block, preferred_element_type=jnp.float32
    )
    grad_scores = probability * (grad_prob - row_delta[:, :, None])
    return (bucket, probability, grad_scores)


def make_fold(queries, query_pos, bias_rows, key_rows):
    head_count = queries.shape[1]

    def fold_keys(state_carry, shard_piece, first_row):
        keys_part, values_part, pos_part = shard_piece
        block_count = keys_part.shape[0] // key_rows
        key_blocks = keys_part.reshape(block_count, key_rows, head_count, HDIM)
        value_blocks = values_part.reshape(block_count, key_rows, head_count, HDIM)
        pos_blocks = pos_part.reshape(block_count, key_rows)

        def fold_one_block(inner, block_item):
            run_peak, run_total, run_acc = inner
            key_block, value_block, pos_block = block_item
            scores = jnp.einsum(
                "qhd,khd->hqk", queries, key_block, preferred_element_type=jnp.float32
            )
            scores = scores + table_bias(bucket_of(query_pos, pos_block), bias_rows)
            new_peak = jnp.maximum(run_peak, jnp.max(scores, axis=-1))
            factor = jnp.exp(run_peak - new_peak)
            weights_exp = jnp.exp(scores - new_peak[:, :, None])
            run_total = run_total * factor + jnp.sum(weights_exp, axis=-1)
            run_acc = run_acc * factor[:, :, None] + jnp.einsum(
                "hqk,khd->hqd",
                weights_exp.astype(jnp.bfloat16),
                value_block,
                preferred_element_type=jnp.float32,
            )
            return ((new_peak, run_total, run_acc), None)

        result, unused = lax.scan(
            fold_one_block, state_carry, (key_blocks, value_blocks, pos_blocks)
        )
        return result

    return fold_keys


def attend_back(
    queries,
    query_pos,
    bias_rows,
    keys_all,
    values_all,
    pos_all,
    grad_att,
    log_total,
    row_delta,
    key_rows,
):
    local_len, head_count = (queries.shape[0], queries.shape[1])
    bucket_count = bias_rows.shape[0]
    block_count = keys_all.shape[0] // key_rows
    key_blocks = keys_all.reshape(block_count, key_rows, head_count, HDIM)
    value_blocks = values_all.reshape(block_count, key_rows, head_count, HDIM)
    pos_blocks = pos_all.reshape(block_count, key_rows)

    def attend_one_block(inner, block_item):
        grad_query, grad_bias = inner
        key_block, value_block, pos_block = block_item
        bucket, probability, grad_scores = pair_terms(
            queries,
            query_pos,
            key_block,
            pos_block,
            value_block,
            grad_att,
            log_total,
            row_delta,
            bias_rows,
        )
        grad_bias = grad_bias + table_grad(bucket, grad_scores, bucket_count)
        scores_low = grad_scores.astype(jnp.bfloat16)
        grad_query = grad_query + jnp.einsum(
            "hqk,khd->qhd", scores_low, key_block, preferred_element_type=jnp.float32
        )
        grad_value = jnp.einsum(
            "hqk,qhd->khd",
            probability.astype(jnp.bfloat16),
            grad_att,
            preferred_element_type=jnp.float32,
        )
        grad_key = jnp.einsum(
            "hqk,qhd->khd", scores_low, queries, preferred_element_type=jnp.float32
        )
        return ((grad_query, grad_bias), (grad_key, grad_value))

    start_state = (
        jnp.zeros((local_len, head_count, HDIM), jnp.float32),
        jnp.zeros((bucket_count, head_count), jnp.float32),
    )
    final_state, stacked = lax.scan(
        attend_one_block, start_state, (key_blocks, value_blocks, pos_blocks)
    )
    total_keys = keys_all.shape[0]
    return (
        final_state[0],
        final_state[1],
        stacked[0].reshape(total_keys, head_count * HDIM),
        stacked[1].reshape(total_keys, head_count * HDIM),
    )


def own_share(grad_term, grad_dim):
    share_len = grad_term.shape[grad_dim] // lax.axis_size("fsdp")
    return lax.dynamic_slice_in_dim(
        grad_term, lax.axis_index("fsdp") * share_len, share_len, grad_dim
    )


def per_device_plain(
    tokens,
    positions,
    w_query,
    w_key,
    w_value,
    w_out,
    w_in,
    w_back,
    gain_one,
    gain_two,
    bias_table,
    cotangent,
):
    micro_count = tokens.shape[0]
    head_count = w_query.shape[1] // HDIM
    head_cols = head_count * HDIM
    hidden_cols = w_in.shape[1]
    bucket_count = bias_table.shape[0] * lax.axis_size("fsdp")
    grad_wq = jnp.zeros((D, head_cols), jnp.float32)
    grad_wk = jnp.zeros((D, head_cols), jnp.float32)
    grad_wv = jnp.zeros((D, head_cols), jnp.float32)
    grad_wo = jnp.zeros((head_cols, D), jnp.float32)
    grad_wi = jnp.zeros((D, hidden_cols), jnp.float32)
    grad_wb = jnp.zeros((hidden_cols, D), jnp.float32)
    grad_table = jnp.zeros((bucket_count, head_count), jnp.float32)
    grad_gain_one = jnp.zeros((D,), jnp.float32)
    grad_gain_two = jnp.zeros((D,), jnp.float32)
    outputs = []
    input_grads = []
    for micro_step in range(micro_count):
        full_wq, full_wk, full_wv, full_wo, full_wi, full_wb, full_g1, full_g2, full_table = (
            lax.all_gather(w_query, "fsdp", axis=0, tiled=True),
            lax.all_gather(w_key, "fsdp", axis=0, tiled=True),
            lax.all_gather(w_value, "fsdp", axis=0, tiled=True),
            lax.all_gather(w_out, "fsdp", axis=1, tiled=True),
            lax.all_gather(w_in, "fsdp", axis=0, tiled=True),
            lax.all_gather(w_back, "fsdp", axis=1, tiled=True),
            lax.all_gather(gain_one, "fsdp", axis=0, tiled=True),
            lax.all_gather(gain_two, "fsdp", axis=0, tiled=True),
            lax.all_gather(bias_table, "fsdp", axis=0, tiled=True),
        )
        gain_first = full_g1.astype(jnp.float32)
        gain_second = full_g2.astype(jnp.float32)
        bias_rows = full_table.astype(jnp.float32)
        token_rows = tokens[micro_step, 0].astype(jnp.float32)
        query_pos = positions[micro_step, 0]
        scale_one = inverse_rms(token_rows)
        normed = spread_rows((token_rows * scale_one * gain_first).astype(jnp.bfloat16))
        local_len = normed.shape[0]
        key_rows = math.gcd(local_len, 256)
        queries_low = jnp.dot(normed, full_wq, preferred_element_type=jnp.float32).astype(
            jnp.bfloat16
        )
        keys_low = jnp.dot(normed, full_wk, preferred_element_type=jnp.float32).astype(jnp.bfloat16)
        values_low = jnp.dot(normed, full_wv, preferred_element_type=jnp.float32).astype(
            jnp.bfloat16
        )
        queries = queries_low.reshape(local_len, head_count, HDIM)
        start_state = (
            jnp.full((head_count, local_len), -1e30, jnp.float32),
            jnp.zeros((head_count, local_len), jnp.float32),
            jnp.zeros((head_count, local_len, HDIM), jnp.float32),
        )
        fold_keys = make_fold(queries, query_pos, bias_rows, key_rows)
        run_peak, run_total, run_acc = fold_keys(
            start_state,
            (
                lax.all_gather(keys_low, "ctx", axis=0, tiled=True),
                lax.all_gather(values_low, "ctx", axis=0, tiled=True),
                lax.all_gather(query_pos, "ctx", axis=0, tiled=True),
            ),
            jnp.int32(0),
        )
        log_total = run_peak + jnp.log(run_total)
        attended_f = jnp.transpose(run_acc / run_total[:, :, None], (1, 0, 2)).reshape(
            local_len, head_cols
        )
        attended = attended_f.astype(jnp.bfloat16)
        middle = token_rows + collect_rows(
            jnp.dot(attended, full_wo, preferred_element_type=jnp.float32)
        )
        scale_two = inverse_rms(middle)
        normed_two = spread_rows((middle * scale_two * gain_second).astype(jnp.bfloat16))
        hidden_pre = jnp.dot(normed_two, full_wi, preferred_element_type=jnp.float32)
        hidden = jax.nn.gelu(hidden_pre, approximate=False).astype(jnp.bfloat16)
        output_rows = middle + collect_rows(
            jnp.dot(hidden, full_wb, preferred_element_type=jnp.float32)
        )
        outputs.append(output_rows.astype(jnp.bfloat16))
        grad_local = cotangent[micro_step, 0]
        grad_full = spread_rows(grad_local)
        grad_wb = grad_wb + left_product(hidden, grad_full)
        grad_hidden = right_product(grad_full, full_wb)
        grad_pre = (grad_hidden * gelu_slope(hidden_pre)).astype(jnp.bfloat16)
        grad_wi = grad_wi + left_product(normed_two, grad_pre)
        grad_normed_two = collect_rows(right_product(grad_pre, full_wi))
        grad_middle, gain_part_two = norm_back(middle, scale_two, gain_second, grad_normed_two)
        grad_middle = grad_middle + grad_local.astype(jnp.float32)
        grad_gain_two = grad_gain_two + gain_part_two
        grad_mixed = spread_rows(grad_middle.astype(jnp.bfloat16))
        grad_wo = grad_wo + left_product(attended, grad_mixed)
        grad_attended = right_product(grad_mixed, full_wo).astype(jnp.bfloat16)
        row_delta = jnp.sum(
            (grad_attended.astype(jnp.float32) * attended_f).reshape(local_len, head_count, HDIM),
            axis=-1,
        ).T
        back_keys, back_values, back_pos = (
            lax.all_gather(keys_low, "ctx", axis=0, tiled=True),
            lax.all_gather(values_low, "ctx", axis=0, tiled=True),
            lax.all_gather(query_pos, "ctx", axis=0, tiled=True),
        )
        grad_att_heads = grad_attended.reshape(local_len, head_count, HDIM)
        grad_queries, table_part, grad_keys_all, grad_values_all = attend_back(
            queries,
            query_pos,
            bias_rows,
            back_keys,
            back_values,
            back_pos,
            grad_att_heads,
            log_total,
            row_delta,
            key_rows,
        )
        grad_keys, grad_values = (
            lax.psum_scatter(
                grad_keys_all.astype(jnp.bfloat16), "ctx", scatter_dimension=0, tiled=True
            ).astype(jnp.float32),
            lax.psum_scatter(
                grad_values_all.astype(jnp.bfloat16), "ctx", scatter_dimension=0, tiled=True
            ).astype(jnp.float32),
        )
        grad_table = grad_table + table_part
        grad_q_low = grad_queries.reshape(local_len, head_cols).astype(jnp.bfloat16)
        grad_k_low = grad_keys.astype(jnp.bfloat16)
        grad_v_low = grad_values.astype(jnp.bfloat16)
        grad_wq = grad_wq + left_product(normed, grad_q_low)
        grad_wk = grad_wk + left_product(normed, grad_k_low)
        grad_wv = grad_wv + left_product(normed, grad_v_low)
        grad_normed = collect_rows(
            right_product(grad_q_low, full_wq)
            + right_product(grad_k_low, full_wk)
            + right_product(grad_v_low, full_wv)
        )
        grad_input, gain_part_one = norm_back(token_rows, scale_one, gain_first, grad_normed)
        grad_gain_one = grad_gain_one + gain_part_one
        input_grads.append((grad_input + grad_middle).astype(jnp.bfloat16))
    gain_total_one, gain_total_two = lax.psum((grad_gain_one, grad_gain_two), ("fsdp", "ctx", "tp"))
    sum_wq, sum_wk, sum_wv, sum_wo, sum_wi, sum_wb, sum_table = lax.psum(
        (grad_wq, grad_wk, grad_wv, grad_wo, grad_wi, grad_wb, grad_table), ("fsdp", "ctx")
    )
    share_wq = own_share(sum_wq, 0)
    share_wk = own_share(sum_wk, 0)
    share_wv = own_share(sum_wv, 0)
    share_wo = own_share(sum_wo, 1)
    share_wi = own_share(sum_wi, 0)
    share_wb = own_share(sum_wb, 1)
    share_table = own_share(sum_table, 0)
    return (
        jnp.stack(outputs)[:, None],
        jnp.stack(input_grads)[:, None],
        own_share(gain_total_one, 0),
        own_share(gain_total_two, 0),
        share_wq,
        share_wk,
        share_wv,
        share_wo,
        share_wi,
        share_wb,
        share_table,
    )


MESH = pl.DeviceIdType.MESH
F32 = jnp.float32
BF16 = jnp.bfloat16
HEADS_HERE = 3
BLK = 128
VALUE_ROWS = (128, 192, 64)


def nn(left, right):
    return lax.dot_general(left, right, (((1,), (0,)), ((), ())), preferred_element_type=F32)


def nt(left, right):
    return lax.dot_general(left, right, (((1,), (1,)), ((), ())), preferred_element_type=F32)


def tn(left, right):
    return lax.dot_general(left, right, (((0,), (0,)), ((), ())), preferred_element_type=F32)


def at_rows(offset, size, unit):
    return pl.ds(pl.multiple_of(offset, unit), size)


def fold_rows(block):
    return jnp.sum(block.reshape(block.shape[0] // 8, 8, block.shape[1]), axis=0)


class Sems:
    def __init__(self):
        self.numbers = {}

    def __call__(self, *name):
        return self.numbers.setdefault(name, len(self.numbers))


PART = 256
REACH = (0, 1, 2, 3, 4, 5, 6, 7, 11, 15, 22, 31, 45, 63, 90, 127)


def grad_chunks(share, hidden):
    head_cols = HEADS_HERE * HDIM
    names = [(f"back{i}", PART, share) for i in range(hidden // PART)]
    names += [(f"in{i}", share, PART) for i in range(hidden // PART)]
    names += [(name, head_cols, share) for name in ("out", "key", "value", "query")]
    chunks, row = [], 0
    for name, rows, cols in names:
        chunks.append((name, row, rows, cols))
        row += rows
    return chunks, row


def layer_kernel(
    nf, nc, micro, rows_own, share, hidden, n_sems, sems,
    tok, pos_in, wq_in, wk_in, wv_in, wo_loc, wi_loc, wb_loc, g1_in, g2_in, table_in, cot,
    out, grad_in, grads_out, small_out,
    w_loc, small_loc, wqkv, wo, wi, wb, small_rx, smallf, n1, g, posb, bkt, bias, qm, kv, e_t, s_t, ds_t, att_t,
    inv, att, keep, keep6, send1, send2, recv1, recv2, zsend, zrecv, gz, n2, hid, gp, gm,
    mid_f, gmid, dq, dom, nds, gacc, tacc, facc, gain2, xs, xr, zr1, zr2, sm, smr,
    ssem, rsem, lsem,
):
    f, c, t = lax.axis_index("fsdp"), lax.axis_index("ctx"), lax.axis_index("tp")
    nt_ = 4
    T = rows_own
    R = nt_ * T
    L = nc * R
    NB = L // BLK
    t1 = t + 1 - 2 * lax.rem(t, 2)
    t2 = lax.rem(t + 2, 4)
    t3 = lax.rem(t1 + 2, 4)
    sib, ypeer = (f, c, t1), (f, c, t2)
    xpeers = [(lax.rem(f + j, nf), c, t) for j in range(1, nf)]
    zpeers = [(f, lax.rem(c + k, nc), t) for k in range(1, nc)]
    below, above = (f, jnp.maximum(c - 1, 0), t), (f, jnp.minimum(c + 1, nc - 1), t)
    half_c = nc // 2
    low_side = c < half_c
    inward = jnp.where(low_side, c + 1, c - 1)
    outward = jnp.clip(jnp.where(low_side, c - 1, c + 1), 0, nc - 1)
    is_mid = (c == half_c - 1) | (c == half_c)
    has_out = (c > 0) & (c < nc - 1)
    if nc == 2:
        has_out = c < 0
    chunks, chunk_rows = grad_chunks(share, hidden)
    pending = []
    zs = xs.at[0]
    scr = s_t.at[pl.ds(0, 4 * rows_own)]

    def send(src, dst, name_s, name_r, dev, when=None):
        copy = pltpu.make_async_remote_copy(
            src, dst, ssem.at[sems(*name_s)], rsem.at[sems(*name_r)], device_id=dev, device_id_type=MESH
        )
        if when is None:
            copy.start()
        else:
            pl.when(when)(copy.start)
        pending.append((name_s, copy, when))

    def sent(*name_s):
        for at, (name, copy, when) in enumerate(pending):
            if name == name_s:
                if when is None:
                    copy.wait_send()
                else:
                    pl.when(when)(copy.wait_send)
                del pending[at]
                return

    def arrived(dst, *name_r):
        pltpu.make_async_remote_copy(
            dst, dst, ssem.at[sems(*name_r)], rsem.at[sems(*name_r)], device_id=sib, device_id_type=MESH
        ).wait_recv()

    def rms(rows):
        return lax.rsqrt(jnp.mean(rows * rows, axis=-1, keepdims=True) + epsilon)

    def piece(m, block, t_of):
        return n1.at[at_rows(m * L + block * R + t_of * T, T, T)]

    def rows_of(m, t_of):
        return at_rows(m * R + t_of * T, T, T)

    posb[0] = jnp.zeros_like(posb[0])
    posb[2] = jnp.zeros_like(posb[2])
    barrier = pltpu.get_barrier_semaphore()
    peers = [sib, ypeer] + xpeers + zpeers
    for dev in peers:
        pl.semaphore_signal(barrier, inc=1, device_id=dev, device_id_type=MESH)
    for m in range(micro):
        rows = tok[m].astype(F32)
        n1[at_rows(m * L + c * R + t * T, T, T)] = (rows * rms(rows)).astype(BF16)
    posb[1] = pos_in[...]
    local = {}

    def local_copy(src, dst, i):
        copy = pltpu.make_async_copy(src, dst, lsem.at[i])
        copy.start()
        local[i] = copy

    share_cols = at_rows(f * share, share, BLK)
    share_rows = at_rows(f * share, share, BLK)
    own_rows = at_rows(t * T, T, T)
    qkv_parts = (
        (wq_in, 0, 0, 192), (wk_in, 0, 256, 192), (wv_in, 128, 448, 64), (wv_in, 0, 512, 128),
    )
    for i, (src, row, at, size) in enumerate(qkv_parts):
        local_copy(src.at[pl.ds(row, size)], w_loc.at[pl.ds(at, size)], 4 + micro + len(chunks) + i)
    local_copy(wo_loc.at[pl.ds(0, 128)], wo.at[pl.ds(128, 128), share_cols], 0)
    local_copy(wo_loc.at[pl.ds(128, 64)], wo.at[pl.ds(64, 64), share_cols], 1)
    local_copy(wi_loc, wi.at[share_rows], 2)
    local_copy(wb_loc, wb.at[:, share_cols], 3)
    for m in range(micro):
        local_copy(cot.at[m], g.at[rows_of(m, t)], 4 + m)
    small_loc[...] = jnp.zeros_like(small_loc)
    small_loc[0:1, share_cols] = g1_in[...].astype(F32).reshape(1, share)
    small_loc[1:2, share_cols] = g2_in[...].astype(F32).reshape(1, share)
    buckets_here = table_in.shape[1]
    spot = lax.broadcasted_iota(jnp.int32, (buckets_here, 128), 1) - f * buckets_here
    spot = spot == lax.broadcasted_iota(jnp.int32, (buckets_here, 128), 0)
    small_loc[0:HEADS_HERE, pl.ds(D, 128)] = nn(table_in[...], jnp.where(spot, 1.0, 0.0).astype(BF16))

    small_rx[f] = small_loc[...]
    pl.semaphore_wait(barrier, len(peers))

    def spread_first(m):
        mine = piece(m, c, t)
        send(mine, mine, ("ny", m, 0), ("ny", m, 0), ypeer)
        send(mine, mine, ("nd", m), ("nz", m, 1), below, c > 0)
        send(mine, mine, ("nu", m), ("nz", m, nc - 1), above, c < nc - 1)
        send(mine, mine, ("ns", m, 0), ("ns", m, 0), sib)

    def send_small():
        for j, dev in enumerate(xpeers):
            send(small_loc, small_rx.at[f], ("small", j), ("small", nf - 2 - j), dev)
        send(pos_in, posb.at[0], ("posu",), ("posu",), (f, jnp.minimum(c + 1, nc - 1), t), c < nc - 1)
        send(pos_in, posb.at[2], ("posd",), ("posd",), (f, jnp.maximum(c - 1, 0), t), c > 0)

    def send_qkv():
        for j, dev in enumerate(xpeers):
            for i, (src, row, at, size) in enumerate(qkv_parts):
                dst = wqkv.at[pl.ds(at, size), share_cols]
                send(src.at[pl.ds(row, size)], dst, ("wqkv", i, j), ("wqkv", i, nf - 2 - j), dev)

    def send_wo():
        for j, dev in enumerate(xpeers):
            send(wo_loc.at[pl.ds(0, 128)], wo.at[pl.ds(128, 128), share_cols], ("woa", j), ("woa", nf - 2 - j), dev)
            send(wo_loc.at[pl.ds(128, 64)], wo.at[pl.ds(64, 64), share_cols], ("wob", j), ("wob", nf - 2 - j), dev)

    def send_wi():
        for j, dev in enumerate(xpeers):
            send(wi_loc, wi.at[share_rows], ("wi", j), ("wi", nf - 2 - j), dev)

    def send_wb():
        for j, dev in enumerate(xpeers):
            send(wb_loc, wb.at[:, share_cols], ("wb", j), ("wb", nf - 2 - j), dev)

    def share_g(m):
        local[4 + m].wait()
        spread_own("g", g, m)

    def clear():
        w_loc[192:256] = jnp.zeros((64, share), BF16)
        wqkv[192:256] = jnp.zeros((64, D), BF16)
        wo[pl.ds(0, 64)] = jnp.zeros((64, D), BF16)
        dom[...] = jnp.zeros_like(dom)
        tacc[...] = jnp.zeros_like(tacc)
        facc[...] = jnp.zeros_like(facc)
        sm[0] = jnp.zeros((8, D + 128), F32)

    def spread_own(name, buf, m):
        mine = buf.at[rows_of(m, t)]
        send(mine, mine, (name, "y", m), (name, "y", m), ypeer)
        send(mine, mine, (name, "s", m), (name, "s", m), sib)

    def spread_on(name, buf, m):
        there = buf.at[rows_of(m, t2)]
        arrived(there, name, "y", m)
        send(there, there, (name, "f", m), (name, "f", m), sib)

    def spread_end(name, buf, m):
        arrived(buf.at[rows_of(m, t1)], name, "s", m)
        arrived(buf.at[rows_of(m, t3)], name, "f", m)

    def line_block(h, low):
        if low:
            return c >= h, jnp.maximum(c - h, 0), nc - h
        return c + h < nc, jnp.minimum(c + h, nc - 1), h

    def gather_z(m, h, low):
        there, z, k = line_block(h, low)
        block = piece(m, z, t)

        @pl.when(there)
        def _():
            arrived(block, "nz", m, k)

        if h < nc - 1 and low:
            send(block, block, ("nzu", m, k), ("nz", m, k - 1), above, there & (c < nc - 1))
        elif h < nc - 1:
            send(block, block, ("nzd", m, k), ("nz", m, k + 1), below, there & (c > 0))
        send(block, block, ("ny", m, k, low), ("ny", m, k), ypeer, there)
        send(block, block, ("ns", m, k, low), ("ns", m, k), sib, there)

    def gather_own(m):
        block = piece(m, c, t2)
        arrived(block, "ny", m, 0)
        send(block, block, ("nf", m, 0), ("nf", m, 0), sib)

    def gather_y(m, h, low):
        there, z, k = line_block(h, low)
        block = piece(m, z, t2)

        @pl.when(there)
        def _():
            arrived(block, "ny", m, k)

        send(block, block, ("nf", m, k, low), ("nf", m, k), sib, there)

    def gather_end(m):
        for k in range(nc):
            z = lax.rem(c + k, nc)
            arrived(piece(m, z, t1), "ns", m, k)
            arrived(piece(m, z, t3), "nf", m, k)

    def take_small():
        for j in range(nf - 1):
            arrived(small_rx.at[lax.rem(f + 1 + j, nf)], "small", j)
        total = small_rx[0]
        for j in range(1, nf):
            total = total + small_rx[j]
        smallf[...] = total

    def take_positions():
        @pl.when(c > 0)
        def _():
            arrived(posb.at[0], "posu")

        @pl.when(c < nc - 1)
        def _():
            arrived(posb.at[2], "posd")

    def bias_of(m):
        for qb in range(2):
            query_row = posb[1, m, :, pl.ds(qb * BLK, BLK)]
            for d in (-1, 0, 1):
                slot, row = ((0, 1), (1, 0), (1, 1), (2, 0))[qb + d + 1]
                key_row = posb[slot, m, :, pl.ds(row * BLK, BLK)]
                key_col = jnp.transpose(jnp.broadcast_to(key_row, (BLK, BLK)))
                relative = key_col - query_row
                size = jnp.abs(relative)
                bucket = jnp.minimum(size, 8)
                for edge_value in bucket_edges:
                    bucket = bucket + (size >= edge_value).astype(jnp.int32)
                bucket = bucket + 16 * (relative > 0).astype(jnp.int32)
                sub = qb * 3 + d + 1
                bkt[m, sub] = bucket
                for h in range(HEADS_HERE):
                    row_of = jnp.broadcast_to(smallf[h : h + 1, pl.ds(D, 128)], (BLK, BLK))
                    bias[m, sub, h] = jnp.take_along_axis(row_of, bucket, axis=1).astype(BF16)

    def fold_gain():
        for i in range(len(qkv_parts)):
            local[4 + micro + len(chunks) + i].wait()
        wqkv[:, share_cols] = w_loc[...]
        for j in range(nf - 1):
            cols = at_rows(lax.rem(f + 1 + j, nf) * share, share, BLK)
            for i, (src, row, at, size) in enumerate(qkv_parts):
                arrived(wqkv.at[pl.ds(at, size), cols], "wqkv", i, j)
        wqkv[...] = (wqkv[...].astype(F32) * smallf[0:1, 0:D]).astype(BF16)

    def reduce_start(slot, rid, kept, value, previous):
        scr[...] = value
        if previous is not None:
            sent("r1", previous)
        send1[slot, 0] = scr[at_rows(t1 * T, T, T)].astype(BF16)
        send1[slot, 1] = scr[at_rows(t3 * T, T, T)].astype(BF16)
        send(send1.at[slot], recv1.at[rid], ("r1", rid), ("r1", rid), sib)
        kept[0] = scr[own_rows].astype(kept.dtype)
        kept[1] = scr[at_rows(t2 * T, T, T)].astype(kept.dtype)

    def reduce_mid(slot, rid, kept, previous):
        arrived(recv1.at[rid], "r1", rid)
        if previous is not None:
            sent("r2", previous)
        send2[slot] = (kept[1].astype(F32) + recv1[rid, 1].astype(F32)).astype(BF16)
        send(send2.at[slot], recv2.at[rid], ("r2", rid), ("r2", rid), ypeer)
        kept[0] = (kept[0].astype(F32) + recv1[rid, 0].astype(F32)).astype(kept.dtype)

    def reduce_end(rid, kept):
        arrived(recv2.at[rid], "r2", rid)
        return kept[0].astype(F32) + recv2[rid].astype(F32)

    def phase(p, m):
        rid = p * micro + m
        return p, rid, keep.at[2 * p + m % 2], (rid - 1 if m > 0 else None)

    def start_phase(p, m, value):
        slot, rid, kept, previous = phase(p, m)
        reduce_start(slot, rid, kept, value, previous)

    def mid_phase(p, m):
        slot, rid, kept, previous = phase(p, m)
        reduce_mid(slot, rid, kept, previous)

    def end_phase(p, m):
        slot, rid, kept, previous = phase(p, m)
        return reduce_end(rid, kept)

    wide_cols = HEADS_HERE * R

    def far_row(kb, below, above):
        parts = []
        for h in range(HEADS_HERE):
            for qb in range(2):
                d = kb - 2 * c - qb
                parts.append(jnp.where(d < -1, below[h], jnp.where(d > 1, above[h], 0.0)))
        return jnp.concatenate(parts, axis=1)

    def near_blocks(use):
        for qb in range(2):
            for d in (-1, 0, 1):
                kb = 2 * c + qb + d
                if qb + d in (0, 1):
                    use(qb, d, kb)
                else:
                    pl.when((kb >= 0) & (kb < NB))(functools.partial(use, qb, d, kb))

    def project(m):
        own = at_rows(m * L + c * R, R, R)
        queries = nt(n1[own], wqkv[0:256])
        lane = lax.broadcasted_iota(jnp.int32, (R, 256), 1)
        for h in range(HEADS_HERE):
            keep_it = (lane >= h * HDIM) & (lane < (h + 1) * HDIM)
            qm[m, pl.ds(h * R, R)] = jnp.where(keep_it, queries, 0.0).astype(BF16)
        kv[pl.ds(m * L, L)] = nt(n1[pl.ds(m * L, L)], wqkv[256:640]).astype(BF16)

    def attend(m):
        first = m * L
        every = pl.ds(first, L)
        s_t[...] = nt(kv[every, 0:256], qm[m])
        tables = [smallf[h : h + 1, pl.ds(D, 128)] for h in range(HEADS_HERE)]
        below = [jnp.broadcast_to(tab[:, 15:16], (1, BLK)) for tab in tables]
        above = [jnp.broadcast_to(tab[:, 31:32], (1, BLK)) for tab in tables]

        def near(qb, d, kb):
            r = at_rows(kb * BLK, BLK, BLK)
            for h in range(HEADS_HERE):
                q = pl.ds(h * R + qb * BLK, BLK)
                s_t[r, q] = s_t[r, q] + bias[m, qb * 3 + d + 1, h].astype(F32)

        near_blocks(near)

        def peak(kb, top):
            block = s_t[at_rows(kb * BLK, BLK, BLK)]
            block = jnp.max(block.reshape(BLK // 8, 8, wide_cols), axis=0)
            return jnp.maximum(top, block + far_row(kb, below, above))

        top = lax.fori_loop(0, NB, peak, jnp.full((8, wide_cols), -jnp.inf, F32))
        top = jnp.max(top, axis=0, keepdims=True)

        def expo(kb, total):
            weights = jnp.exp(s_t[at_rows(kb * BLK, BLK, BLK)] - (top - far_row(kb, below, above)))
            e_t[at_rows(first + kb * BLK, BLK, BLK)] = weights.astype(BF16)
            return total + fold_rows(weights)

        total = lax.fori_loop(0, NB, expo, jnp.zeros((8, wide_cols), F32))
        over = 1.0 / jnp.sum(total, axis=0, keepdims=True)
        inv[m] = jnp.broadcast_to(over, (8, wide_cols))
        mixed = tn(kv[every, 128:384], e_t[every])
        for h in range(HEADS_HERE):
            v0 = VALUE_ROWS[h]
            cols = slice(h * R, (h + 1) * R)
            att_t[m, pl.ds(v0, HDIM)] = mixed[v0 : v0 + HDIM, cols] * over[:, cols]
        att_t[m, pl.ds(0, HDIM)] = jnp.zeros((HDIM, R), F32)
        attended = jnp.transpose(att_t[m]).astype(BF16)
        att[pl.ds(m * R, R)] = attended

    def mix(m):
        start_phase(0, m, nn(att[pl.ds(m * R, R)], wo[...]))

    def take_wo():
        local[0].wait()
        local[1].wait()
        for j in range(nf - 1):
            cols = at_rows(lax.rem(f + 1 + j, nf) * share, share, BLK)
            arrived(wo.at[pl.ds(128, 128), cols], "woa", j)
            arrived(wo.at[pl.ds(64, 64), cols], "wob", j)

    def take_wi():
        local[2].wait()
        for j in range(nf - 1):
            arrived(wi.at[at_rows(lax.rem(f + 1 + j, nf) * share, share, BLK)], "wi", j)

    def take_wb():
        local[3].wait()
        for j in range(nf - 1):
            arrived(wb.at[:, at_rows(lax.rem(f + 1 + j, nf) * share, share, BLK)], "wb", j)

    def norm_two(m):
        middle = tok[m].astype(F32) + end_phase(0, m)
        mid_f[m] = middle
        n2[rows_of(m, t)] = (middle * rms(middle) * smallf[1:2, 0:D]).astype(BF16)
        spread_own("n2", n2, m)

    def feed(m):
        spread_end("n2", n2, m)
        here = pl.ds(m * R, R)
        rows = n2[here]

        def one(i, unused):
            cols = at_rows(i * 256, 256, 256)
            pre = nn(rows, wi[:, cols])
            slope = nt(g[here], wb[cols])
            bell = 0.5 * (1.0 + lax.erf(pre * 0.7071067811865476))
            hid[here, cols] = (pre * bell).astype(BF16)
            bell = bell + pre * jnp.exp(-0.5 * pre * pre) * 0.3989422804014327
            gp[here, cols] = (slope * bell).astype(BF16)
            return unused

        lax.fori_loop(0, hidden // 256, one, 0)
        start_phase(1, m, nt(gp[here], wi[...]))
        start_phase(2, m, nn(hid[here], wb[...]))

    def output_rows(m):
        out[m] = (mid_f[m] + end_phase(2, m)).astype(BF16)

    def back_two(m):
        grad_normed = end_phase(1, m)
        middle = mid_f[m]
        scale = rms(middle)
        unit = middle * scale
        part = fold_rows(grad_normed * unit)
        gain2[...] = part if m == 0 else gain2[...] + part
        weighted = smallf[1:2, 0:D] * grad_normed
        grad = scale * (weighted - unit * jnp.mean(unit * weighted, axis=-1, keepdims=True))
        grad = grad + g[rows_of(m, t)].astype(F32)
        gmid[m] = grad
        gm[rows_of(m, t)] = grad.astype(BF16)
        spread_own("gm", gm, m)

    def attend_back(m):
        first = m * L
        every = pl.ds(first, L)
        grad_att = nt(wo[...], gm[pl.ds(m * R, R)]).astype(BF16).astype(F32)
        deltas = []
        for h in range(HEADS_HERE):
            v0 = VALUE_ROWS[h]
            scaled = (grad_att[v0 : v0 + HDIM] * inv[m, 0:1, pl.ds(h * R, R)]).astype(BF16)
            dom[pl.ds(v0, HDIM), pl.ds(h * R, R)] = scaled
            deltas.append(jnp.sum(scaled.astype(F32) * att_t[m, pl.ds(v0, HDIM)], axis=0, keepdims=True))
        delta = jnp.concatenate(deltas, axis=1)
        s_t[...] = nn(kv[every, 128:384], dom[...])
        half = lax.rem(lax.broadcasted_iota(jnp.int32, (8, wide_cols), 1) // BLK, 2)

        def one_block(kb, sums):
            r = at_rows(kb * BLK, BLK, BLK)
            grad = e_t[at_rows(first + kb * BLK, BLK, BLK)].astype(F32) * (s_t[r] - delta)
            ds_t[r] = grad.astype(BF16)
            part = fold_rows(grad)
            d = kb - 2 * c - half
            return sums[0] + jnp.where(d < -1, part, 0.0), sums[1] + jnp.where(d > 1, part, 0.0)

        zero = jnp.zeros((8, wide_cols), F32)
        low, high = lax.fori_loop(0, NB, one_block, (zero, zero))
        facc[0] += low
        facc[1] += high

        def save(qb, d, kb):
            r = at_rows(kb * BLK, BLK, BLK)
            for h in range(HEADS_HERE):
                nds[m, qb * 3 + d + 1, h] = ds_t[r, pl.ds(h * R + qb * BLK, BLK)]

        near_blocks(save)
        grad_q = tn(kv[every, 0:256], ds_t[...])
        columns = [grad_q[h * HDIM : (h + 1) * HDIM, h * R : (h + 1) * R] for h in range(HEADS_HERE)]
        columns.append(jnp.zeros((HDIM, R), F32))
        dq[pl.ds(m * R, R)] = jnp.transpose(jnp.concatenate(columns, axis=0)).astype(BF16)
        grad_k = nn(ds_t[...], qm[m])
        grad_v = nt(e_t[every], dom[...])
        kv[every, 0:128] = grad_k[:, 0:128].astype(BF16)
        kv[every, 128:256] = (grad_k[:, 128:256] + grad_v[:, 0:128]).astype(BF16)
        kv[every, 256:384] = grad_v[:, 128:256].astype(BF16)

    def merged(block, spots):
        where_at, parts = spots
        size = BLK // parts
        out_block = block[(parts - 1) * size :]
        for i in range(parts - 2, -1, -1):
            out_block = jnp.where(where_at == i, block[i * size : (i + 1) * size], out_block)
        return out_block

    def spots_of(parts):
        size = BLK // parts
        lane = lax.broadcasted_iota(jnp.int32, (size, BLK), 1)
        tile = lax.broadcasted_iota(jnp.int32, (size, BLK), 0) // 8
        away = lane - 8 * tile - 4 + size // 2
        spot = jnp.zeros((size, BLK), jnp.int32)
        for i in range(1, parts):
            spot = spot + (away >= i * size).astype(jnp.int32)
        return spot, parts

    def bin_table(m):
        def use(qb, d, kb):
            sub = qb * 3 + d + 1

            def bins(names, ids, blocks):
                for b in names:
                    same = ids == b
                    for h in range(HEADS_HERE):
                        tacc[h, b] += fold_rows(jnp.where(same, blocks[h], 0.0))

            if d == 0:
                ids = bkt[m, sub]
                blocks = [nds[m, sub, h].astype(F32) for h in range(HEADS_HERE)]
                for parts, sizes in ((4, range(0, 9)), (2, range(9, 11))):
                    spots = spots_of(parts)
                    both = [b for b in sizes] + [16 + b for b in sizes if b > 0]
                    bins(both, merged(ids, spots), [merged(block, spots) for block in blocks])
                bins([b + s for b in range(11, 16) for s in (0, 16)], ids, blocks)
            else:
                for size in range(1, 16):
                    rows = min(BLK, (REACH[size] + 7) // 8 * 8)
                    low = (rows + 15) // 16 * 16
                    r = pl.ds(BLK - rows if d < 0 else 0, rows)
                    part = slice(low - rows, low) if d < 0 else slice(0, rows)
                    low = pl.ds(BLK - low if d < 0 else 0, low)
                    blocks = [nds[m, sub, h, low].astype(F32)[part] for h in range(HEADS_HERE)]
                    bins([size if d < 0 else 16 + size], bkt[m, sub, r], blocks)

        near_blocks(use)

    def six(m, k):
        return 3 + k, 3 * micro + m * nc + k, keep6.at[k], (3 * micro + (m - 1) * nc + k if m > 0 else None)

    def back_start(m, k):
        r = at_rows(m * L + lax.rem(c + k, nc) * R, R, R)
        value = nn(kv[r], wqkv[256:640])
        if k == 0:
            value = value + nn(dq[pl.ds(m * R, R)], wqkv[0:256])
        slot, rid, kept, previous = six(m, k)
        reduce_start(slot, rid, kept, value, previous)

    def back_mid(m, k):
        slot, rid, kept, previous = six(m, k)
        reduce_mid(slot, rid, kept, previous)

    def back_out(m, k):
        slot, rid, kept, previous = six(m, k)
        gz[m] = reduce_end(rid, kept)

    def line_slot(m, h, up):
        if h == 0:
            return zrecv.at[m, nc - 1 + int(up)]
        return zrecv.at[m, (h if up else nc - h) - 1]

    def back_pass(m, h, up):
        there, z, k = line_block(h, not up)
        slot, rid, kept, previous = six(m, k)
        if m > 0:
            sent("gs", m - 1, h, up)
        more = c > 0 if up else c < nc - 1

        @pl.when(there & more)
        def _():
            arrived(line_slot(m, h, up), "gp", m, h, up)
            total = reduce_end(rid, kept) + line_slot(m, h, up)[...].astype(F32)
            zsend[k - 1] = total.astype(BF16)

        @pl.when(there & jnp.logical_not(more))
        def _():
            zsend[k - 1] = reduce_end(rid, kept).astype(BF16)

        dev = above if up else below
        send(zsend.at[k - 1], line_slot(m, h - 1, up), ("gs", m, h, up), ("gp", m, h - 1, up), dev, there)

    def back_one(m):
        for up, some in ((True, c > 0), (False, c < nc - 1)):

            @pl.when(some)
            def _(up=up):
                arrived(line_slot(m, 0, up), "gp", m, 0, up)
                gz[m] += line_slot(m, 0, up)[...].astype(F32)

        weighted = gz[m]
        rows = tok[m].astype(F32)
        scale = rms(rows)
        unit = rows * scale
        grad = scale * (weighted - unit * jnp.mean(unit * weighted, axis=-1, keepdims=True))
        grad_in[m] = (gmid[m] + grad).astype(BF16)

    def gather_grads(m):
        own = at_rows(m * L + c * R, R, R)
        every = pl.ds(m * L, L)
        for rows, value in (
            (pl.ds(0, 256), tn(dq[pl.ds(m * R, R)], n1[own])),
            (pl.ds(256, 384), tn(kv[every], n1[every])),
        ):
            gacc[rows] = value if m == 0 else gacc[rows] + value

    def each_part(chunk, part, use):
        name, row, rows, cols = chunk
        share_at = at_rows(part, share, BLK)
        if name.startswith("back"):
            use(row, rows, tn(hid[:, pl.ds(int(name[4:]) * PART, PART)], g[:, share_at]), None)
        elif name.startswith("in"):
            use(row, rows, tn(n2[:, share_at], gp[:, pl.ds(int(name[2:]) * PART, PART)]), None)
        elif name == "out":
            value = tn(att[...], gm[:, share_at])
            use(row, 128, value[128:], None)
            use(row + 128, 64, value[64:128], None)
        elif name == "value":
            use(row, 128, gacc[pl.ds(512, 128), share_at], 512)
            use(row + 128, 64, gacc[pl.ds(448, 64), share_at], 448)
        else:
            first = 0 if name == "query" else 256
            use(row, rows, gacc[pl.ds(first, rows), share_at], first)

    def share_out(q):
        chunk = chunks[q]
        name, row, rows, cols = chunk
        for j, dev in enumerate(xpeers):
            part = lax.rem(f + 1 + j, nf) * share

            def use(at, size, value, first, j=j):
                xs[j, pl.ds(at, size), 0:cols] = value.astype(BF16)

            each_part(chunk, part, use)
            src = xs.at[j, pl.ds(row, rows), pl.ds(0, cols)]
            dst = xr.at[nf - 2 - j, pl.ds(row, rows), pl.ds(0, cols)]
            send(src, dst, ("x", q, j), ("x", q, nf - 2 - j), dev)

    def own_share(q):
        chunk = chunks[q]
        name, row, rows, cols = chunk
        for j in range(nf - 1):
            arrived(xr.at[j, pl.ds(row, rows), pl.ds(0, cols)], "x", q, j)
        sent("x", q, 0)

        def use(at, size, value, first):
            for j in range(nf - 1):
                value = value + xr[j, pl.ds(at, size), 0:cols].astype(F32)
            if first is not None:
                weight = w_loc[pl.ds(first, size)].astype(F32)
                sm[0, 0:1, share_cols] += jnp.sum(weight * value, axis=0, keepdims=True)
                value = value * smallf[0:1, share_cols]
            zs[pl.ds(at, size), 0:cols] = value.astype(BF16)

        each_part(chunk, f * share, use)

    def first_inward(q):
        own_share(q)
        name, row, rows, cols = chunks[q]
        at = (pl.ds(row, rows), pl.ds(0, cols))
        dev = (f, inward, t)
        if nc == 2:
            send(zs.at[at], zr2.at[at], ("ze", q), ("zx", q), dev)
        else:
            send(zs.at[at], zr1.at[at], ("ze", q), ("zi", q), dev, jnp.logical_not(has_out))

    def then_inward(q):
        if nc == 2:
            return
        name, row, rows, cols = chunks[q]
        at = (pl.ds(row, rows), pl.ds(0, cols))

        @pl.when(has_out)
        def _():
            arrived(zr1.at[at], "zi", q)
            zs[at] = (zs[at].astype(F32) + zr1[at].astype(F32)).astype(BF16)

        send(zs.at[at], zr2.at[at], ("zm", q), ("zx", q), (f, inward, t), is_mid)

    def then_outward(q):
        name, row, rows, cols = chunks[q]
        at = (pl.ds(row, rows), pl.ds(0, cols))

        @pl.when(is_mid)
        def _():
            arrived(zr2.at[at], "zx", q)
            zr2[at] = (zs[at].astype(F32) + zr2[at].astype(F32)).astype(BF16)

        if nc > 2:
            send(zr2.at[at], zr2.at[at], ("zo", q), ("zo", q), (f, outward, t), has_out)

    def last_outward(q):
        name, row, rows, cols = chunks[q]
        at = (pl.ds(row, rows), pl.ds(0, cols))

        @pl.when(jnp.logical_not(is_mid))
        def _():
            arrived(zr2.at[at], "zo", q)

        local_copy(zr2.at[at], grads_out.at[at], 4 + micro + q)

    def small_start():
        g2 = jnp.sum(gain2[...], axis=0, keepdims=True)
        sm[0, 1:2, 0:D] = g2
        for h in range(HEADS_HERE):
            below = jnp.sum(jnp.sum(facc[0, :, pl.ds(h * R, R)], axis=0, keepdims=True), axis=1, keepdims=True)
            above = jnp.sum(jnp.sum(facc[1, :, pl.ds(h * R, R)], axis=0, keepdims=True), axis=1, keepdims=True)
            per = jnp.sum(tacc[h], axis=1)
            per = jnp.sum(jnp.concatenate([per, jnp.zeros((96, 128), F32)], axis=0), axis=1, keepdims=True)
            line = jnp.transpose(jnp.broadcast_to(per, (128, 128)))[0:1, :]
            lane = lax.broadcasted_iota(jnp.int32, (1, 128), 1)
            line = line + jnp.where(lane == 15, below, 0.0) + jnp.where(lane == 31, above, 0.0)
            sm[0, h : h + 1, pl.ds(D, 128)] = line

    def small_send(step):
        if step == 0:
            send(sm.at[0], smr.at[0], ("m", 0), ("m", 0), sib)
        elif step == 1:
            send(sm.at[1], smr.at[1], ("m", 1), ("m", 1), ypeer)
        elif step == 2:
            for j, dev in enumerate(xpeers):
                send(sm.at[2], smr.at[2 + nf - 2 - j], ("mx", j), ("mx", nf - 2 - j), dev)
        else:
            for k in range(1, nc):
                send(sm.at[3], smr.at[1 + nf + nc - k - 1], ("mz", k), ("mz", nc - k), zpeers[k - 1])

    def small_take(step):
        if step < 2:
            arrived(smr.at[step], "m", step)
            lanes = lax.broadcasted_iota(jnp.int32, (8, D + 128), 1)
            sm[step + 1] = sm[step] + jnp.where(lanes < D, smr[step], 0.0)
        elif step == 2:
            total = sm[2]
            for j in range(nf - 1):
                arrived(smr.at[2 + j], "mx", j)
                total = total + smr[2 + j]
            sm[3] = total
        else:
            total = sm[3]
            for k in range(1, nc):
                arrived(smr.at[1 + nf + k - 1], "mz", k)
                total = total + smr[1 + nf + k - 1]
            small_out[...] = total
            smr[0] = total
            for i in range(2):
                small_out[i : i + 1, 0:share] = smr[0, i : i + 1, share_cols]

    spread_first(0)
    share_g(0)
    send_small()
    send_qkv()
    send_wo()
    send_wi()
    send_wb()
    clear()
    spread_first(1)
    spread_first(2)
    share_g(2)
    share_g(1)
    take_positions()
    take_small()
    bias_of(0)
    bias_of(1)
    bias_of(2)
    gather_z(0, 1, False)
    gather_own(0)
    gather_z(0, 1, True)
    gather_z(1, 1, False)
    gather_z(1, 1, True)
    spread_on("g", g, 0)
    spread_end("g", g, 0)
    gather_own(1)
    gather_z(2, 1, False)
    gather_z(2, 1, True)
    gather_z(0, 2, False)
    gather_z(0, 2, True)
    gather_own(2)
    gather_z(1, 2, False)
    spread_on("g", g, 2)
    gather_z(1, 2, True)
    fold_gain()
    spread_end("g", g, 2)
    spread_on("g", g, 1)
    gather_z(2, 2, False)
    gather_z(2, 2, True)
    take_wo()
    spread_end("g", g, 1)
    gather_z(0, 3, True)
    gather_z(0, 3, False)
    gather_y(0, 1, False)
    gather_z(1, 3, True)
    gather_y(0, 1, True)
    gather_z(1, 3, False)
    gather_y(1, 1, False)
    gather_z(2, 3, False)
    gather_z(2, 3, True)
    gather_y(1, 1, True)
    gather_y(2, 1, False)
    gather_y(2, 1, True)
    take_wi()
    gather_y(0, 2, False)
    gather_y(0, 2, True)
    gather_y(0, 3, False)
    gather_y(0, 3, True)
    gather_end(0)
    project(0)
    gather_y(1, 3, True)
    gather_y(1, 2, False)
    gather_y(1, 2, True)
    gather_y(1, 3, False)
    attend(0)
    gather_y(2, 3, True)
    gather_y(2, 2, True)
    gather_y(2, 3, False)
    mix(0)
    gather_y(2, 2, False)
    gather_end(1)
    project(1)
    mid_phase(0, 0)
    attend(1)
    mix(1)
    gather_end(2)
    project(2)
    norm_two(0)
    attend(2)
    take_wb()
    mix(2)
    mid_phase(0, 1)
    mid_phase(0, 2)
    spread_on("n2", n2, 0)
    feed(0)
    norm_two(1)
    mid_phase(1, 0)
    norm_two(2)
    mid_phase(2, 0)
    spread_on("n2", n2, 1)
    feed(1)
    back_two(0)
    mid_phase(1, 1)
    mid_phase(2, 1)
    spread_on("n2", n2, 2)
    output_rows(0)
    feed(2)
    share_out(1)
    spread_on("gm", gm, 0)
    share_out(0)
    share_out(4)
    share_out(5)
    spread_end("gm", gm, 0)
    attend_back(0)
    back_start(0, 1)
    back_start(0, 2)
    back_start(0, 3)
    mid_phase(2, 2)
    back_mid(0, 1)
    first_inward(1)
    back_mid(0, 3)
    back_mid(0, 2)
    mid_phase(1, 2)
    bin_table(0)
    output_rows(1)
    gather_grads(0)
    output_rows(2)
    back_start(0, 0)
    share_out(3)
    share_out(2)
    first_inward(0)
    back_mid(0, 0)
    back_two(1)
    back_pass(0, 3, False)
    then_inward(1)
    back_pass(0, 3, True)
    first_inward(4)
    then_inward(0)
    back_two(2)
    first_inward(5)
    back_pass(0, 2, True)
    then_outward(1)
    back_pass(0, 2, False)
    back_out(0, 0)
    spread_on("gm", gm, 1)
    then_inward(4)
    first_inward(3)
    spread_on("gm", gm, 2)
    then_outward(0)
    spread_end("gm", gm, 1)
    attend_back(1)
    spread_end("gm", gm, 2)
    bin_table(1)
    then_inward(5)
    first_inward(2)
    back_start(1, 0)
    then_outward(4)
    back_pass(0, 1, False)
    back_start(1, 3)
    last_outward(1)
    gather_grads(1)
    back_mid(1, 3)
    back_pass(0, 1, True)
    back_start(1, 1)
    back_start(1, 2)
    last_outward(0)
    share_out(6)
    back_mid(1, 0)
    back_mid(1, 1)
    back_mid(1, 2)
    then_inward(3)
    attend_back(2)
    then_outward(5)
    gather_grads(2)
    share_out(8)
    first_inward(6)
    back_out(1, 0)
    share_out(9)
    back_pass(1, 3, True)
    back_start(2, 0)
    back_pass(1, 3, False)
    then_inward(2)
    bin_table(2)
    back_one(0)
    then_outward(3)
    back_mid(2, 0)
    last_outward(4)
    share_out(7)
    first_inward(8)
    last_outward(5)
    then_inward(6)
    back_pass(1, 2, False)
    back_pass(1, 2, True)
    back_out(2, 0)
    then_outward(2)
    first_inward(9)
    back_start(2, 2)
    last_outward(3)
    back_mid(2, 2)
    then_outward(6)
    then_inward(8)
    first_inward(7)
    small_start()
    small_send(0)
    back_pass(1, 1, False)
    back_start(2, 3)
    back_pass(1, 1, True)
    back_start(2, 1)
    last_outward(2)
    back_mid(2, 3)
    back_mid(2, 1)
    small_take(0)
    small_send(1)
    then_inward(9)
    then_outward(8)
    last_outward(6)
    back_pass(2, 3, True)
    then_inward(7)
    back_pass(2, 3, False)
    then_outward(9)
    back_one(1)
    small_take(1)
    small_send(2)
    last_outward(8)
    back_pass(2, 2, True)
    then_outward(7)
    back_pass(2, 2, False)
    small_take(2)
    small_send(3)
    last_outward(9)
    back_pass(2, 1, True)
    back_pass(2, 1, False)
    last_outward(7)
    small_take(3)
    back_one(2)
    for q in range(len(chunks)):
        local[4 + micro + q].wait()
    for name, copy, when in pending:
        if when is None:
            copy.wait_send()
        else:
            pl.when(when)(copy.wait_send)
    assert len(sems.numbers) <= n_sems, len(sems.numbers)


def kernel_scratch(nf, nc, micro, T, share, hidden, n_sems):
    R = 4 * T
    L = nc * R
    vm = lambda shape, kind=BF16: pltpu.VMEM(shape, kind)
    rids = 3 * micro + nc * micro
    chunks, chunk_rows = grad_chunks(share, hidden)
    wide = max(384, share)
    return [
        vm((640, share)), vm((8, D + 128), F32),
        vm((640, D)), vm((256, D)), vm((D, hidden)), vm((hidden, D)),
        vm((nf, 8, D + 128), F32), vm((8, D + 128), F32),
        vm((micro * L, D)), vm((micro * R, D)),
        vm((3, micro, 1, R), jnp.int32), vm((micro, 6, BLK, BLK), jnp.int32),
        vm((micro, 6, HEADS_HERE, BLK, BLK)),
        vm((micro, HEADS_HERE * R, 256)), vm((micro * L, 384)),
        vm((micro * L, HEADS_HERE * R)), vm((L, HEADS_HERE * R), F32), vm((L, HEADS_HERE * R)),
        vm((micro, 256, R), F32), vm((micro, 8, HEADS_HERE * R), F32), vm((micro * R, 256)),
        vm((6, 2, T, D), F32), vm((nc, 2, T, D)),
        vm((3 + nc, 2, T, D)), vm((3 + nc, T, D)), vm((rids, 2, T, D)), vm((rids, T, D)),
        vm((nc - 1, T, D)), vm((micro, nc + 1, T, D)), vm((micro, T, D), F32),
        vm((micro * R, D)), vm((micro * R, hidden)), vm((micro * R, hidden)), vm((micro * R, D)),
        vm((micro, T, D), F32), vm((micro, T, D), F32), vm((micro * R, 256)),
        vm((256, HEADS_HERE * R)), vm((micro, 6, HEADS_HERE, BLK, BLK)), vm((640, D), F32),
        vm((HEADS_HERE, 32, 8, 128), F32), vm((2, 8, HEADS_HERE * R), F32), vm((8, D), F32),
        vm((nf - 1, chunk_rows, wide)), vm((nf - 1, chunk_rows, wide)),
        vm((chunk_rows, wide)), vm((chunk_rows, wide)),
        vm((4, 8, D + 128), F32), vm((1 + nf + nc - 1, 8, D + 128), F32),
        pltpu.SemaphoreType.DMA((n_sems,)), pltpu.SemaphoreType.DMA((n_sems,)),
        pltpu.SemaphoreType.DMA((8 + micro + len(chunks),)),
    ]


def finish_kernel(
    share, hidden, out_low, in_low, grads, sums,
    out, grad_in, gain_one, gain_two, grad_q, grad_k, grad_v, grad_o, grad_i, grad_b, grad_t, turned,
):
    out[:, 0] = out_low[...]
    grad_in[:, 0] = in_low[...]
    gain_one[...] = sums[0:1, 0:share].reshape(share)
    gain_two[...] = sums[1:2, 0:share].reshape(share)
    turned[...] = jnp.transpose(
        jnp.concatenate([sums[:, pl.ds(D, 128)], jnp.zeros((120, 128), F32)], axis=0)
    )
    here = grad_t.shape[1]
    part = turned[pl.ds(pl.multiple_of(lax.axis_index("fsdp") * here, here), here)]
    part = jnp.transpose(jnp.concatenate([part, jnp.zeros((128 - here, 128), F32)], axis=0))
    grad_t[...] = part[0:HEADS_HERE, 0:here]
    chunks, unused = grad_chunks(share, hidden)
    for name, row, rows, cols in chunks:
        value = grads[pl.ds(row, rows), 0:cols].astype(F32)
        if name.startswith("back"):
            grad_b[pl.ds(int(name[4:]) * PART, PART)] = value
        elif name.startswith("in"):
            grad_i[:, pl.ds(int(name[2:]) * PART, PART)] = value
        else:
            {"query": grad_q, "key": grad_k, "value": grad_v, "out": grad_o}[name][...] = value


def per_device(
    nf, nc,
    tokens, positions, w_query, w_key, w_value, w_out, w_in, w_back, gain_one, gain_two, bias_table, cotangent,
):
    micro, T = tokens.shape[0], tokens.shape[2]
    share, hidden = w_in.shape
    chunks, chunk_rows = grad_chunks(share, hidden)
    wide = max(384, share)
    n_sems = 320
    sems = Sems()
    vmem, anywhere = pl.BlockSpec(memory_space=pltpu.VMEM), pl.BlockSpec(memory_space=pl.ANY)
    low = pl.pallas_call(
        functools.partial(layer_kernel, nf, nc, micro, T, share, hidden, n_sems, sems),
        out_shape=[
            jax.ShapeDtypeStruct((micro, T, D), BF16),
            jax.ShapeDtypeStruct((micro, T, D), BF16),
            jax.ShapeDtypeStruct((chunk_rows, wide), BF16),
            jax.ShapeDtypeStruct((8, D + 128), F32),
        ],
        in_specs=[vmem] * 2 + [anywhere] * 6 + [vmem] * 3 + [anywhere],
        out_specs=[vmem, vmem, anywhere, vmem],
        scratch_shapes=kernel_scratch(nf, nc, micro, T, share, hidden, n_sems),
        compiler_params=pltpu.CompilerParams(
            collective_id=0, has_side_effects=True, vmem_limit_bytes=61800 * 1024
        ),
    )(
        tokens[:, 0], positions, w_query.T, w_key.T, w_value.T, w_out, w_in, w_back,
        gain_one, gain_two, bias_table.T, cotangent[:, 0],
    )
    shapes = [
        (tokens.shape, BF16), (tokens.shape, BF16), (gain_one.shape, F32), (gain_two.shape, F32),
        (w_query.T.shape, F32), (w_key.T.shape, F32), (w_value.T.shape, F32), (w_out.shape, F32),
        (w_in.shape, F32), (w_back.shape, F32), (bias_table.T.shape, F32),
    ]
    done = pl.pallas_call(
        functools.partial(finish_kernel, share, hidden),
        out_shape=[jax.ShapeDtypeStruct(shape, kind) for shape, kind in shapes],
        in_specs=[vmem] * 4,
        out_specs=[vmem] * len(shapes),
        scratch_shapes=[pltpu.VMEM((128, 128), F32)],
        compiler_params=pltpu.CompilerParams(vmem_limit_bytes=61800 * 1024),
    )(*low)
    return tuple(x.T if i in (4, 5, 6, 10) else x for i, x in enumerate(done))


def solution(mesh):
    nf, nc = mesh.shape["fsdp"], mesh.shape["ctx"]
    fits = D // nf % BLK == 0 and nc <= 4 and nc % 2 == 0 and mesh.shape["tp"] == 4
    return jax.shard_map(
        functools.partial(per_device, nf, nc) if fits else per_device_plain,
        mesh=mesh,
        in_specs=(
            P(None, "fsdp", ("ctx", "tp"), None),
            P(None, "fsdp", "ctx"),
            P("fsdp", "tp"),
            P("fsdp", "tp"),
            P("fsdp", "tp"),
            P("tp", "fsdp"),
            P("fsdp", "tp"),
            P("tp", "fsdp"),
            P("fsdp"),
            P("fsdp"),
            P("fsdp", "tp"),
            P(None, "fsdp", ("ctx", "tp"), None),
        ),
        out_specs=(
            P(None, "fsdp", ("ctx", "tp"), None),
            P(None, "fsdp", ("ctx", "tp"), None),
            P("fsdp"),
            P("fsdp"),
            P("fsdp", "tp"),
            P("fsdp", "tp"),
            P("fsdp", "tp"),
            P("tp", "fsdp"),
            P("fsdp", "tp"),
            P("tp", "fsdp"),
            P("fsdp", "tp"),
        ),
        check_vma=False,
    )
```

```python
import functools
import math

import jax
import jax.numpy as jnp
from jax import lax
from jax.experimental import pallas as pl
from jax.experimental.pallas import tpu as pltpu
from jax.sharding import PartitionSpec as P

D = 768
HDIM = 64


epsilon = 1e-06
bucket_edges = (12, 16, 23, 32, 46, 64, 91)


def bucket_of(query_pos, key_pos):
    relative = (key_pos[None, :] - query_pos[:, None]).astype(jnp.int32)
    magnitude = jnp.abs(relative)
    bucket = jnp.minimum(magnitude, 8)
    for edge_value in bucket_edges:
        bucket = bucket + (magnitude >= edge_value).astype(jnp.int32)
    return bucket + 16 * (relative > 0).astype(jnp.int32)


def table_bias(bucket, bias_rows):
    slot_ids = jnp.arange(bias_rows.shape[0], dtype=jnp.int32)
    matches = bucket[None, :, :, None] == slot_ids[None, None, None, :]
    return jnp.sum(jnp.where(matches, bias_rows.T[:, None, None, :], 0.0), axis=-1)


def table_grad(bucket, grad_scores, bucket_count):
    slot_ids = jnp.arange(bucket_count, dtype=jnp.int32)
    matches = bucket[None, None, :, :] == slot_ids[:, None, None, None]
    return jnp.sum(jnp.where(matches, grad_scores[None], 0.0), axis=(2, 3))


def inverse_rms(token_rows):
    return lax.rsqrt(jnp.mean(token_rows * token_rows, axis=-1, keepdims=True) + epsilon)


def norm_back(token_rows, scale_rows, gain_full, grad_normed):
    weighted = gain_full * grad_normed
    grad_rows = scale_rows * weighted - token_rows * scale_rows**3 * jnp.mean(
        token_rows * weighted, axis=-1, keepdims=True
    )
    return (grad_rows, jnp.sum(grad_normed * token_rows * scale_rows, axis=0))


def gelu_slope(values_in):
    return (
        0.5 * (1.0 + jax.scipy.special.erf(values_in * 0.7071067811865476))
        + values_in * jnp.exp(-0.5 * values_in * values_in) * 0.3989422804014327
    )


def left_product(left, right):
    return jnp.einsum("ra,rb->ab", left, right, preferred_element_type=jnp.float32)


def right_product(left, right):
    return jnp.einsum("ra,ba->rb", left, right, preferred_element_type=jnp.float32)


def spread_rows(local_rows):
    return lax.all_gather(local_rows, "tp", axis=0, tiled=True)


def collect_rows(partial_rows):
    return lax.psum_scatter(
        partial_rows.astype(jnp.bfloat16), "tp", scatter_dimension=0, tiled=True
    ).astype(jnp.float32)


def pair_terms(
    query_block,
    query_pos,
    key_block,
    key_pos,
    value_block,
    grad_att,
    log_total,
    row_delta,
    bias_rows,
):
    bucket = bucket_of(query_pos, key_pos)
    scores = jnp.einsum("qhd,khd->hqk", query_block, key_block, preferred_element_type=jnp.float32)
    scores = scores + table_bias(bucket, bias_rows)
    probability = jnp.exp(scores - log_total[:, :, None])
    grad_prob = jnp.einsum(
        "qhd,khd->hqk", grad_att, value_block, preferred_element_type=jnp.float32
    )
    grad_scores = probability * (grad_prob - row_delta[:, :, None])
    return (bucket, probability, grad_scores)


def make_fold(queries, query_pos, bias_rows, key_rows):
    head_count = queries.shape[1]

    def fold_keys(state_carry, shard_piece, first_row):
        keys_part, values_part, pos_part = shard_piece
        block_count = keys_part.shape[0] // key_rows
        key_blocks = keys_part.reshape(block_count, key_rows, head_count, HDIM)
        value_blocks = values_part.reshape(block_count, key_rows, head_count, HDIM)
        pos_blocks = pos_part.reshape(block_count, key_rows)

        def fold_one_block(inner, block_item):
            run_peak, run_total, run_acc = inner
            key_block, value_block, pos_block = block_item
            scores = jnp.einsum(
                "qhd,khd->hqk", queries, key_block, preferred_element_type=jnp.float32
            )
            scores = scores + table_bias(bucket_of(query_pos, pos_block), bias_rows)
            new_peak = jnp.maximum(run_peak, jnp.max(scores, axis=-1))
            factor = jnp.exp(run_peak - new_peak)
            weights_exp = jnp.exp(scores - new_peak[:, :, None])
            run_total = run_total * factor + jnp.sum(weights_exp, axis=-1)
            run_acc = run_acc * factor[:, :, None] + jnp.einsum(
                "hqk,khd->hqd",
                weights_exp.astype(jnp.bfloat16),
                value_block,
                preferred_element_type=jnp.float32,
            )
            return ((new_peak, run_total, run_acc), None)

        result, unused = lax.scan(
            fold_one_block, state_carry, (key_blocks, value_blocks, pos_blocks)
        )
        return result

    return fold_keys


def attend_back(
    queries,
    query_pos,
    bias_rows,
    keys_all,
    values_all,
    pos_all,
    grad_att,
    log_total,
    row_delta,
    key_rows,
):
    local_len, head_count = (queries.shape[0], queries.shape[1])
    bucket_count = bias_rows.shape[0]
    block_count = keys_all.shape[0] // key_rows
    key_blocks = keys_all.reshape(block_count, key_rows, head_count, HDIM)
    value_blocks = values_all.reshape(block_count, key_rows, head_count, HDIM)
    pos_blocks = pos_all.reshape(block_count, key_rows)

    def attend_one_block(inner, block_item):
        grad_query, grad_bias = inner
        key_block, value_block, pos_block = block_item
        bucket, probability, grad_scores = pair_terms(
            queries,
            query_pos,
            key_block,
            pos_block,
            value_block,
            grad_att,
            log_total,
            row_delta,
            bias_rows,
        )
        grad_bias = grad_bias + table_grad(bucket, grad_scores, bucket_count)
        scores_low = grad_scores.astype(jnp.bfloat16)
        grad_query = grad_query + jnp.einsum(
            "hqk,khd->qhd", scores_low, key_block, preferred_element_type=jnp.float32
        )
        grad_value = jnp.einsum(
            "hqk,qhd->khd",
            probability.astype(jnp.bfloat16),
            grad_att,
            preferred_element_type=jnp.float32,
        )
        grad_key = jnp.einsum(
            "hqk,qhd->khd", scores_low, queries, preferred_element_type=jnp.float32
        )
        return ((grad_query, grad_bias), (grad_key, grad_value))

    start_state = (
        jnp.zeros((local_len, head_count, HDIM), jnp.float32),
        jnp.zeros((bucket_count, head_count), jnp.float32),
    )
    final_state, stacked = lax.scan(
        attend_one_block, start_state, (key_blocks, value_blocks, pos_blocks)
    )
    total_keys = keys_all.shape[0]
    return (
        final_state[0],
        final_state[1],
        stacked[0].reshape(total_keys, head_count * HDIM),
        stacked[1].reshape(total_keys, head_count * HDIM),
    )


def own_share(grad_term, grad_dim):
    share_len = grad_term.shape[grad_dim] // lax.axis_size("fsdp")
    return lax.dynamic_slice_in_dim(
        grad_term, lax.axis_index("fsdp") * share_len, share_len, grad_dim
    )


def per_device_plain(
    tokens,
    positions,
    w_query,
    w_key,
    w_value,
    w_out,
    w_in,
    w_back,
    gain_one,
    gain_two,
    bias_table,
    cotangent,
):
    micro_count = tokens.shape[0]
    head_count = w_query.shape[1] // HDIM
    head_cols = head_count * HDIM
    hidden_cols = w_in.shape[1]
    bucket_count = bias_table.shape[0] * lax.axis_size("fsdp")
    grad_wq = jnp.zeros((D, head_cols), jnp.float32)
    grad_wk = jnp.zeros((D, head_cols), jnp.float32)
    grad_wv = jnp.zeros((D, head_cols), jnp.float32)
    grad_wo = jnp.zeros((head_cols, D), jnp.float32)
    grad_wi = jnp.zeros((D, hidden_cols), jnp.float32)
    grad_wb = jnp.zeros((hidden_cols, D), jnp.float32)
    grad_table = jnp.zeros((bucket_count, head_count), jnp.float32)
    grad_gain_one = jnp.zeros((D,), jnp.float32)
    grad_gain_two = jnp.zeros((D,), jnp.float32)
    outputs = []
    input_grads = []
    for micro_step in range(micro_count):
        full_wq, full_wk, full_wv, full_wo, full_wi, full_wb, full_g1, full_g2, full_table = (
            lax.all_gather(w_query, "fsdp", axis=0, tiled=True),
            lax.all_gather(w_key, "fsdp", axis=0, tiled=True),
            lax.all_gather(w_value, "fsdp", axis=0, tiled=True),
            lax.all_gather(w_out, "fsdp", axis=1, tiled=True),
            lax.all_gather(w_in, "fsdp", axis=0, tiled=True),
            lax.all_gather(w_back, "fsdp", axis=1, tiled=True),
            lax.all_gather(gain_one, "fsdp", axis=0, tiled=True),
            lax.all_gather(gain_two, "fsdp", axis=0, tiled=True),
            lax.all_gather(bias_table, "fsdp", axis=0, tiled=True),
        )
        gain_first = full_g1.astype(jnp.float32)
        gain_second = full_g2.astype(jnp.float32)
        bias_rows = full_table.astype(jnp.float32)
        token_rows = tokens[micro_step, 0].astype(jnp.float32)
        query_pos = positions[micro_step, 0]
        scale_one = inverse_rms(token_rows)
        normed = spread_rows((token_rows * scale_one * gain_first).astype(jnp.bfloat16))
        local_len = normed.shape[0]
        key_rows = math.gcd(local_len, 256)
        queries_low = jnp.dot(normed, full_wq, preferred_element_type=jnp.float32).astype(
            jnp.bfloat16
        )
        keys_low = jnp.dot(normed, full_wk, preferred_element_type=jnp.float32).astype(jnp.bfloat16)
        values_low = jnp.dot(normed, full_wv, preferred_element_type=jnp.float32).astype(
            jnp.bfloat16
        )
        queries = queries_low.reshape(local_len, head_count, HDIM)
        start_state = (
            jnp.full((head_count, local_len), -1e30, jnp.float32),
            jnp.zeros((head_count, local_len), jnp.float32),
            jnp.zeros((head_count, local_len, HDIM), jnp.float32),
        )
        fold_keys = make_fold(queries, query_pos, bias_rows, key_rows)
        run_peak, run_total, run_acc = fold_keys(
            start_state,
            (
                lax.all_gather(keys_low, "ctx", axis=0, tiled=True),
                lax.all_gather(values_low, "ctx", axis=0, tiled=True),
                lax.all_gather(query_pos, "ctx", axis=0, tiled=True),
            ),
            jnp.int32(0),
        )
        log_total = run_peak + jnp.log(run_total)
        attended_f = jnp.transpose(run_acc / run_total[:, :, None], (1, 0, 2)).reshape(
            local_len, head_cols
        )
        attended = attended_f.astype(jnp.bfloat16)
        middle = token_rows + collect_rows(
            jnp.dot(attended, full_wo, preferred_element_type=jnp.float32)
        )
        scale_two = inverse_rms(middle)
        normed_two = spread_rows((middle * scale_two * gain_second).astype(jnp.bfloat16))
        hidden_pre = jnp.dot(normed_two, full_wi, preferred_element_type=jnp.float32)
        hidden = jax.nn.gelu(hidden_pre, approximate=False).astype(jnp.bfloat16)
        output_rows = middle + collect_rows(
            jnp.dot(hidden, full_wb, preferred_element_type=jnp.float32)
        )
        outputs.append(output_rows.astype(jnp.bfloat16))
        grad_local = cotangent[micro_step, 0]
        grad_full = spread_rows(grad_local)
        grad_wb = grad_wb + left_product(hidden, grad_full)
        grad_hidden = right_product(grad_full, full_wb)
        grad_pre = (grad_hidden * gelu_slope(hidden_pre)).astype(jnp.bfloat16)
        grad_wi = grad_wi + left_product(normed_two, grad_pre)
        grad_normed_two = collect_rows(right_product(grad_pre, full_wi))
        grad_middle, gain_part_two = norm_back(middle, scale_two, gain_second, grad_normed_two)
        grad_middle = grad_middle + grad_local.astype(jnp.float32)
        grad_gain_two = grad_gain_two + gain_part_two
        grad_mixed = spread_rows(grad_middle.astype(jnp.bfloat16))
        grad_wo = grad_wo + left_product(attended, grad_mixed)
        grad_attended = right_product(grad_mixed, full_wo).astype(jnp.bfloat16)
        row_delta = jnp.sum(
            (grad_attended.astype(jnp.float32) * attended_f).reshape(local_len, head_count, HDIM),
            axis=-1,
        ).T
        back_keys, back_values, back_pos = (
            lax.all_gather(keys_low, "ctx", axis=0, tiled=True),
            lax.all_gather(values_low, "ctx", axis=0, tiled=True),
            lax.all_gather(query_pos, "ctx", axis=0, tiled=True),
        )
        grad_att_heads = grad_attended.reshape(local_len, head_count, HDIM)
        grad_queries, table_part, grad_keys_all, grad_values_all = attend_back(
            queries,
            query_pos,
            bias_rows,
            back_keys,
            back_values,
            back_pos,
            grad_att_heads,
            log_total,
            row_delta,
            key_rows,
        )
        grad_keys, grad_values = (
            lax.psum_scatter(
                grad_keys_all.astype(jnp.bfloat16), "ctx", scatter_dimension=0, tiled=True
            ).astype(jnp.float32),
            lax.psum_scatter(
                grad_values_all.astype(jnp.bfloat16), "ctx", scatter_dimension=0, tiled=True
            ).astype(jnp.float32),
        )
        grad_table = grad_table + table_part
        grad_q_low = grad_queries.reshape(local_len, head_cols).astype(jnp.bfloat16)
        grad_k_low = grad_keys.astype(jnp.bfloat16)
        grad_v_low = grad_values.astype(jnp.bfloat16)
        grad_wq = grad_wq + left_product(normed, grad_q_low)
        grad_wk = grad_wk + left_product(normed, grad_k_low)
        grad_wv = grad_wv + left_product(normed, grad_v_low)
        grad_normed = collect_rows(
            right_product(grad_q_low, full_wq)
            + right_product(grad_k_low, full_wk)
            + right_product(grad_v_low, full_wv)
        )
        grad_input, gain_part_one = norm_back(token_rows, scale_one, gain_first, grad_normed)
        grad_gain_one = grad_gain_one + gain_part_one
        input_grads.append((grad_input + grad_middle).astype(jnp.bfloat16))
    gain_total_one, gain_total_two = lax.psum((grad_gain_one, grad_gain_two), ("fsdp", "ctx", "tp"))
    sum_wq, sum_wk, sum_wv, sum_wo, sum_wi, sum_wb, sum_table = lax.psum(
        (grad_wq, grad_wk, grad_wv, grad_wo, grad_wi, grad_wb, grad_table), ("fsdp", "ctx")
    )
    share_wq = own_share(sum_wq, 0)
    share_wk = own_share(sum_wk, 0)
    share_wv = own_share(sum_wv, 0)
    share_wo = own_share(sum_wo, 1)
    share_wi = own_share(sum_wi, 0)
    share_wb = own_share(sum_wb, 1)
    share_table = own_share(sum_table, 0)
    return (
        jnp.stack(outputs)[:, None],
        jnp.stack(input_grads)[:, None],
        own_share(gain_total_one, 0),
        own_share(gain_total_two, 0),
        share_wq,
        share_wk,
        share_wv,
        share_wo,
        share_wi,
        share_wb,
        share_table,
    )


MESH = pl.DeviceIdType.MESH
F32 = jnp.float32
BF16 = jnp.bfloat16
HEADS_HERE = 3
BLK = 128
VALUE_ROWS = (128, 192, 64)


def nn(left, right):
    return lax.dot_general(left, right, (((1,), (0,)), ((), ())), preferred_element_type=F32)


def nt(left, right):
    return lax.dot_general(left, right, (((1,), (1,)), ((), ())), preferred_element_type=F32)


def tn(left, right):
    return lax.dot_general(left, right, (((0,), (0,)), ((), ())), preferred_element_type=F32)


def at_rows(offset, size, unit):
    return pl.ds(pl.multiple_of(offset, unit), size)


def fold_rows(block):
    return jnp.sum(block.reshape(block.shape[0] // 8, 8, block.shape[1]), axis=0)


class Sems:
    def __init__(self):
        self.numbers = {}

    def __call__(self, *name):
        return self.numbers.setdefault(name, len(self.numbers))


PART = 256
REACH = (0, 1, 2, 3, 4, 5, 6, 7, 11, 15, 22, 31, 45, 63, 90, 127)


def grad_chunks(share, hidden):
    head_cols = HEADS_HERE * HDIM
    names = [(f"back{i}", PART, share) for i in range(hidden // PART)]
    names += [(f"in{i}", share, PART) for i in range(hidden // PART)]
    names += [(name, head_cols, share) for name in ("out", "key", "value", "query")]
    chunks, row = [], 0
    for name, rows, cols in names:
        chunks.append((name, row, rows, cols))
        row += rows
    return chunks, row


def layer_kernel(
    nf, nc, micro, rows_own, share, hidden, n_sems, sems,
    tok, pos_in, wq_in, wk_in, wv_in, wo_loc, wi_loc, wb_loc, g1_in, g2_in, table_in, cot,
    out, grad_in, grads_out, small_out,
    w_loc, small_loc, wqkv, wo, wi, wb, small_rx, smallf, n1, g, posb, bkt, bias, qm, kv, e_t, s_t, ds_t, att_t,
    inv, att, keep, keep6, send1, send2, recv1, recv2, zsend, zrecv, gz, n2, hid, gp, gm,
    mid_f, gmid, dq, dom, nds, gacc, tacc, facc, gain2, xs, xr, zr1, zr2, sm, smr,
    ssem, rsem, lsem,
):
    f, c, t = lax.axis_index("fsdp"), lax.axis_index("ctx"), lax.axis_index("tp")
    nt_ = 4
    T = rows_own
    R = nt_ * T
    L = nc * R
    NB = L // BLK
    t1 = t + 1 - 2 * lax.rem(t, 2)
    t2 = lax.rem(t + 2, 4)
    t3 = lax.rem(t1 + 2, 4)
    sib, ypeer = (f, c, t1), (f, c, t2)
    xpeers = [(lax.rem(f + j, nf), c, t) for j in range(1, nf)]
    zpeers = [(f, lax.rem(c + k, nc), t) for k in range(1, nc)]
    below, above = (f, jnp.maximum(c - 1, 0), t), (f, jnp.minimum(c + 1, nc - 1), t)
    half_c = nc // 2
    low_side = c < half_c
    inward = jnp.where(low_side, c + 1, c - 1)
    outward = jnp.clip(jnp.where(low_side, c - 1, c + 1), 0, nc - 1)
    is_mid = (c == half_c - 1) | (c == half_c)
    has_out = (c > 0) & (c < nc - 1)
    if nc == 2:
        has_out = c < 0
    chunks, chunk_rows = grad_chunks(share, hidden)
    pending = []
    zs = xs.at[0]
    scr = s_t.at[pl.ds(0, 4 * rows_own)]

    def send(src, dst, name_s, name_r, dev, when=None):
        copy = pltpu.make_async_remote_copy(
            src, dst, ssem.at[sems(*name_s)], rsem.at[sems(*name_r)], device_id=dev, device_id_type=MESH
        )
        if when is None:
            copy.start()
        else:
            pl.when(when)(copy.start)
        pending.append((name_s, copy, when))

    def sent(*name_s):
        assert any(name == name_s for name, copy, when in pending), name_s
        for at, (name, copy, when) in enumerate(pending):
            if name == name_s:
                if when is None:
                    copy.wait_send()
                else:
                    pl.when(when)(copy.wait_send)
                del pending[at]
                return

    def arrived(dst, *name_r):
        pltpu.make_async_remote_copy(
            dst, dst, ssem.at[sems(*name_r)], rsem.at[sems(*name_r)], device_id=sib, device_id_type=MESH
        ).wait_recv()

    def rms(rows):
        return lax.rsqrt(jnp.mean(rows * rows, axis=-1, keepdims=True) + epsilon)

    def piece(m, block, t_of):
        return n1.at[at_rows(m * L + block * R + t_of * T, T, T)]

    def rows_of(m, t_of):
        return at_rows(m * R + t_of * T, T, T)

    posb[0] = jnp.zeros_like(posb[0])
    posb[2] = jnp.zeros_like(posb[2])
    barrier = pltpu.get_barrier_semaphore()
    peers = [sib, ypeer] + xpeers + zpeers
    for dev in peers:
        pl.semaphore_signal(barrier, inc=1, device_id=dev, device_id_type=MESH)
    for m in range(micro):
        rows = tok[m].astype(F32)
        n1[at_rows(m * L + c * R + t * T, T, T)] = (rows * rms(rows)).astype(BF16)
    posb[1] = pos_in[...]
    local = {}

    def local_copy(src, dst, i):
        copy = pltpu.make_async_copy(src, dst, lsem.at[i])
        copy.start()
        local[i] = copy

    share_cols = at_rows(f * share, share, BLK)
    share_rows = at_rows(f * share, share, BLK)
    own_rows = at_rows(t * T, T, T)
    qkv_parts = (
        (wq_in, 0, 0, 192), (wk_in, 0, 256, 192), (wv_in, 128, 448, 64), (wv_in, 0, 512, 128),
    )
    for i, (src, row, at, size) in enumerate(qkv_parts):
        local_copy(src.at[pl.ds(row, size)], w_loc.at[pl.ds(at, size)], 4 + micro + len(chunks) + i)
    local_copy(wo_loc.at[pl.ds(0, 128)], wo.at[pl.ds(128, 128), share_cols], 0)
    local_copy(wo_loc.at[pl.ds(128, 64)], wo.at[pl.ds(64, 64), share_cols], 1)
    local_copy(wi_loc, wi.at[share_rows], 2)
    local_copy(wb_loc, wb.at[:, share_cols], 3)
    for m in range(micro):
        local_copy(cot.at[m], g.at[rows_of(m, t)], 4 + m)
    small_loc[...] = jnp.zeros_like(small_loc)
    small_loc[0:1, share_cols] = g1_in[...].astype(F32).reshape(1, share)
    small_loc[1:2, share_cols] = g2_in[...].astype(F32).reshape(1, share)
    buckets_here = table_in.shape[1]
    spot = lax.broadcasted_iota(jnp.int32, (buckets_here, 128), 1) - f * buckets_here
    spot = spot == lax.broadcasted_iota(jnp.int32, (buckets_here, 128), 0)
    small_loc[0:HEADS_HERE, pl.ds(D, 128)] = nn(table_in[...], jnp.where(spot, 1.0, 0.0).astype(BF16))

    small_rx[f] = small_loc[...]
    pl.semaphore_wait(barrier, len(peers))

    def spread_first(m):
        mine = piece(m, c, t)
        send(mine, mine, ("ny", m, 0), ("ny", m, 0), ypeer)
        send(mine, mine, ("nd", m), ("nz", m, 1), below, c > 0)
        send(mine, mine, ("nu", m), ("nz", m, nc - 1), above, c < nc - 1)
        send(mine, mine, ("ns", m, 0), ("ns", m, 0), sib)

    def send_small():
        for j, dev in enumerate(xpeers):
            send(small_loc, small_rx.at[f], ("small", j), ("small", nf - 2 - j), dev)
        send(pos_in, posb.at[0], ("posu",), ("posu",), (f, jnp.minimum(c + 1, nc - 1), t), c < nc - 1)
        send(pos_in, posb.at[2], ("posd",), ("posd",), (f, jnp.maximum(c - 1, 0), t), c > 0)

    def send_qkv():
        for j, dev in enumerate(xpeers):
            for i, (src, row, at, size) in enumerate(qkv_parts):
                dst = wqkv.at[pl.ds(at, size), share_cols]
                send(src.at[pl.ds(row, size)], dst, ("wqkv", i, j), ("wqkv", i, nf - 2 - j), dev)

    def send_wo():
        for j, dev in enumerate(xpeers):
            send(wo_loc.at[pl.ds(0, 128)], wo.at[pl.ds(128, 128), share_cols], ("woa", j), ("woa", nf - 2 - j), dev)
            send(wo_loc.at[pl.ds(128, 64)], wo.at[pl.ds(64, 64), share_cols], ("wob", j), ("wob", nf - 2 - j), dev)

    def send_wi():
        for j, dev in enumerate(xpeers):
            send(wi_loc, wi.at[share_rows], ("wi", j), ("wi", nf - 2 - j), dev)

    def send_wb():
        for j, dev in enumerate(xpeers):
            send(wb_loc, wb.at[:, share_cols], ("wb", j), ("wb", nf - 2 - j), dev)

    def share_g(m):
        local[4 + m].wait()
        spread_own("g", g, m)

    def clear():
        w_loc[192:256] = jnp.zeros((64, share), BF16)
        wqkv[192:256] = jnp.zeros((64, D), BF16)
        wo[pl.ds(0, 64)] = jnp.zeros((64, D), BF16)
        dom[...] = jnp.zeros_like(dom)
        tacc[...] = jnp.zeros_like(tacc)
        facc[...] = jnp.zeros_like(facc)
        sm[0] = jnp.zeros((8, D + 128), F32)

    def spread_own(name, buf, m):
        mine = buf.at[rows_of(m, t)]
        send(mine, mine, (name, "y", m), (name, "y", m), ypeer)
        send(mine, mine, (name, "s", m), (name, "s", m), sib)

    def spread_on(name, buf, m):
        there = buf.at[rows_of(m, t2)]
        arrived(there, name, "y", m)
        send(there, there, (name, "f", m), (name, "f", m), sib)

    def spread_end(name, buf, m):
        arrived(buf.at[rows_of(m, t1)], name, "s", m)
        arrived(buf.at[rows_of(m, t3)], name, "f", m)

    def line_block(h, low):
        if low:
            return c >= h, jnp.maximum(c - h, 0), nc - h
        return c + h < nc, jnp.minimum(c + h, nc - 1), h

    def gather_z(m, h, low):
        there, z, k = line_block(h, low)
        block = piece(m, z, t)

        @pl.when(there)
        def _():
            arrived(block, "nz", m, k)

        if h < nc - 1 and low:
            send(block, block, ("nzu", m, k), ("nz", m, k - 1), above, there & (c < nc - 1))
        elif h < nc - 1:
            send(block, block, ("nzd", m, k), ("nz", m, k + 1), below, there & (c > 0))
        send(block, block, ("ny", m, k, low), ("ny", m, k), ypeer, there)
        send(block, block, ("ns", m, k, low), ("ns", m, k), sib, there)

    def gather_own(m):
        block = piece(m, c, t2)
        arrived(block, "ny", m, 0)
        send(block, block, ("nf", m, 0), ("nf", m, 0), sib)

    def gather_y(m, h, low):
        there, z, k = line_block(h, low)
        block = piece(m, z, t2)

        @pl.when(there)
        def _():
            arrived(block, "ny", m, k)

        send(block, block, ("nf", m, k, low), ("nf", m, k), sib, there)

    def gather_end(m):
        for k in range(nc):
            z = lax.rem(c + k, nc)
            arrived(piece(m, z, t1), "ns", m, k)
            arrived(piece(m, z, t3), "nf", m, k)

    def take_small():
        for j in range(nf - 1):
            arrived(small_rx.at[lax.rem(f + 1 + j, nf)], "small", j)
        total = small_rx[0]
        for j in range(1, nf):
            total = total + small_rx[j]
        smallf[...] = total

    def take_positions():
        @pl.when(c > 0)
        def _():
            arrived(posb.at[0], "posu")

        @pl.when(c < nc - 1)
        def _():
            arrived(posb.at[2], "posd")

    def bias_of(m):
        for qb in range(2):
            query_row = posb[1, m, :, pl.ds(qb * BLK, BLK)]
            for d in (-1, 0, 1):
                slot, row = ((0, 1), (1, 0), (1, 1), (2, 0))[qb + d + 1]
                key_row = posb[slot, m, :, pl.ds(row * BLK, BLK)]
                key_col = jnp.transpose(jnp.broadcast_to(key_row, (BLK, BLK)))
                relative = key_col - query_row
                size = jnp.abs(relative)
                bucket = jnp.minimum(size, 8)
                for edge_value in bucket_edges:
                    bucket = bucket + (size >= edge_value).astype(jnp.int32)
                bucket = bucket + 16 * (relative > 0).astype(jnp.int32)
                sub = qb * 3 + d + 1
                bkt[m, sub] = bucket
                for h in range(HEADS_HERE):
                    row_of = jnp.broadcast_to(smallf[h : h + 1, pl.ds(D, 128)], (BLK, BLK))
                    bias[m, sub, h] = jnp.take_along_axis(row_of, bucket, axis=1).astype(BF16)

    def fold_gain():
        for i in range(len(qkv_parts)):
            local[4 + micro + len(chunks) + i].wait()
        wqkv[:, share_cols] = w_loc[...]
        for j in range(nf - 1):
            cols = at_rows(lax.rem(f + 1 + j, nf) * share, share, BLK)
            for i, (src, row, at, size) in enumerate(qkv_parts):
                arrived(wqkv.at[pl.ds(at, size), cols], "wqkv", i, j)
        wqkv[...] = (wqkv[...].astype(F32) * smallf[0:1, 0:D]).astype(BF16)

    def reduce_start(slot, rid, kept, value, previous):
        scr[...] = value
        if previous is not None:
            sent("r1", previous)
        send1[slot, 0] = scr[at_rows(t1 * T, T, T)].astype(BF16)
        send1[slot, 1] = scr[at_rows(t3 * T, T, T)].astype(BF16)
        send(send1.at[slot], recv1.at[rid], ("r1", rid), ("r1", rid), sib)
        kept[0] = scr[own_rows].astype(kept.dtype)
        kept[1] = scr[at_rows(t2 * T, T, T)].astype(kept.dtype)

    def reduce_mid(slot, rid, kept, previous):
        arrived(recv1.at[rid], "r1", rid)
        if previous is not None:
            sent("r2", previous)
        send2[slot] = (kept[1].astype(F32) + recv1[rid, 1].astype(F32)).astype(BF16)
        send(send2.at[slot], recv2.at[rid], ("r2", rid), ("r2", rid), ypeer)
        kept[0] = (kept[0].astype(F32) + recv1[rid, 0].astype(F32)).astype(kept.dtype)

    def reduce_end(rid, kept):
        arrived(recv2.at[rid], "r2", rid)
        return kept[0].astype(F32) + recv2[rid].astype(F32)

    def phase(p, m):
        rid = p * micro + m
        return p, rid, keep.at[2 * p + m % 2], (rid - 1 if m > 0 else None)

    def start_phase(p, m, value):
        slot, rid, kept, previous = phase(p, m)
        reduce_start(slot, rid, kept, value, previous)

    def mid_phase(p, m):
        slot, rid, kept, previous = phase(p, m)
        reduce_mid(slot, rid, kept, previous)

    def end_phase(p, m):
        slot, rid, kept, previous = phase(p, m)
        return reduce_end(rid, kept)

    wide_cols = HEADS_HERE * R

    def far_row(kb, below, above):
        parts = []
        for h in range(HEADS_HERE):
            for qb in range(2):
                d = kb - 2 * c - qb
                parts.append(jnp.where(d < -1, below[h], jnp.where(d > 1, above[h], 0.0)))
        return jnp.concatenate(parts, axis=1)

    def near_blocks(use):
        for qb in range(2):
            for d in (-1, 0, 1):
                kb = 2 * c + qb + d
                if qb + d in (0, 1):
                    use(qb, d, kb)
                else:
                    pl.when((kb >= 0) & (kb < NB))(functools.partial(use, qb, d, kb))

    def project(m):
        own = at_rows(m * L + c * R, R, R)
        queries = nt(n1[own], wqkv[0:256])
        lane = lax.broadcasted_iota(jnp.int32, (R, 256), 1)
        for h in range(HEADS_HERE):
            keep_it = (lane >= h * HDIM) & (lane < (h + 1) * HDIM)
            qm[m, pl.ds(h * R, R)] = jnp.where(keep_it, queries, 0.0).astype(BF16)
        kv[pl.ds(m * L, L)] = nt(n1[pl.ds(m * L, L)], wqkv[256:640]).astype(BF16)

    def attend(m):
        first = m * L
        every = pl.ds(first, L)
        s_t[...] = nt(kv[every, 0:256], qm[m])
        tables = [smallf[h : h + 1, pl.ds(D, 128)] for h in range(HEADS_HERE)]
        below = [jnp.broadcast_to(tab[:, 15:16], (1, BLK)) for tab in tables]
        above = [jnp.broadcast_to(tab[:, 31:32], (1, BLK)) for tab in tables]

        def near(qb, d, kb):
            r = at_rows(kb * BLK, BLK, BLK)
            for h in range(HEADS_HERE):
                q = pl.ds(h * R + qb * BLK, BLK)
                s_t[r, q] = s_t[r, q] + bias[m, qb * 3 + d + 1, h].astype(F32)

        near_blocks(near)

        def peak(kb, top):
            block = s_t[at_rows(kb * BLK, BLK, BLK)]
            block = jnp.max(block.reshape(BLK // 8, 8, wide_cols), axis=0)
            return jnp.maximum(top, block + far_row(kb, below, above))

        top = lax.fori_loop(0, NB, peak, jnp.full((8, wide_cols), -jnp.inf, F32))
        top = jnp.max(top, axis=0, keepdims=True)

        def expo(kb, total):
            weights = jnp.exp(s_t[at_rows(kb * BLK, BLK, BLK)] - (top - far_row(kb, below, above)))
            e_t[at_rows(first + kb * BLK, BLK, BLK)] = weights.astype(BF16)
            return total + fold_rows(weights)

        total = lax.fori_loop(0, NB, expo, jnp.zeros((8, wide_cols), F32))
        over = 1.0 / jnp.sum(total, axis=0, keepdims=True)
        inv[m] = jnp.broadcast_to(over, (8, wide_cols))
        mixed = tn(kv[every, 128:384], e_t[every])
        for h in range(HEADS_HERE):
            v0 = VALUE_ROWS[h]
            cols = slice(h * R, (h + 1) * R)
            att_t[m, pl.ds(v0, HDIM)] = mixed[v0 : v0 + HDIM, cols] * over[:, cols]
        att_t[m, pl.ds(0, HDIM)] = jnp.zeros((HDIM, R), F32)
        attended = jnp.transpose(att_t[m]).astype(BF16)
        att[pl.ds(m * R, R)] = attended

    def mix(m):
        start_phase(0, m, nn(att[pl.ds(m * R, R)], wo[...]))

    def take_wo():
        local[0].wait()
        local[1].wait()
        for j in range(nf - 1):
            cols = at_rows(lax.rem(f + 1 + j, nf) * share, share, BLK)
            arrived(wo.at[pl.ds(128, 128), cols], "woa", j)
            arrived(wo.at[pl.ds(64, 64), cols], "wob", j)

    def take_wi():
        local[2].wait()
        for j in range(nf - 1):
            arrived(wi.at[at_rows(lax.rem(f + 1 + j, nf) * share, share, BLK)], "wi", j)

    def take_wb():
        local[3].wait()
        for j in range(nf - 1):
            arrived(wb.at[:, at_rows(lax.rem(f + 1 + j, nf) * share, share, BLK)], "wb", j)

    def norm_two(m):
        middle = tok[m].astype(F32) + end_phase(0, m)
        mid_f[m] = middle
        n2[rows_of(m, t)] = (middle * rms(middle) * smallf[1:2, 0:D]).astype(BF16)
        spread_own("n2", n2, m)

    def feed(m):
        spread_end("n2", n2, m)
        here = pl.ds(m * R, R)
        rows = n2[here]

        def one(i, unused):
            cols = at_rows(i * 256, 256, 256)
            pre = nn(rows, wi[:, cols])
            slope = nt(g[here], wb[cols])
            bell = 0.5 * (1.0 + lax.erf(pre * 0.7071067811865476))
            hid[here, cols] = (pre * bell).astype(BF16)
            bell = bell + pre * jnp.exp(-0.5 * pre * pre) * 0.3989422804014327
            gp[here, cols] = (slope * bell).astype(BF16)
            return unused

        lax.fori_loop(0, hidden // 256, one, 0)
        start_phase(1, m, nt(gp[here], wi[...]))
        start_phase(2, m, nn(hid[here], wb[...]))

    def output_rows(m):
        out[m] = (mid_f[m] + end_phase(2, m)).astype(BF16)

    def back_two(m):
        grad_normed = end_phase(1, m)
        middle = mid_f[m]
        scale = rms(middle)
        unit = middle * scale
        part = fold_rows(grad_normed * unit)
        gain2[...] = part if m == 0 else gain2[...] + part
        weighted = smallf[1:2, 0:D] * grad_normed
        grad = scale * (weighted - unit * jnp.mean(unit * weighted, axis=-1, keepdims=True))
        grad = grad + g[rows_of(m, t)].astype(F32)
        gmid[m] = grad
        gm[rows_of(m, t)] = grad.astype(BF16)
        spread_own("gm", gm, m)

    def attend_back(m):
        first = m * L
        every = pl.ds(first, L)
        grad_att = nt(wo[...], gm[pl.ds(m * R, R)]).astype(BF16).astype(F32)
        deltas = []
        for h in range(HEADS_HERE):
            v0 = VALUE_ROWS[h]
            scaled = (grad_att[v0 : v0 + HDIM] * inv[m, 0:1, pl.ds(h * R, R)]).astype(BF16)
            dom[pl.ds(v0, HDIM), pl.ds(h * R, R)] = scaled
            deltas.append(jnp.sum(scaled.astype(F32) * att_t[m, pl.ds(v0, HDIM)], axis=0, keepdims=True))
        delta = jnp.concatenate(deltas, axis=1)
        s_t[...] = nn(kv[every, 128:384], dom[...])
        half = lax.rem(lax.broadcasted_iota(jnp.int32, (8, wide_cols), 1) // BLK, 2)

        def one_block(kb, sums):
            r = at_rows(kb * BLK, BLK, BLK)
            grad = e_t[at_rows(first + kb * BLK, BLK, BLK)].astype(F32) * (s_t[r] - delta)
            ds_t[r] = grad.astype(BF16)
            part = fold_rows(grad)
            d = kb - 2 * c - half
            return sums[0] + jnp.where(d < -1, part, 0.0), sums[1] + jnp.where(d > 1, part, 0.0)

        zero = jnp.zeros((8, wide_cols), F32)
        low, high = lax.fori_loop(0, NB, one_block, (zero, zero))
        facc[0] += low
        facc[1] += high

        def save(qb, d, kb):
            r = at_rows(kb * BLK, BLK, BLK)
            for h in range(HEADS_HERE):
                nds[m, qb * 3 + d + 1, h] = ds_t[r, pl.ds(h * R + qb * BLK, BLK)]

        near_blocks(save)
        grad_q = tn(kv[every, 0:256], ds_t[...])
        columns = [grad_q[h * HDIM : (h + 1) * HDIM, h * R : (h + 1) * R] for h in range(HEADS_HERE)]
        columns.append(jnp.zeros((HDIM, R), F32))
        dq[pl.ds(m * R, R)] = jnp.transpose(jnp.concatenate(columns, axis=0)).astype(BF16)
        grad_k = nn(ds_t[...], qm[m])
        grad_v = nt(e_t[every], dom[...])
        kv[every, 0:128] = grad_k[:, 0:128].astype(BF16)
        kv[every, 128:256] = (grad_k[:, 128:256] + grad_v[:, 0:128]).astype(BF16)
        kv[every, 256:384] = grad_v[:, 128:256].astype(BF16)

    def merged(block, spots):
        where_at, parts = spots
        size = BLK // parts
        out_block = block[(parts - 1) * size :]
        for i in range(parts - 2, -1, -1):
            out_block = jnp.where(where_at == i, block[i * size : (i + 1) * size], out_block)
        return out_block

    def spots_of(parts):
        size = BLK // parts
        lane = lax.broadcasted_iota(jnp.int32, (size, BLK), 1)
        tile = lax.broadcasted_iota(jnp.int32, (size, BLK), 0) // 8
        away = lane - 8 * tile - 4 + size // 2
        spot = jnp.zeros((size, BLK), jnp.int32)
        for i in range(1, parts):
            spot = spot + (away >= i * size).astype(jnp.int32)
        return spot, parts

    def bin_table(m):
        def use(qb, d, kb):
            sub = qb * 3 + d + 1

            def bins(names, ids, blocks):
                for b in names:
                    same = ids == b
                    for h in range(HEADS_HERE):
                        tacc[h, b] += fold_rows(jnp.where(same, blocks[h], 0.0))

            if d == 0:
                ids = bkt[m, sub]
                blocks = [nds[m, sub, h].astype(F32) for h in range(HEADS_HERE)]
                for parts, sizes in ((4, range(0, 9)), (2, range(9, 11))):
                    spots = spots_of(parts)
                    both = [b for b in sizes] + [16 + b for b in sizes if b > 0]
                    bins(both, merged(ids, spots), [merged(block, spots) for block in blocks])
                bins([b + s for b in range(11, 16) for s in (0, 16)], ids, blocks)
            else:
                for size in range(1, 16):
                    rows = min(BLK, (REACH[size] + 7) // 8 * 8)
                    low = (rows + 15) // 16 * 16
                    r = pl.ds(BLK - rows if d < 0 else 0, rows)
                    part = slice(low - rows, low) if d < 0 else slice(0, rows)
                    low = pl.ds(BLK - low if d < 0 else 0, low)
                    blocks = [nds[m, sub, h, low].astype(F32)[part] for h in range(HEADS_HERE)]
                    bins([size if d < 0 else 16 + size], bkt[m, sub, r], blocks)

        near_blocks(use)

    def six(m, k):
        return 3 + k, 3 * micro + m * nc + k, keep6.at[k], (3 * micro + (m - 1) * nc + k if m > 0 else None)

    def back_start(m, k):
        r = at_rows(m * L + lax.rem(c + k, nc) * R, R, R)
        value = nn(kv[r], wqkv[256:640])
        if k == 0:
            value = value + nn(dq[pl.ds(m * R, R)], wqkv[0:256])
        slot, rid, kept, previous = six(m, k)
        reduce_start(slot, rid, kept, value, previous)

    def back_mid(m, k):
        slot, rid, kept, previous = six(m, k)
        reduce_mid(slot, rid, kept, previous)

    def back_out(m, k):
        slot, rid, kept, previous = six(m, k)
        gz[m] = reduce_end(rid, kept)

    def line_slot(m, h, up):
        if h == 0:
            return zrecv.at[m, nc - 1 + int(up)]
        return zrecv.at[m, (h if up else nc - h) - 1]

    def back_pass(m, h, up):
        there, z, k = line_block(h, not up)
        slot, rid, kept, previous = six(m, k)
        if m > 0:
            sent("gs", m - 1, h, up)
        more = c > 0 if up else c < nc - 1

        @pl.when(there & more)
        def _():
            arrived(line_slot(m, h, up), "gp", m, h, up)
            total = reduce_end(rid, kept) + line_slot(m, h, up)[...].astype(F32)
            zsend[k - 1] = total.astype(BF16)

        @pl.when(there & jnp.logical_not(more))
        def _():
            zsend[k - 1] = reduce_end(rid, kept).astype(BF16)

        dev = above if up else below
        send(zsend.at[k - 1], line_slot(m, h - 1, up), ("gs", m, h, up), ("gp", m, h - 1, up), dev, there)

    def back_one(m):
        for up, some in ((True, c > 0), (False, c < nc - 1)):

            @pl.when(some)
            def _(up=up):
                arrived(line_slot(m, 0, up), "gp", m, 0, up)
                gz[m] += line_slot(m, 0, up)[...].astype(F32)

        weighted = gz[m]
        rows = tok[m].astype(F32)
        scale = rms(rows)
        unit = rows * scale
        grad = scale * (weighted - unit * jnp.mean(unit * weighted, axis=-1, keepdims=True))
        grad_in[m] = (gmid[m] + grad).astype(BF16)

    def gather_grads(m):
        own = at_rows(m * L + c * R, R, R)
        every = pl.ds(m * L, L)
        for rows, value in (
            (pl.ds(0, 256), tn(dq[pl.ds(m * R, R)], n1[own])),
            (pl.ds(256, 384), tn(kv[every], n1[every])),
        ):
            gacc[rows] = value if m == 0 else gacc[rows] + value

    def each_part(chunk, part, use):
        name, row, rows, cols = chunk
        share_at = at_rows(part, share, BLK)
        if name.startswith("back"):
            use(row, rows, tn(hid[:, pl.ds(int(name[4:]) * PART, PART)], g[:, share_at]), None)
        elif name.startswith("in"):
            use(row, rows, tn(n2[:, share_at], gp[:, pl.ds(int(name[2:]) * PART, PART)]), None)
        elif name == "out":
            value = tn(att[...], gm[:, share_at])
            use(row, 128, value[128:], None)
            use(row + 128, 64, value[64:128], None)
        elif name == "value":
            use(row, 128, gacc[pl.ds(512, 128), share_at], 512)
            use(row + 128, 64, gacc[pl.ds(448, 64), share_at], 448)
        else:
            first = 0 if name == "query" else 256
            use(row, rows, gacc[pl.ds(first, rows), share_at], first)

    def share_out(q):
        chunk = chunks[q]
        name, row, rows, cols = chunk
        for j, dev in enumerate(xpeers):
            part = lax.rem(f + 1 + j, nf) * share

            def use(at, size, value, first, j=j):
                xs[j, pl.ds(at, size), 0:cols] = value.astype(BF16)

            each_part(chunk, part, use)
            src = xs.at[j, pl.ds(row, rows), pl.ds(0, cols)]
            dst = xr.at[nf - 2 - j, pl.ds(row, rows), pl.ds(0, cols)]
            send(src, dst, ("x", q, j), ("x", q, nf - 2 - j), dev)

    def own_share(q):
        chunk = chunks[q]
        name, row, rows, cols = chunk
        for j in range(nf - 1):
            arrived(xr.at[j, pl.ds(row, rows), pl.ds(0, cols)], "x", q, j)
        sent("x", q, 0)

        def use(at, size, value, first):
            for j in range(nf - 1):
                value = value + xr[j, pl.ds(at, size), 0:cols].astype(F32)
            if first is not None:
                weight = w_loc[pl.ds(first, size)].astype(F32)
                sm[0, 0:1, share_cols] += jnp.sum(weight * value, axis=0, keepdims=True)
                value = value * smallf[0:1, share_cols]
            zs[pl.ds(at, size), 0:cols] = value.astype(BF16)

        each_part(chunk, f * share, use)

    def first_inward(q):
        own_share(q)
        name, row, rows, cols = chunks[q]
        at = (pl.ds(row, rows), pl.ds(0, cols))
        dev = (f, inward, t)
        if nc == 2:
            send(zs.at[at], zr2.at[at], ("ze", q), ("zx", q), dev)
        else:
            send(zs.at[at], zr1.at[at], ("ze", q), ("zi", q), dev, jnp.logical_not(has_out))

    def then_inward(q):
        if nc == 2:
            return
        name, row, rows, cols = chunks[q]
        at = (pl.ds(row, rows), pl.ds(0, cols))

        @pl.when(has_out)
        def _():
            arrived(zr1.at[at], "zi", q)
            zs[at] = (zs[at].astype(F32) + zr1[at].astype(F32)).astype(BF16)

        send(zs.at[at], zr2.at[at], ("zm", q), ("zx", q), (f, inward, t), is_mid)

    def then_outward(q):
        name, row, rows, cols = chunks[q]
        at = (pl.ds(row, rows), pl.ds(0, cols))

        @pl.when(is_mid)
        def _():
            arrived(zr2.at[at], "zx", q)
            zr2[at] = (zs[at].astype(F32) + zr2[at].astype(F32)).astype(BF16)

        if nc > 2:
            send(zr2.at[at], zr2.at[at], ("zo", q), ("zo", q), (f, outward, t), has_out)

    def last_outward(q):
        name, row, rows, cols = chunks[q]
        at = (pl.ds(row, rows), pl.ds(0, cols))

        @pl.when(jnp.logical_not(is_mid))
        def _():
            arrived(zr2.at[at], "zo", q)

        local_copy(zr2.at[at], grads_out.at[at], 4 + micro + q)

    def small_start():
        g2 = jnp.sum(gain2[...], axis=0, keepdims=True)
        sm[0, 1:2, 0:D] = g2
        for h in range(HEADS_HERE):
            below = jnp.sum(jnp.sum(facc[0, :, pl.ds(h * R, R)], axis=0, keepdims=True), axis=1, keepdims=True)
            above = jnp.sum(jnp.sum(facc[1, :, pl.ds(h * R, R)], axis=0, keepdims=True), axis=1, keepdims=True)
            per = jnp.sum(tacc[h], axis=1)
            per = jnp.sum(jnp.concatenate([per, jnp.zeros((96, 128), F32)], axis=0), axis=1, keepdims=True)
            line = jnp.transpose(jnp.broadcast_to(per, (128, 128)))[0:1, :]
            lane = lax.broadcasted_iota(jnp.int32, (1, 128), 1)
            line = line + jnp.where(lane == 15, below, 0.0) + jnp.where(lane == 31, above, 0.0)
            sm[0, h : h + 1, pl.ds(D, 128)] = line

    def small_send(step):
        if step == 0:
            send(sm.at[0], smr.at[0], ("m", 0), ("m", 0), sib)
        elif step == 1:
            send(sm.at[1], smr.at[1], ("m", 1), ("m", 1), ypeer)
        elif step == 2:
            for j, dev in enumerate(xpeers):
                send(sm.at[2], smr.at[2 + nf - 2 - j], ("mx", j), ("mx", nf - 2 - j), dev)
        else:
            for k in range(1, nc):
                send(sm.at[3], smr.at[1 + nf + nc - k - 1], ("mz", k), ("mz", nc - k), zpeers[k - 1])

    def small_take(step):
        if step < 2:
            arrived(smr.at[step], "m", step)
            lanes = lax.broadcasted_iota(jnp.int32, (8, D + 128), 1)
            sm[step + 1] = sm[step] + jnp.where(lanes < D, smr[step], 0.0)
        elif step == 2:
            total = sm[2]
            for j in range(nf - 1):
                arrived(smr.at[2 + j], "mx", j)
                total = total + smr[2 + j]
            sm[3] = total
        else:
            total = sm[3]
            for k in range(1, nc):
                arrived(smr.at[1 + nf + k - 1], "mz", k)
                total = total + smr[1 + nf + k - 1]
            small_out[...] = total
            smr[0] = total
            for i in range(2):
                small_out[i : i + 1, 0:share] = smr[0, i : i + 1, share_cols]

    spread_first(0)
    send_small()
    share_g(0)
    send_qkv()
    spread_first(1)
    send_wo()
    send_wi()
    gather_z(0, 1, False)
    gather_z(0, 1, True)
    gather_z(0, 2, True)
    gather_z(1, 1, False)
    gather_z(0, 2, False)
    gather_z(0, 3, False)
    spread_first(2)
    send_wb()
    gather_z(1, 1, True)
    gather_z(1, 2, False)
    gather_own(0)
    clear()
    take_positions()
    gather_y(0, 1, True)
    gather_z(2, 1, False)
    take_small()
    gather_y(0, 3, False)
    gather_z(2, 2, False)
    spread_on("g", g, 0)
    gather_y(0, 1, False)
    gather_z(2, 1, True)
    take_wo()
    gather_z(0, 3, True)
    gather_y(0, 2, True)
    gather_z(1, 3, False)
    gather_y(0, 2, False)
    gather_z(1, 2, True)
    gather_z(1, 3, True)
    gather_z(2, 3, False)
    bias_of(0)
    gather_y(0, 3, True)
    gather_z(2, 2, True)
    gather_own(1)
    fold_gain()
    gather_own(2)
    gather_end(0)
    share_g(2)
    project(0)
    attend(0)
    gather_z(2, 3, True)
    mix(0)
    gather_y(1, 1, True)
    mid_phase(0, 0)
    gather_y(1, 1, False)
    bias_of(1)
    gather_y(1, 3, False)
    gather_y(1, 2, False)
    gather_y(1, 3, True)
    bias_of(2)
    gather_y(2, 2, False)
    gather_y(1, 2, True)
    spread_end("g", g, 0)
    gather_end(1)
    project(1)
    share_g(1)
    gather_y(2, 1, True)
    attend(1)
    gather_y(2, 3, True)
    mix(1)
    gather_y(2, 2, True)
    gather_y(2, 1, False)
    gather_y(2, 3, False)
    gather_end(2)
    norm_two(0)
    take_wi()
    project(2)
    mid_phase(0, 1)
    attend(2)
    mix(2)
    spread_on("g", g, 2)
    spread_on("n2", n2, 0)
    mid_phase(0, 2)
    norm_two(1)
    take_wb()
    feed(0)
    norm_two(2)
    spread_on("g", g, 1)
    spread_end("g", g, 1)
    mid_phase(1, 0)
    mid_phase(2, 0)
    spread_on("n2", n2, 1)
    feed(1)
    back_two(0)
    spread_end("g", g, 2)
    spread_on("n2", n2, 2)
    mid_phase(1, 1)
    output_rows(0)
    feed(2)
    share_out(1)
    share_out(4)
    spread_on("gm", gm, 0)
    spread_end("gm", gm, 0)
    mid_phase(1, 2)
    back_two(1)
    attend_back(0)
    back_start(0, 3)
    share_out(0)
    first_inward(1)
    back_two(2)
    back_start(0, 2)
    share_out(2)
    back_start(0, 1)
    spread_on("gm", gm, 1)
    gather_grads(0)
    back_mid(0, 1)
    then_inward(1)
    back_mid(0, 2)
    spread_end("gm", gm, 1)
    first_inward(4)
    spread_on("gm", gm, 2)
    mid_phase(2, 1)
    back_mid(0, 3)
    back_start(0, 0)
    share_out(5)
    then_inward(4)
    first_inward(0)
    attend_back(1)
    then_outward(1)
    first_inward(2)
    then_inward(0)
    share_out(3)
    back_pass(0, 3, False)
    spread_end("gm", gm, 2)
    attend_back(2)
    back_mid(0, 0)
    then_outward(4)
    back_pass(0, 3, True)
    then_inward(2)
    first_inward(5)
    back_pass(0, 2, False)
    then_outward(0)
    gather_grads(1)
    share_out(6)
    back_pass(0, 2, True)
    then_inward(5)
    then_outward(2)
    first_inward(3)
    back_pass(0, 1, False)
    back_start(1, 2)
    gather_grads(2)
    share_out(8)
    share_out(9)
    back_start(1, 3)
    last_outward(1)
    back_pass(0, 1, True)
    back_out(0, 0)
    then_inward(3)
    then_outward(5)
    back_start(1, 1)
    back_mid(1, 2)
    back_mid(1, 3)
    first_inward(6)
    then_inward(6)
    back_start(1, 0)
    back_mid(1, 1)
    then_outward(3)
    first_inward(9)
    first_inward(8)
    then_inward(9)
    share_out(7)
    bin_table(0)
    back_one(0)
    mid_phase(2, 2)
    then_outward(6)
    back_pass(1, 3, True)
    bin_table(1)
    then_inward(8)
    back_pass(1, 3, False)
    back_mid(1, 0)
    first_inward(7)
    then_outward(9)
    back_pass(1, 2, True)
    back_pass(1, 2, False)
    back_start(2, 2)
    output_rows(2)
    bin_table(2)
    small_start()
    small_send(0)
    then_inward(7)
    last_outward(4)
    back_mid(2, 2)
    then_outward(8)
    small_take(0)
    small_send(1)
    back_pass(1, 1, False)
    back_start(2, 3)
    back_pass(1, 1, True)
    back_mid(2, 3)
    back_pass(2, 3, True)
    back_start(2, 1)
    back_mid(2, 1)
    back_pass(2, 3, False)
    last_outward(3)
    last_outward(8)
    small_take(1)
    last_outward(0)
    small_send(2)
    then_outward(7)
    back_out(1, 0)
    last_outward(9)
    back_pass(2, 2, True)
    back_pass(2, 2, False)
    last_outward(5)
    small_take(2)
    small_send(3)
    back_start(2, 0)
    back_mid(2, 0)
    back_pass(2, 1, True)
    back_pass(2, 1, False)
    output_rows(1)
    last_outward(7)
    back_one(1)
    last_outward(6)
    small_take(3)
    last_outward(2)
    back_out(2, 0)
    back_one(2)
    for q in range(len(chunks)):
        local[4 + micro + q].wait()
    for name, copy, when in pending:
        if when is None:
            copy.wait_send()
        else:
            pl.when(when)(copy.wait_send)
    assert len(sems.numbers) <= n_sems, len(sems.numbers)


def kernel_scratch(nf, nc, micro, T, share, hidden, n_sems):
    R = 4 * T
    L = nc * R
    vm = lambda shape, kind=BF16: pltpu.VMEM(shape, kind)
    rids = 3 * micro + nc * micro
    chunks, chunk_rows = grad_chunks(share, hidden)
    wide = max(384, share)
    return [
        vm((640, share)), vm((8, D + 128), F32),
        vm((640, D)), vm((256, D)), vm((D, hidden)), vm((hidden, D)),
        vm((nf, 8, D + 128), F32), vm((8, D + 128), F32),
        vm((micro * L, D)), vm((micro * R, D)),
        vm((3, micro, 1, R), jnp.int32), vm((micro, 6, BLK, BLK), jnp.int32),
        vm((micro, 6, HEADS_HERE, BLK, BLK)),
        vm((micro, HEADS_HERE * R, 256)), vm((micro * L, 384)),
        vm((micro * L, HEADS_HERE * R)), vm((L, HEADS_HERE * R), F32), vm((L, HEADS_HERE * R)),
        vm((micro, 256, R), F32), vm((micro, 8, HEADS_HERE * R), F32), vm((micro * R, 256)),
        vm((6, 2, T, D), F32), vm((nc, 2, T, D)),
        vm((3 + nc, 2, T, D)), vm((3 + nc, T, D)), vm((rids, 2, T, D)), vm((rids, T, D)),
        vm((nc - 1, T, D)), vm((micro, nc + 1, T, D)), vm((micro, T, D), F32),
        vm((micro * R, D)), vm((micro * R, hidden)), vm((micro * R, hidden)), vm((micro * R, D)),
        vm((micro, T, D), F32), vm((micro, T, D), F32), vm((micro * R, 256)),
        vm((256, HEADS_HERE * R)), vm((micro, 6, HEADS_HERE, BLK, BLK)), vm((640, D), F32),
        vm((HEADS_HERE, 32, 8, 128), F32), vm((2, 8, HEADS_HERE * R), F32), vm((8, D), F32),
        vm((nf - 1, chunk_rows, wide)), vm((nf - 1, chunk_rows, wide)),
        vm((chunk_rows, wide)), vm((chunk_rows, wide)),
        vm((4, 8, D + 128), F32), vm((1 + nf + nc - 1, 8, D + 128), F32),
        pltpu.SemaphoreType.DMA((n_sems,)), pltpu.SemaphoreType.DMA((n_sems,)),
        pltpu.SemaphoreType.DMA((8 + micro + len(chunks),)),
    ]


def finish_kernel(
    share, hidden, out_low, in_low, grads, sums,
    out, grad_in, gain_one, gain_two, grad_q, grad_k, grad_v, grad_o, grad_i, grad_b, grad_t, turned,
):
    out[:, 0] = out_low[...]
    grad_in[:, 0] = in_low[...]
    gain_one[...] = sums[0:1, 0:share].reshape(share)
    gain_two[...] = sums[1:2, 0:share].reshape(share)
    turned[...] = jnp.transpose(
        jnp.concatenate([sums[:, pl.ds(D, 128)], jnp.zeros((120, 128), F32)], axis=0)
    )
    here = grad_t.shape[1]
    part = turned[pl.ds(pl.multiple_of(lax.axis_index("fsdp") * here, here), here)]
    part = jnp.transpose(jnp.concatenate([part, jnp.zeros((128 - here, 128), F32)], axis=0))
    grad_t[...] = part[0:HEADS_HERE, 0:here]
    chunks, unused = grad_chunks(share, hidden)
    for name, row, rows, cols in chunks:
        value = grads[pl.ds(row, rows), 0:cols].astype(F32)
        if name.startswith("back"):
            grad_b[pl.ds(int(name[4:]) * PART, PART)] = value
        elif name.startswith("in"):
            grad_i[:, pl.ds(int(name[2:]) * PART, PART)] = value
        else:
            {"query": grad_q, "key": grad_k, "value": grad_v, "out": grad_o}[name][...] = value


def per_device(
    nf, nc,
    tokens, positions, w_query, w_key, w_value, w_out, w_in, w_back, gain_one, gain_two, bias_table, cotangent,
):
    micro, T = tokens.shape[0], tokens.shape[2]
    share, hidden = w_in.shape
    chunks, chunk_rows = grad_chunks(share, hidden)
    wide = max(384, share)
    n_sems = 320
    sems = Sems()
    vmem, anywhere = pl.BlockSpec(memory_space=pltpu.VMEM), pl.BlockSpec(memory_space=pl.ANY)
    low = pl.pallas_call(
        functools.partial(layer_kernel, nf, nc, micro, T, share, hidden, n_sems, sems),
        out_shape=[
            jax.ShapeDtypeStruct((micro, T, D), BF16),
            jax.ShapeDtypeStruct((micro, T, D), BF16),
            jax.ShapeDtypeStruct((chunk_rows, wide), BF16),
            jax.ShapeDtypeStruct((8, D + 128), F32),
        ],
        in_specs=[vmem] * 2 + [anywhere] * 6 + [vmem] * 3 + [anywhere],
        out_specs=[vmem, vmem, anywhere, vmem],
        scratch_shapes=kernel_scratch(nf, nc, micro, T, share, hidden, n_sems),
        compiler_params=pltpu.CompilerParams(
            collective_id=0, has_side_effects=True, vmem_limit_bytes=61800 * 1024
        ),
    )(
        tokens[:, 0], positions, w_query.T, w_key.T, w_value.T, w_out, w_in, w_back,
        gain_one, gain_two, bias_table.T, cotangent[:, 0],
    )
    shapes = [
        (tokens.shape, BF16), (tokens.shape, BF16), (gain_one.shape, F32), (gain_two.shape, F32),
        (w_query.T.shape, F32), (w_key.T.shape, F32), (w_value.T.shape, F32), (w_out.shape, F32),
        (w_in.shape, F32), (w_back.shape, F32), (bias_table.T.shape, F32),
    ]
    done = pl.pallas_call(
        functools.partial(finish_kernel, share, hidden),
        out_shape=[jax.ShapeDtypeStruct(shape, kind) for shape, kind in shapes],
        in_specs=[vmem] * 4,
        out_specs=[vmem] * len(shapes),
        scratch_shapes=[pltpu.VMEM((128, 128), F32)],
        compiler_params=pltpu.CompilerParams(vmem_limit_bytes=61800 * 1024),
    )(*low)
    return tuple(x.T if i in (4, 5, 6, 10) else x for i, x in enumerate(done))


def solution(mesh):
    nf, nc = mesh.shape["fsdp"], mesh.shape["ctx"]
    fits = D // nf % BLK == 0 and nc <= 4 and nc % 2 == 0 and mesh.shape["tp"] == 4
    return jax.shard_map(
        functools.partial(per_device, nf, nc) if fits else per_device_plain,
        mesh=mesh,
        in_specs=(
            P(None, "fsdp", ("ctx", "tp"), None),
            P(None, "fsdp", "ctx"),
            P("fsdp", "tp"),
            P("fsdp", "tp"),
            P("fsdp", "tp"),
            P("tp", "fsdp"),
            P("fsdp", "tp"),
            P("tp", "fsdp"),
            P("fsdp"),
            P("fsdp"),
            P("fsdp", "tp"),
            P(None, "fsdp", ("ctx", "tp"), None),
        ),
        out_specs=(
            P(None, "fsdp", ("ctx", "tp"), None),
            P(None, "fsdp", ("ctx", "tp"), None),
            P("fsdp"),
            P("fsdp"),
            P("fsdp", "tp"),
            P("fsdp", "tp"),
            P("fsdp", "tp"),
            P("tp", "fsdp"),
            P("fsdp", "tp"),
            P("tp", "fsdp"),
            P("fsdp", "tp"),
        ),
        check_vma=False,
    )
```

```python
import functools
import math

import jax
import jax.numpy as jnp
from jax import lax
from jax.experimental import pallas as pl
from jax.experimental.pallas import tpu as pltpu
from jax.sharding import PartitionSpec as P

D = 768
HDIM = 64


epsilon = 1e-06
bucket_edges = (12, 16, 23, 32, 46, 64, 91)


def bucket_of(query_pos, key_pos):
    relative = (key_pos[None, :] - query_pos[:, None]).astype(jnp.int32)
    magnitude = jnp.abs(relative)
    bucket = jnp.minimum(magnitude, 8)
    for edge_value in bucket_edges:
        bucket = bucket + (magnitude >= edge_value).astype(jnp.int32)
    return bucket + 16 * (relative > 0).astype(jnp.int32)


def table_bias(bucket, bias_rows):
    slot_ids = jnp.arange(bias_rows.shape[0], dtype=jnp.int32)
    matches = bucket[None, :, :, None] == slot_ids[None, None, None, :]
    return jnp.sum(jnp.where(matches, bias_rows.T[:, None, None, :], 0.0), axis=-1)


def table_grad(bucket, grad_scores, bucket_count):
    slot_ids = jnp.arange(bucket_count, dtype=jnp.int32)
    matches = bucket[None, None, :, :] == slot_ids[:, None, None, None]
    return jnp.sum(jnp.where(matches, grad_scores[None], 0.0), axis=(2, 3))


def inverse_rms(token_rows):
    return lax.rsqrt(jnp.mean(token_rows * token_rows, axis=-1, keepdims=True) + epsilon)


def norm_back(token_rows, scale_rows, gain_full, grad_normed):
    weighted = gain_full * grad_normed
    grad_rows = scale_rows * weighted - token_rows * scale_rows**3 * jnp.mean(
        token_rows * weighted, axis=-1, keepdims=True
    )
    return (grad_rows, jnp.sum(grad_normed * token_rows * scale_rows, axis=0))


def gelu_slope(values_in):
    return (
        0.5 * (1.0 + jax.scipy.special.erf(values_in * 0.7071067811865476))
        + values_in * jnp.exp(-0.5 * values_in * values_in) * 0.3989422804014327
    )


def left_product(left, right):
    return jnp.einsum("ra,rb->ab", left, right, preferred_element_type=jnp.float32)


def right_product(left, right):
    return jnp.einsum("ra,ba->rb", left, right, preferred_element_type=jnp.float32)


def spread_rows(local_rows):
    return lax.all_gather(local_rows, "tp", axis=0, tiled=True)


def collect_rows(partial_rows):
    return lax.psum_scatter(
        partial_rows.astype(jnp.bfloat16), "tp", scatter_dimension=0, tiled=True
    ).astype(jnp.float32)


def pair_terms(
    query_block,
    query_pos,
    key_block,
    key_pos,
    value_block,
    grad_att,
    log_total,
    row_delta,
    bias_rows,
):
    bucket = bucket_of(query_pos, key_pos)
    scores = jnp.einsum("qhd,khd->hqk", query_block, key_block, preferred_element_type=jnp.float32)
    scores = scores + table_bias(bucket, bias_rows)
    probability = jnp.exp(scores - log_total[:, :, None])
    grad_prob = jnp.einsum(
        "qhd,khd->hqk", grad_att, value_block, preferred_element_type=jnp.float32
    )
    grad_scores = probability * (grad_prob - row_delta[:, :, None])
    return (bucket, probability, grad_scores)


def make_fold(queries, query_pos, bias_rows, key_rows):
    head_count = queries.shape[1]

    def fold_keys(state_carry, shard_piece, first_row):
        keys_part, values_part, pos_part = shard_piece
        block_count = keys_part.shape[0] // key_rows
        key_blocks = keys_part.reshape(block_count, key_rows, head_count, HDIM)
        value_blocks = values_part.reshape(block_count, key_rows, head_count, HDIM)
        pos_blocks = pos_part.reshape(block_count, key_rows)

        def fold_one_block(inner, block_item):
            run_peak, run_total, run_acc = inner
            key_block, value_block, pos_block = block_item
            scores = jnp.einsum(
                "qhd,khd->hqk", queries, key_block, preferred_element_type=jnp.float32
            )
            scores = scores + table_bias(bucket_of(query_pos, pos_block), bias_rows)
            new_peak = jnp.maximum(run_peak, jnp.max(scores, axis=-1))
            factor = jnp.exp(run_peak - new_peak)
            weights_exp = jnp.exp(scores - new_peak[:, :, None])
            run_total = run_total * factor + jnp.sum(weights_exp, axis=-1)
            run_acc = run_acc * factor[:, :, None] + jnp.einsum(
                "hqk,khd->hqd",
                weights_exp.astype(jnp.bfloat16),
                value_block,
                preferred_element_type=jnp.float32,
            )
            return ((new_peak, run_total, run_acc), None)

        result, unused = lax.scan(
            fold_one_block, state_carry, (key_blocks, value_blocks, pos_blocks)
        )
        return result

    return fold_keys


def attend_back(
    queries,
    query_pos,
    bias_rows,
    keys_all,
    values_all,
    pos_all,
    grad_att,
    log_total,
    row_delta,
    key_rows,
):
    local_len, head_count = (queries.shape[0], queries.shape[1])
    bucket_count = bias_rows.shape[0]
    block_count = keys_all.shape[0] // key_rows
    key_blocks = keys_all.reshape(block_count, key_rows, head_count, HDIM)
    value_blocks = values_all.reshape(block_count, key_rows, head_count, HDIM)
    pos_blocks = pos_all.reshape(block_count, key_rows)

    def attend_one_block(inner, block_item):
        grad_query, grad_bias = inner
        key_block, value_block, pos_block = block_item
        bucket, probability, grad_scores = pair_terms(
            queries,
            query_pos,
            key_block,
            pos_block,
            value_block,
            grad_att,
            log_total,
            row_delta,
            bias_rows,
        )
        grad_bias = grad_bias + table_grad(bucket, grad_scores, bucket_count)
        scores_low = grad_scores.astype(jnp.bfloat16)
        grad_query = grad_query + jnp.einsum(
            "hqk,khd->qhd", scores_low, key_block, preferred_element_type=jnp.float32
        )
        grad_value = jnp.einsum(
            "hqk,qhd->khd",
            probability.astype(jnp.bfloat16),
            grad_att,
            preferred_element_type=jnp.float32,
        )
        grad_key = jnp.einsum(
            "hqk,qhd->khd", scores_low, queries, preferred_element_type=jnp.float32
        )
        return ((grad_query, grad_bias), (grad_key, grad_value))

    start_state = (
        jnp.zeros((local_len, head_count, HDIM), jnp.float32),
        jnp.zeros((bucket_count, head_count), jnp.float32),
    )
    final_state, stacked = lax.scan(
        attend_one_block, start_state, (key_blocks, value_blocks, pos_blocks)
    )
    total_keys = keys_all.shape[0]
    return (
        final_state[0],
        final_state[1],
        stacked[0].reshape(total_keys, head_count * HDIM),
        stacked[1].reshape(total_keys, head_count * HDIM),
    )


def own_share(grad_term, grad_dim):
    share_len = grad_term.shape[grad_dim] // lax.axis_size("fsdp")
    return lax.dynamic_slice_in_dim(
        grad_term, lax.axis_index("fsdp") * share_len, share_len, grad_dim
    )


def per_device_plain(
    tokens,
    positions,
    w_query,
    w_key,
    w_value,
    w_out,
    w_in,
    w_back,
    gain_one,
    gain_two,
    bias_table,
    cotangent,
):
    micro_count = tokens.shape[0]
    head_count = w_query.shape[1] // HDIM
    head_cols = head_count * HDIM
    hidden_cols = w_in.shape[1]
    bucket_count = bias_table.shape[0] * lax.axis_size("fsdp")
    grad_wq = jnp.zeros((D, head_cols), jnp.float32)
    grad_wk = jnp.zeros((D, head_cols), jnp.float32)
    grad_wv = jnp.zeros((D, head_cols), jnp.float32)
    grad_wo = jnp.zeros((head_cols, D), jnp.float32)
    grad_wi = jnp.zeros((D, hidden_cols), jnp.float32)
    grad_wb = jnp.zeros((hidden_cols, D), jnp.float32)
    grad_table = jnp.zeros((bucket_count, head_count), jnp.float32)
    grad_gain_one = jnp.zeros((D,), jnp.float32)
    grad_gain_two = jnp.zeros((D,), jnp.float32)
    outputs = []
    input_grads = []
    for micro_step in range(micro_count):
        full_wq, full_wk, full_wv, full_wo, full_wi, full_wb, full_g1, full_g2, full_table = (
            lax.all_gather(w_query, "fsdp", axis=0, tiled=True),
            lax.all_gather(w_key, "fsdp", axis=0, tiled=True),
            lax.all_gather(w_value, "fsdp", axis=0, tiled=True),
            lax.all_gather(w_out, "fsdp", axis=1, tiled=True),
            lax.all_gather(w_in, "fsdp", axis=0, tiled=True),
            lax.all_gather(w_back, "fsdp", axis=1, tiled=True),
            lax.all_gather(gain_one, "fsdp", axis=0, tiled=True),
            lax.all_gather(gain_two, "fsdp", axis=0, tiled=True),
            lax.all_gather(bias_table, "fsdp", axis=0, tiled=True),
        )
        gain_first = full_g1.astype(jnp.float32)
        gain_second = full_g2.astype(jnp.float32)
        bias_rows = full_table.astype(jnp.float32)
        token_rows = tokens[micro_step, 0].astype(jnp.float32)
        query_pos = positions[micro_step, 0]
        scale_one = inverse_rms(token_rows)
        normed = spread_rows((token_rows * scale_one * gain_first).astype(jnp.bfloat16))
        local_len = normed.shape[0]
        key_rows = math.gcd(local_len, 256)
        queries_low = jnp.dot(normed, full_wq, preferred_element_type=jnp.float32).astype(
            jnp.bfloat16
        )
        keys_low = jnp.dot(normed, full_wk, preferred_element_type=jnp.float32).astype(jnp.bfloat16)
        values_low = jnp.dot(normed, full_wv, preferred_element_type=jnp.float32).astype(
            jnp.bfloat16
        )
        queries = queries_low.reshape(local_len, head_count, HDIM)
        start_state = (
            jnp.full((head_count, local_len), -1e30, jnp.float32),
            jnp.zeros((head_count, local_len), jnp.float32),
            jnp.zeros((head_count, local_len, HDIM), jnp.float32),
        )
        fold_keys = make_fold(queries, query_pos, bias_rows, key_rows)
        run_peak, run_total, run_acc = fold_keys(
            start_state,
            (
                lax.all_gather(keys_low, "ctx", axis=0, tiled=True),
                lax.all_gather(values_low, "ctx", axis=0, tiled=True),
                lax.all_gather(query_pos, "ctx", axis=0, tiled=True),
            ),
            jnp.int32(0),
        )
        log_total = run_peak + jnp.log(run_total)
        attended_f = jnp.transpose(run_acc / run_total[:, :, None], (1, 0, 2)).reshape(
            local_len, head_cols
        )
        attended = attended_f.astype(jnp.bfloat16)
        middle = token_rows + collect_rows(
            jnp.dot(attended, full_wo, preferred_element_type=jnp.float32)
        )
        scale_two = inverse_rms(middle)
        normed_two = spread_rows((middle * scale_two * gain_second).astype(jnp.bfloat16))
        hidden_pre = jnp.dot(normed_two, full_wi, preferred_element_type=jnp.float32)
        hidden = jax.nn.gelu(hidden_pre, approximate=False).astype(jnp.bfloat16)
        output_rows = middle + collect_rows(
            jnp.dot(hidden, full_wb, preferred_element_type=jnp.float32)
        )
        outputs.append(output_rows.astype(jnp.bfloat16))
        grad_local = cotangent[micro_step, 0]
        grad_full = spread_rows(grad_local)
        grad_wb = grad_wb + left_product(hidden, grad_full)
        grad_hidden = right_product(grad_full, full_wb)
        grad_pre = (grad_hidden * gelu_slope(hidden_pre)).astype(jnp.bfloat16)
        grad_wi = grad_wi + left_product(normed_two, grad_pre)
        grad_normed_two = collect_rows(right_product(grad_pre, full_wi))
        grad_middle, gain_part_two = norm_back(middle, scale_two, gain_second, grad_normed_two)
        grad_middle = grad_middle + grad_local.astype(jnp.float32)
        grad_gain_two = grad_gain_two + gain_part_two
        grad_mixed = spread_rows(grad_middle.astype(jnp.bfloat16))
        grad_wo = grad_wo + left_product(attended, grad_mixed)
        grad_attended = right_product(grad_mixed, full_wo).astype(jnp.bfloat16)
        row_delta = jnp.sum(
            (grad_attended.astype(jnp.float32) * attended_f).reshape(local_len, head_count, HDIM),
            axis=-1,
        ).T
        back_keys, back_values, back_pos = (
            lax.all_gather(keys_low, "ctx", axis=0, tiled=True),
            lax.all_gather(values_low, "ctx", axis=0, tiled=True),
            lax.all_gather(query_pos, "ctx", axis=0, tiled=True),
        )
        grad_att_heads = grad_attended.reshape(local_len, head_count, HDIM)
        grad_queries, table_part, grad_keys_all, grad_values_all = attend_back(
            queries,
            query_pos,
            bias_rows,
            back_keys,
            back_values,
            back_pos,
            grad_att_heads,
            log_total,
            row_delta,
            key_rows,
        )
        grad_keys, grad_values = (
            lax.psum_scatter(
                grad_keys_all.astype(jnp.bfloat16), "ctx", scatter_dimension=0, tiled=True
            ).astype(jnp.float32),
            lax.psum_scatter(
                grad_values_all.astype(jnp.bfloat16), "ctx", scatter_dimension=0, tiled=True
            ).astype(jnp.float32),
        )
        grad_table = grad_table + table_part
        grad_q_low = grad_queries.reshape(local_len, head_cols).astype(jnp.bfloat16)
        grad_k_low = grad_keys.astype(jnp.bfloat16)
        grad_v_low = grad_values.astype(jnp.bfloat16)
        grad_wq = grad_wq + left_product(normed, grad_q_low)
        grad_wk = grad_wk + left_product(normed, grad_k_low)
        grad_wv = grad_wv + left_product(normed, grad_v_low)
        grad_normed = collect_rows(
            right_product(grad_q_low, full_wq)
            + right_product(grad_k_low, full_wk)
            + right_product(grad_v_low, full_wv)
        )
        grad_input, gain_part_one = norm_back(token_rows, scale_one, gain_first, grad_normed)
        grad_gain_one = grad_gain_one + gain_part_one
        input_grads.append((grad_input + grad_middle).astype(jnp.bfloat16))
    gain_total_one, gain_total_two = lax.psum((grad_gain_one, grad_gain_two), ("fsdp", "ctx", "tp"))
    sum_wq, sum_wk, sum_wv, sum_wo, sum_wi, sum_wb, sum_table = lax.psum(
        (grad_wq, grad_wk, grad_wv, grad_wo, grad_wi, grad_wb, grad_table), ("fsdp", "ctx")
    )
    share_wq = own_share(sum_wq, 0)
    share_wk = own_share(sum_wk, 0)
    share_wv = own_share(sum_wv, 0)
    share_wo = own_share(sum_wo, 1)
    share_wi = own_share(sum_wi, 0)
    share_wb = own_share(sum_wb, 1)
    share_table = own_share(sum_table, 0)
    return (
        jnp.stack(outputs)[:, None],
        jnp.stack(input_grads)[:, None],
        own_share(gain_total_one, 0),
        own_share(gain_total_two, 0),
        share_wq,
        share_wk,
        share_wv,
        share_wo,
        share_wi,
        share_wb,
        share_table,
    )


MESH = pl.DeviceIdType.MESH
F32 = jnp.float32
BF16 = jnp.bfloat16
HEADS_HERE = 3
BLK = 128
VALUE_ROWS = (128, 192, 64)


def nn(left, right):
    return lax.dot_general(left, right, (((1,), (0,)), ((), ())), preferred_element_type=F32)


def nt(left, right):
    return lax.dot_general(left, right, (((1,), (1,)), ((), ())), preferred_element_type=F32)


def tn(left, right):
    return lax.dot_general(left, right, (((0,), (0,)), ((), ())), preferred_element_type=F32)


def at_rows(offset, size, unit):
    return pl.ds(pl.multiple_of(offset, unit), size)


def fold_rows(block):
    return jnp.sum(block.reshape(block.shape[0] // 8, 8, block.shape[1]), axis=0)


class Sems:
    def __init__(self):
        self.numbers = {}

    def __call__(self, *name):
        return self.numbers.setdefault(name, len(self.numbers))


PART = 256
BACK_PART = 128
REACH = (0, 1, 2, 3, 4, 5, 6, 7, 11, 15, 22, 31, 45, 63, 90, 127)


def grad_chunks(share, hidden):
    head_cols = HEADS_HERE * HDIM
    names = [(f"back{i}", BACK_PART, share) for i in range(hidden // BACK_PART)]
    names += [(f"in{i}", share, PART) for i in range(hidden // PART)]
    names += [(name, head_cols, share) for name in ("out", "key", "value", "query")]
    chunks, row = [], 0
    for name, rows, cols in names:
        chunks.append((name, row, rows, cols))
        row += rows
    return chunks, row


def layer_kernel(
    nf, nc, micro, rows_own, share, hidden, n_sems, sems,
    tok, pos_in, wq_in, wk_in, wv_in, wo_loc, wi_loc, wb_loc, g1_in, g2_in, table_in, cot,
    out, grad_in, grads_out, small_out,
    w_loc, small_loc, wqkv, wo, wi, wb, small_rx, smallf, n1, g, posb, bkt, bias, qm, kv, e_t, s_t, ds_t, att_t,
    inv, att, keep, keep6, send1, send2, recv1, recv2, zsend, zrecv, gz, n2, hid, gp, gm,
    mid_f, gmid, dq, dom, nds, gacc, tacc, facc, gain2, xs, xr, zr1, zr2, sm, smr,
    ssem, rsem, lsem,
):
    f, c, t = lax.axis_index("fsdp"), lax.axis_index("ctx"), lax.axis_index("tp")
    nt_ = 4
    T = rows_own
    R = nt_ * T
    L = nc * R
    NB = L // BLK
    t1 = t + 1 - 2 * lax.rem(t, 2)
    t2 = lax.rem(t + 2, 4)
    t3 = lax.rem(t1 + 2, 4)
    sib, ypeer = (f, c, t1), (f, c, t2)
    xpeers = [(lax.rem(f + j, nf), c, t) for j in range(1, nf)]
    zpeers = [(f, lax.rem(c + k, nc), t) for k in range(1, nc)]
    below, above = (f, jnp.maximum(c - 1, 0), t), (f, jnp.minimum(c + 1, nc - 1), t)
    half_c = nc // 2
    low_side = c < half_c
    inward = jnp.where(low_side, c + 1, c - 1)
    outward = jnp.clip(jnp.where(low_side, c - 1, c + 1), 0, nc - 1)
    is_mid = (c == half_c - 1) | (c == half_c)
    has_out = (c > 0) & (c < nc - 1)
    if nc == 2:
        has_out = c < 0
    chunks, chunk_rows = grad_chunks(share, hidden)
    pending = []
    zs = xs.at[0]
    scr = s_t.at[pl.ds(0, 4 * rows_own)]

    def send(src, dst, name_s, name_r, dev, when=None):
        copy = pltpu.make_async_remote_copy(
            src, dst, ssem.at[sems(*name_s)], rsem.at[sems(*name_r)], device_id=dev, device_id_type=MESH
        )
        if when is None:
            copy.start()
        else:
            pl.when(when)(copy.start)
        pending.append((name_s, copy, when))

    def sent(*name_s):
        assert any(name == name_s for name, copy, when in pending), name_s
        for at, (name, copy, when) in enumerate(pending):
            if name == name_s:
                if when is None:
                    copy.wait_send()
                else:
                    pl.when(when)(copy.wait_send)
                del pending[at]
                return

    def arrived(dst, *name_r):
        pltpu.make_async_remote_copy(
            dst, dst, ssem.at[sems(*name_r)], rsem.at[sems(*name_r)], device_id=sib, device_id_type=MESH
        ).wait_recv()

    def rms(rows):
        return lax.rsqrt(jnp.mean(rows * rows, axis=-1, keepdims=True) + epsilon)

    def piece(m, block, t_of):
        return n1.at[at_rows(m * L + block * R + t_of * T, T, T)]

    def rows_of(m, t_of):
        return at_rows(m * R + t_of * T, T, T)

    posb[0] = jnp.zeros_like(posb[0])
    posb[2] = jnp.zeros_like(posb[2])
    barrier = pltpu.get_barrier_semaphore()
    peers = [sib, ypeer] + xpeers + zpeers
    for dev in peers:
        pl.semaphore_signal(barrier, inc=1, device_id=dev, device_id_type=MESH)
    for m in range(micro):
        rows = tok[m].astype(F32)
        n1[at_rows(m * L + c * R + t * T, T, T)] = (rows * rms(rows)).astype(BF16)
    posb[1] = pos_in[...]
    local = {}

    def local_copy(src, dst, i):
        copy = pltpu.make_async_copy(src, dst, lsem.at[i])
        copy.start()
        local[i] = copy

    share_cols = at_rows(f * share, share, BLK)
    share_rows = at_rows(f * share, share, BLK)
    own_rows = at_rows(t * T, T, T)
    qkv_parts = (
        (wq_in, 0, 0, 192), (wk_in, 0, 256, 192), (wv_in, 128, 448, 64), (wv_in, 0, 512, 128),
    )
    for i, (src, row, at, size) in enumerate(qkv_parts):
        local_copy(src.at[pl.ds(row, size)], w_loc.at[pl.ds(at, size)], 4 + micro + len(chunks) + i)
    local_copy(wo_loc.at[pl.ds(0, 128)], wo.at[pl.ds(128, 128), share_cols], 0)
    local_copy(wo_loc.at[pl.ds(128, 64)], wo.at[pl.ds(64, 64), share_cols], 1)
    local_copy(wi_loc, wi.at[share_rows], 2)
    local_copy(wb_loc, wb.at[:, share_cols], 3)
    for m in range(micro):
        local_copy(cot.at[m], g.at[rows_of(m, t)], 4 + m)
    small_loc[...] = jnp.zeros_like(small_loc)
    small_loc[0:1, share_cols] = g1_in[...].astype(F32).reshape(1, share)
    small_loc[1:2, share_cols] = g2_in[...].astype(F32).reshape(1, share)
    buckets_here = table_in.shape[1]
    spot = lax.broadcasted_iota(jnp.int32, (buckets_here, 128), 1) - f * buckets_here
    spot = spot == lax.broadcasted_iota(jnp.int32, (buckets_here, 128), 0)
    small_loc[0:HEADS_HERE, pl.ds(D, 128)] = nn(table_in[...], jnp.where(spot, 1.0, 0.0).astype(BF16))

    small_rx[f] = small_loc[...]
    pl.semaphore_wait(barrier, len(peers))

    def spread_first(m):
        mine = piece(m, c, t)
        send(mine, mine, ("ny", m, 0), ("ny", m, 0), ypeer)
        send(mine, mine, ("nd", m), ("nz", m, 1), below, c > 0)
        send(mine, mine, ("nu", m), ("nz", m, nc - 1), above, c < nc - 1)
        send(mine, mine, ("ns", m, 0), ("ns", m, 0), sib)

    def send_small():
        for j, dev in enumerate(xpeers):
            send(small_loc, small_rx.at[f], ("small", j), ("small", nf - 2 - j), dev)
        send(pos_in, posb.at[0], ("posu",), ("posu",), (f, jnp.minimum(c + 1, nc - 1), t), c < nc - 1)
        send(pos_in, posb.at[2], ("posd",), ("posd",), (f, jnp.maximum(c - 1, 0), t), c > 0)

    def send_qkv():
        for j, dev in enumerate(xpeers):
            for i, (src, row, at, size) in enumerate(qkv_parts):
                dst = wqkv.at[pl.ds(at, size), share_cols]
                send(src.at[pl.ds(row, size)], dst, ("wqkv", i, j), ("wqkv", i, nf - 2 - j), dev)

    def send_wo():
        for j, dev in enumerate(xpeers):
            send(wo_loc.at[pl.ds(0, 128)], wo.at[pl.ds(128, 128), share_cols], ("woa", j), ("woa", nf - 2 - j), dev)
            send(wo_loc.at[pl.ds(128, 64)], wo.at[pl.ds(64, 64), share_cols], ("wob", j), ("wob", nf - 2 - j), dev)

    def send_wi():
        for j, dev in enumerate(xpeers):
            send(wi_loc, wi.at[share_rows], ("wi", j), ("wi", nf - 2 - j), dev)

    def send_wb():
        for j, dev in enumerate(xpeers):
            send(wb_loc, wb.at[:, share_cols], ("wb", j), ("wb", nf - 2 - j), dev)

    def share_g(m):
        local[4 + m].wait()
        spread_own("g", g, m)

    def clear():
        w_loc[192:256] = jnp.zeros((64, share), BF16)
        wqkv[192:256] = jnp.zeros((64, D), BF16)
        wo[pl.ds(0, 64)] = jnp.zeros((64, D), BF16)
        dom[...] = jnp.zeros_like(dom)
        tacc[...] = jnp.zeros_like(tacc)
        facc[...] = jnp.zeros_like(facc)
        sm[0] = jnp.zeros((8, D + 128), F32)

    def spread_own(name, buf, m):
        mine = buf.at[rows_of(m, t)]
        send(mine, mine, (name, "y", m), (name, "y", m), ypeer)
        send(mine, mine, (name, "s", m), (name, "s", m), sib)

    def spread_on(name, buf, m):
        there = buf.at[rows_of(m, t2)]
        arrived(there, name, "y", m)
        send(there, there, (name, "f", m), (name, "f", m), sib)

    def spread_end(name, buf, m):
        arrived(buf.at[rows_of(m, t1)], name, "s", m)
        arrived(buf.at[rows_of(m, t3)], name, "f", m)

    def line_block(h, low):
        if low:
            return c >= h, jnp.maximum(c - h, 0), nc - h
        return c + h < nc, jnp.minimum(c + h, nc - 1), h

    def gather_z(m, h, low):
        there, z, k = line_block(h, low)
        block = piece(m, z, t)

        @pl.when(there)
        def _():
            arrived(block, "nz", m, k)

        if h < nc - 1 and low:
            send(block, block, ("nzu", m, k), ("nz", m, k - 1), above, there & (c < nc - 1))
        elif h < nc - 1:
            send(block, block, ("nzd", m, k), ("nz", m, k + 1), below, there & (c > 0))
        send(block, block, ("ny", m, k, low), ("ny", m, k), ypeer, there)
        send(block, block, ("ns", m, k, low), ("ns", m, k), sib, there)

    def gather_own(m):
        block = piece(m, c, t2)
        arrived(block, "ny", m, 0)
        send(block, block, ("nf", m, 0), ("nf", m, 0), sib)

    def gather_y(m, h, low):
        there, z, k = line_block(h, low)
        block = piece(m, z, t2)

        @pl.when(there)
        def _():
            arrived(block, "ny", m, k)

        send(block, block, ("nf", m, k, low), ("nf", m, k), sib, there)

    def gather_end(m):
        for k in range(nc):
            z = lax.rem(c + k, nc)
            arrived(piece(m, z, t1), "ns", m, k)
            arrived(piece(m, z, t3), "nf", m, k)

    def take_small():
        for j in range(nf - 1):
            arrived(small_rx.at[lax.rem(f + 1 + j, nf)], "small", j)
        total = small_rx[0]
        for j in range(1, nf):
            total = total + small_rx[j]
        smallf[...] = total

    def take_positions():
        @pl.when(c > 0)
        def _():
            arrived(posb.at[0], "posu")

        @pl.when(c < nc - 1)
        def _():
            arrived(posb.at[2], "posd")

    def bias_of(m):
        for qb in range(2):
            query_row = posb[1, m, :, pl.ds(qb * BLK, BLK)]
            for d in (-1, 0, 1):
                slot, row = ((0, 1), (1, 0), (1, 1), (2, 0))[qb + d + 1]
                key_row = posb[slot, m, :, pl.ds(row * BLK, BLK)]
                key_col = jnp.transpose(jnp.broadcast_to(key_row, (BLK, BLK)))
                relative = key_col - query_row
                size = jnp.abs(relative)
                bucket = jnp.minimum(size, 8)
                for edge_value in bucket_edges:
                    bucket = bucket + (size >= edge_value).astype(jnp.int32)
                bucket = bucket + 16 * (relative > 0).astype(jnp.int32)
                sub = qb * 3 + d + 1
                bkt[m, sub] = bucket
                for h in range(HEADS_HERE):
                    row_of = jnp.broadcast_to(smallf[h : h + 1, pl.ds(D, 128)], (BLK, BLK))
                    bias[m, sub, h] = jnp.take_along_axis(row_of, bucket, axis=1).astype(BF16)

    def fold_gain():
        for i in range(len(qkv_parts)):
            local[4 + micro + len(chunks) + i].wait()
        wqkv[:, share_cols] = w_loc[...]
        for j in range(nf - 1):
            cols = at_rows(lax.rem(f + 1 + j, nf) * share, share, BLK)
            for i, (src, row, at, size) in enumerate(qkv_parts):
                arrived(wqkv.at[pl.ds(at, size), cols], "wqkv", i, j)
        wqkv[...] = (wqkv[...].astype(F32) * smallf[0:1, 0:D]).astype(BF16)

    def reduce_start(slot, rid, kept, value, previous):
        scr[...] = value
        if previous is not None:
            sent("r1", previous)
        send1[slot, 0] = scr[at_rows(t1 * T, T, T)].astype(BF16)
        send1[slot, 1] = scr[at_rows(t3 * T, T, T)].astype(BF16)
        send(send1.at[slot], recv1.at[rid], ("r1", rid), ("r1", rid), sib)
        kept[0] = scr[own_rows].astype(kept.dtype)
        kept[1] = scr[at_rows(t2 * T, T, T)].astype(kept.dtype)

    def reduce_mid(slot, rid, kept, previous):
        arrived(recv1.at[rid], "r1", rid)
        if previous is not None:
            sent("r2", previous)
        send2[slot] = (kept[1].astype(F32) + recv1[rid, 1].astype(F32)).astype(BF16)
        send(send2.at[slot], recv2.at[rid], ("r2", rid), ("r2", rid), ypeer)
        kept[0] = (kept[0].astype(F32) + recv1[rid, 0].astype(F32)).astype(kept.dtype)

    def reduce_end(rid, kept):
        arrived(recv2.at[rid], "r2", rid)
        return kept[0].astype(F32) + recv2[rid].astype(F32)

    def phase(p, m):
        rid = p * micro + m
        return p, rid, keep.at[2 * p + m % 2], (rid - 1 if m > 0 else None)

    def start_phase(p, m, value):
        slot, rid, kept, previous = phase(p, m)
        reduce_start(slot, rid, kept, value, previous)

    def mid_phase(p, m):
        slot, rid, kept, previous = phase(p, m)
        reduce_mid(slot, rid, kept, previous)

    def end_phase(p, m):
        slot, rid, kept, previous = phase(p, m)
        return reduce_end(rid, kept)

    wide_cols = HEADS_HERE * R

    def far_row(kb, below, above):
        parts = []
        for h in range(HEADS_HERE):
            for qb in range(2):
                d = kb - 2 * c - qb
                parts.append(jnp.where(d < -1, below[h], jnp.where(d > 1, above[h], 0.0)))
        return jnp.concatenate(parts, axis=1)

    def near_blocks(use):
        for qb in range(2):
            for d in (-1, 0, 1):
                kb = 2 * c + qb + d
                if qb + d in (0, 1):
                    use(qb, d, kb)
                else:
                    pl.when((kb >= 0) & (kb < NB))(functools.partial(use, qb, d, kb))

    def project(m):
        own = at_rows(m * L + c * R, R, R)
        queries = nt(n1[own], wqkv[0:256])
        lane = lax.broadcasted_iota(jnp.int32, (R, 256), 1)
        for h in range(HEADS_HERE):
            keep_it = (lane >= h * HDIM) & (lane < (h + 1) * HDIM)
            qm[m, pl.ds(h * R, R)] = jnp.where(keep_it, queries, 0.0).astype(BF16)
        kv[pl.ds(m * L, L)] = nt(n1[pl.ds(m * L, L)], wqkv[256:640]).astype(BF16)

    def attend(m):
        first = m * L
        every = pl.ds(first, L)
        s_t[...] = nt(kv[every, 0:256], qm[m])
        tables = [smallf[h : h + 1, pl.ds(D, 128)] for h in range(HEADS_HERE)]
        below = [jnp.broadcast_to(tab[:, 15:16], (1, BLK)) for tab in tables]
        above = [jnp.broadcast_to(tab[:, 31:32], (1, BLK)) for tab in tables]

        def near(qb, d, kb):
            r = at_rows(kb * BLK, BLK, BLK)
            for h in range(HEADS_HERE):
                q = pl.ds(h * R + qb * BLK, BLK)
                s_t[r, q] = s_t[r, q] + bias[m, qb * 3 + d + 1, h].astype(F32)

        near_blocks(near)

        def peak(kb, top):
            block = s_t[at_rows(kb * BLK, BLK, BLK)]
            block = jnp.max(block.reshape(BLK // 8, 8, wide_cols), axis=0)
            return jnp.maximum(top, block + far_row(kb, below, above))

        top = lax.fori_loop(0, NB, peak, jnp.full((8, wide_cols), -jnp.inf, F32))
        top = jnp.max(top, axis=0, keepdims=True)

        def expo(kb, total):
            weights = jnp.exp(s_t[at_rows(kb * BLK, BLK, BLK)] - (top - far_row(kb, below, above)))
            e_t[at_rows(first + kb * BLK, BLK, BLK)] = weights.astype(BF16)
            return total + fold_rows(weights)

        total = lax.fori_loop(0, NB, expo, jnp.zeros((8, wide_cols), F32))
        over = 1.0 / jnp.sum(total, axis=0, keepdims=True)
        inv[m] = jnp.broadcast_to(over, (8, wide_cols))
        mixed = tn(kv[every, 128:384], e_t[every])
        for h in range(HEADS_HERE):
            v0 = VALUE_ROWS[h]
            cols = slice(h * R, (h + 1) * R)
            att_t[m, pl.ds(v0, HDIM)] = mixed[v0 : v0 + HDIM, cols] * over[:, cols]
        att_t[m, pl.ds(0, HDIM)] = jnp.zeros((HDIM, R), F32)
        attended = jnp.transpose(att_t[m]).astype(BF16)
        att[pl.ds(m * R, R)] = attended

    def mix(m):
        start_phase(0, m, nn(att[pl.ds(m * R, R)], wo[...]))

    def take_wo():
        local[0].wait()
        local[1].wait()
        for j in range(nf - 1):
            cols = at_rows(lax.rem(f + 1 + j, nf) * share, share, BLK)
            arrived(wo.at[pl.ds(128, 128), cols], "woa", j)
            arrived(wo.at[pl.ds(64, 64), cols], "wob", j)

    def take_wi():
        local[2].wait()
        for j in range(nf - 1):
            arrived(wi.at[at_rows(lax.rem(f + 1 + j, nf) * share, share, BLK)], "wi", j)

    def take_wb():
        local[3].wait()
        for j in range(nf - 1):
            arrived(wb.at[:, at_rows(lax.rem(f + 1 + j, nf) * share, share, BLK)], "wb", j)

    def norm_two(m):
        middle = tok[m].astype(F32) + end_phase(0, m)
        mid_f[m] = middle
        n2[rows_of(m, t)] = (middle * rms(middle) * smallf[1:2, 0:D]).astype(BF16)
        spread_own("n2", n2, m)

    def feed(m):
        spread_end("n2", n2, m)
        here = pl.ds(m * R, R)
        rows = n2[here]

        def one(i, unused):
            cols = at_rows(i * 256, 256, 256)
            pre = nn(rows, wi[:, cols])
            slope = nt(g[here], wb[cols])
            bell = 0.5 * (1.0 + lax.erf(pre * 0.7071067811865476))
            hid[here, cols] = (pre * bell).astype(BF16)
            bell = bell + pre * jnp.exp(-0.5 * pre * pre) * 0.3989422804014327
            gp[here, cols] = (slope * bell).astype(BF16)
            return unused

        lax.fori_loop(0, hidden // 256, one, 0)
        start_phase(1, m, nt(gp[here], wi[...]))
        start_phase(2, m, nn(hid[here], wb[...]))

    def output_rows(m):
        out[m] = (mid_f[m] + end_phase(2, m)).astype(BF16)

    def back_two(m):
        grad_normed = end_phase(1, m)
        middle = mid_f[m]
        scale = rms(middle)
        unit = middle * scale
        part = fold_rows(grad_normed * unit)
        gain2[...] = part if m == 0 else gain2[...] + part
        weighted = smallf[1:2, 0:D] * grad_normed
        grad = scale * (weighted - unit * jnp.mean(unit * weighted, axis=-1, keepdims=True))
        grad = grad + g[rows_of(m, t)].astype(F32)
        gmid[m] = grad
        gm[rows_of(m, t)] = grad.astype(BF16)
        spread_own("gm", gm, m)

    def attend_back(m):
        first = m * L
        every = pl.ds(first, L)
        grad_att = nt(wo[...], gm[pl.ds(m * R, R)]).astype(BF16).astype(F32)
        deltas = []
        for h in range(HEADS_HERE):
            v0 = VALUE_ROWS[h]
            scaled = (grad_att[v0 : v0 + HDIM] * inv[m, 0:1, pl.ds(h * R, R)]).astype(BF16)
            dom[pl.ds(v0, HDIM), pl.ds(h * R, R)] = scaled
            deltas.append(jnp.sum(scaled.astype(F32) * att_t[m, pl.ds(v0, HDIM)], axis=0, keepdims=True))
        delta = jnp.concatenate(deltas, axis=1)
        s_t[...] = nn(kv[every, 128:384], dom[...])
        half = lax.rem(lax.broadcasted_iota(jnp.int32, (8, wide_cols), 1) // BLK, 2)

        def one_block(kb, sums):
            r = at_rows(kb * BLK, BLK, BLK)
            grad = e_t[at_rows(first + kb * BLK, BLK, BLK)].astype(F32) * (s_t[r] - delta)
            ds_t[r] = grad.astype(BF16)
            part = fold_rows(grad)
            d = kb - 2 * c - half
            return sums[0] + jnp.where(d < -1, part, 0.0), sums[1] + jnp.where(d > 1, part, 0.0)

        zero = jnp.zeros((8, wide_cols), F32)
        low, high = lax.fori_loop(0, NB, one_block, (zero, zero))
        facc[0] += low
        facc[1] += high

        def save(qb, d, kb):
            r = at_rows(kb * BLK, BLK, BLK)
            for h in range(HEADS_HERE):
                nds[m, qb * 3 + d + 1, h] = ds_t[r, pl.ds(h * R + qb * BLK, BLK)]

        near_blocks(save)
        grad_q = tn(kv[every, 0:256], ds_t[...])
        columns = [grad_q[h * HDIM : (h + 1) * HDIM, h * R : (h + 1) * R] for h in range(HEADS_HERE)]
        columns.append(jnp.zeros((HDIM, R), F32))
        dq[pl.ds(m * R, R)] = jnp.transpose(jnp.concatenate(columns, axis=0)).astype(BF16)
        grad_k = nn(ds_t[...], qm[m])
        grad_v = nt(e_t[every], dom[...])
        kv[every, 0:128] = grad_k[:, 0:128].astype(BF16)
        kv[every, 128:256] = (grad_k[:, 128:256] + grad_v[:, 0:128]).astype(BF16)
        kv[every, 256:384] = grad_v[:, 128:256].astype(BF16)

    def merged(block, spots):
        where_at, parts = spots
        size = BLK // parts
        out_block = block[(parts - 1) * size :]
        for i in range(parts - 2, -1, -1):
            out_block = jnp.where(where_at == i, block[i * size : (i + 1) * size], out_block)
        return out_block

    def spots_of(parts):
        size = BLK // parts
        lane = lax.broadcasted_iota(jnp.int32, (size, BLK), 1)
        tile = lax.broadcasted_iota(jnp.int32, (size, BLK), 0) // 8
        away = lane - 8 * tile - 4 + size // 2
        spot = jnp.zeros((size, BLK), jnp.int32)
        for i in range(1, parts):
            spot = spot + (away >= i * size).astype(jnp.int32)
        return spot, parts

    def bin_table(m):
        def use(qb, d, kb):
            sub = qb * 3 + d + 1

            def bins(names, ids, blocks):
                for b in names:
                    same = ids == b
                    for h in range(HEADS_HERE):
                        tacc[h, b] += fold_rows(jnp.where(same, blocks[h], 0.0))

            if d == 0:
                ids = bkt[m, sub]
                blocks = [nds[m, sub, h].astype(F32) for h in range(HEADS_HERE)]
                for parts, sizes in ((4, range(0, 9)), (2, range(9, 11))):
                    spots = spots_of(parts)
                    both = [b for b in sizes] + [16 + b for b in sizes if b > 0]
                    bins(both, merged(ids, spots), [merged(block, spots) for block in blocks])
                bins([b + s for b in range(11, 16) for s in (0, 16)], ids, blocks)
            else:
                for size in range(1, 16):
                    rows = min(BLK, (REACH[size] + 7) // 8 * 8)
                    low = (rows + 15) // 16 * 16
                    r = pl.ds(BLK - rows if d < 0 else 0, rows)
                    part = slice(low - rows, low) if d < 0 else slice(0, rows)
                    low = pl.ds(BLK - low if d < 0 else 0, low)
                    blocks = [nds[m, sub, h, low].astype(F32)[part] for h in range(HEADS_HERE)]
                    bins([size if d < 0 else 16 + size], bkt[m, sub, r], blocks)

        near_blocks(use)

    def six(m, k):
        return 3 + k, 3 * micro + m * nc + k, keep6.at[k], (3 * micro + (m - 1) * nc + k if m > 0 else None)

    def back_start(m, k):
        r = at_rows(m * L + lax.rem(c + k, nc) * R, R, R)
        value = nn(kv[r], wqkv[256:640])
        if k == 0:
            value = value + nn(dq[pl.ds(m * R, R)], wqkv[0:256])
        slot, rid, kept, previous = six(m, k)
        reduce_start(slot, rid, kept, value, previous)

    def back_mid(m, k):
        slot, rid, kept, previous = six(m, k)
        reduce_mid(slot, rid, kept, previous)

    def back_out(m, k):
        slot, rid, kept, previous = six(m, k)
        gz[m] = reduce_end(rid, kept)

    def line_slot(m, h, up):
        if h == 0:
            return zrecv.at[m, nc - 1 + int(up)]
        return zrecv.at[m, (h if up else nc - h) - 1]

    def back_pass(m, h, up):
        there, z, k = line_block(h, not up)
        slot, rid, kept, previous = six(m, k)
        if m > 0:
            sent("gs", m - 1, h, up)
        more = c > 0 if up else c < nc - 1

        @pl.when(there & more)
        def _():
            arrived(line_slot(m, h, up), "gp", m, h, up)
            total = reduce_end(rid, kept) + line_slot(m, h, up)[...].astype(F32)
            zsend[k - 1] = total.astype(BF16)

        @pl.when(there & jnp.logical_not(more))
        def _():
            zsend[k - 1] = reduce_end(rid, kept).astype(BF16)

        dev = above if up else below
        send(zsend.at[k - 1], line_slot(m, h - 1, up), ("gs", m, h, up), ("gp", m, h - 1, up), dev, there)

    def back_one(m):
        for up, some in ((True, c > 0), (False, c < nc - 1)):

            @pl.when(some)
            def _(up=up):
                arrived(line_slot(m, 0, up), "gp", m, 0, up)
                gz[m] += line_slot(m, 0, up)[...].astype(F32)

        weighted = gz[m]
        rows = tok[m].astype(F32)
        scale = rms(rows)
        unit = rows * scale
        grad = scale * (weighted - unit * jnp.mean(unit * weighted, axis=-1, keepdims=True))
        grad_in[m] = (gmid[m] + grad).astype(BF16)

    def gather_grads(m):
        own = at_rows(m * L + c * R, R, R)
        every = pl.ds(m * L, L)
        for rows, value in (
            (pl.ds(0, 256), tn(dq[pl.ds(m * R, R)], n1[own])),
            (pl.ds(256, 384), tn(kv[every], n1[every])),
        ):
            gacc[rows] = value if m == 0 else gacc[rows] + value

    def each_part(chunk, part, use):
        name, row, rows, cols = chunk
        share_at = at_rows(part, share, BLK)
        if name.startswith("back"):
            use(row, rows, tn(hid[:, pl.ds(int(name[4:]) * BACK_PART, BACK_PART)], g[:, share_at]), None)
        elif name.startswith("in"):
            use(row, rows, tn(n2[:, share_at], gp[:, pl.ds(int(name[2:]) * PART, PART)]), None)
        elif name == "out":
            value = tn(att[...], gm[:, share_at])
            use(row, 128, value[128:], None)
            use(row + 128, 64, value[64:128], None)
        elif name == "value":
            use(row, 128, gacc[pl.ds(512, 128), share_at], 512)
            use(row + 128, 64, gacc[pl.ds(448, 64), share_at], 448)
        else:
            first = 0 if name == "query" else 256
            use(row, rows, gacc[pl.ds(first, rows), share_at], first)

    def share_out(q):
        chunk = chunks[q]
        name, row, rows, cols = chunk
        for j, dev in enumerate(xpeers):
            part = lax.rem(f + 1 + j, nf) * share

            def use(at, size, value, first, j=j):
                xs[j, pl.ds(at, size), 0:cols] = value.astype(BF16)

            each_part(chunk, part, use)
            src = xs.at[j, pl.ds(row, rows), pl.ds(0, cols)]
            dst = xr.at[nf - 2 - j, pl.ds(row, rows), pl.ds(0, cols)]
            send(src, dst, ("x", q, j), ("x", q, nf - 2 - j), dev)

    def own_share(q):
        chunk = chunks[q]
        name, row, rows, cols = chunk
        for j in range(nf - 1):
            arrived(xr.at[j, pl.ds(row, rows), pl.ds(0, cols)], "x", q, j)
        sent("x", q, 0)

        def use(at, size, value, first):
            for j in range(nf - 1):
                value = value + xr[j, pl.ds(at, size), 0:cols].astype(F32)
            if first is not None:
                weight = w_loc[pl.ds(first, size)].astype(F32)
                sm[0, 0:1, share_cols] += jnp.sum(weight * value, axis=0, keepdims=True)
                value = value * smallf[0:1, share_cols]
            zs[pl.ds(at, size), 0:cols] = value.astype(BF16)

        each_part(chunk, f * share, use)

    def first_inward(q):
        own_share(q)
        name, row, rows, cols = chunks[q]
        at = (pl.ds(row, rows), pl.ds(0, cols))
        dev = (f, inward, t)
        if nc == 2:
            send(zs.at[at], zr2.at[at], ("ze", q), ("zx", q), dev)
        else:
            send(zs.at[at], zr1.at[at], ("ze", q), ("zi", q), dev, jnp.logical_not(has_out))

    def then_inward(q):
        if nc == 2:
            return
        name, row, rows, cols = chunks[q]
        at = (pl.ds(row, rows), pl.ds(0, cols))

        @pl.when(has_out)
        def _():
            arrived(zr1.at[at], "zi", q)
            zs[at] = (zs[at].astype(F32) + zr1[at].astype(F32)).astype(BF16)

        send(zs.at[at], zr2.at[at], ("zm", q), ("zx", q), (f, inward, t), is_mid)

    def then_outward(q):
        name, row, rows, cols = chunks[q]
        at = (pl.ds(row, rows), pl.ds(0, cols))

        @pl.when(is_mid)
        def _():
            arrived(zr2.at[at], "zx", q)
            zr2[at] = (zs[at].astype(F32) + zr2[at].astype(F32)).astype(BF16)

        if nc > 2:
            send(zr2.at[at], zr2.at[at], ("zo", q), ("zo", q), (f, outward, t), has_out)

    def last_outward(q):
        name, row, rows, cols = chunks[q]
        at = (pl.ds(row, rows), pl.ds(0, cols))

        @pl.when(jnp.logical_not(is_mid))
        def _():
            arrived(zr2.at[at], "zo", q)

        local_copy(zr2.at[at], grads_out.at[at], 4 + micro + q)

    def small_start():
        g2 = jnp.sum(gain2[...], axis=0, keepdims=True)
        sm[0, 1:2, 0:D] = g2
        for h in range(HEADS_HERE):
            below = jnp.sum(jnp.sum(facc[0, :, pl.ds(h * R, R)], axis=0, keepdims=True), axis=1, keepdims=True)
            above = jnp.sum(jnp.sum(facc[1, :, pl.ds(h * R, R)], axis=0, keepdims=True), axis=1, keepdims=True)
            per = jnp.sum(tacc[h], axis=1)
            per = jnp.sum(jnp.concatenate([per, jnp.zeros((96, 128), F32)], axis=0), axis=1, keepdims=True)
            line = jnp.transpose(jnp.broadcast_to(per, (128, 128)))[0:1, :]
            lane = lax.broadcasted_iota(jnp.int32, (1, 128), 1)
            line = line + jnp.where(lane == 15, below, 0.0) + jnp.where(lane == 31, above, 0.0)
            sm[0, h : h + 1, pl.ds(D, 128)] = line

    def small_send(step):
        if step == 0:
            send(sm.at[0], smr.at[0], ("m", 0), ("m", 0), sib)
        elif step == 1:
            send(sm.at[1], smr.at[1], ("m", 1), ("m", 1), ypeer)
        elif step == 2:
            for j, dev in enumerate(xpeers):
                send(sm.at[2], smr.at[2 + nf - 2 - j], ("mx", j), ("mx", nf - 2 - j), dev)
        else:
            for k in range(1, nc):
                send(sm.at[3], smr.at[1 + nf + nc - k - 1], ("mz", k), ("mz", nc - k), zpeers[k - 1])

    def small_take(step):
        if step < 2:
            arrived(smr.at[step], "m", step)
            lanes = lax.broadcasted_iota(jnp.int32, (8, D + 128), 1)
            sm[step + 1] = sm[step] + jnp.where(lanes < D, smr[step], 0.0)
        elif step == 2:
            total = sm[2]
            for j in range(nf - 1):
                arrived(smr.at[2 + j], "mx", j)
                total = total + smr[2 + j]
            sm[3] = total
        else:
            total = sm[3]
            for k in range(1, nc):
                arrived(smr.at[1 + nf + k - 1], "mz", k)
                total = total + smr[1 + nf + k - 1]
            small_out[...] = total
            smr[0] = total
            for i in range(2):
                small_out[i : i + 1, 0:share] = smr[0, i : i + 1, share_cols]

    spread_first(0)
    send_small()
    share_g(0)
    send_qkv()
    spread_first(1)
    send_wo()
    send_wi()
    gather_z(0, 1, False)
    gather_z(0, 1, True)
    gather_z(0, 2, True)
    gather_z(1, 1, False)
    gather_z(0, 2, False)
    gather_z(0, 3, False)
    spread_first(2)
    send_wb()
    gather_z(1, 1, True)
    gather_z(1, 2, False)
    gather_own(0)
    clear()
    take_positions()
    gather_y(0, 1, True)
    gather_z(2, 1, False)
    take_small()
    gather_y(0, 3, False)
    gather_z(2, 2, False)
    spread_on("g", g, 0)
    gather_y(0, 1, False)
    gather_z(2, 1, True)
    take_wo()
    gather_z(0, 3, True)
    gather_y(0, 2, True)
    gather_z(1, 3, False)
    gather_y(0, 2, False)
    gather_z(1, 2, True)
    gather_z(1, 3, True)
    gather_z(2, 3, False)
    bias_of(0)
    gather_y(0, 3, True)
    gather_z(2, 2, True)
    gather_own(1)
    fold_gain()
    gather_own(2)
    gather_end(0)
    share_g(2)
    project(0)
    attend(0)
    gather_z(2, 3, True)
    mix(0)
    gather_y(1, 1, True)
    mid_phase(0, 0)
    gather_y(1, 1, False)
    bias_of(1)
    gather_y(1, 3, False)
    gather_y(1, 2, False)
    gather_y(1, 3, True)
    bias_of(2)
    gather_y(2, 2, False)
    gather_y(1, 2, True)
    spread_end("g", g, 0)
    gather_end(1)
    project(1)
    share_g(1)
    gather_y(2, 1, True)
    attend(1)
    gather_y(2, 3, True)
    mix(1)
    gather_y(2, 2, True)
    gather_y(2, 1, False)
    gather_y(2, 3, False)
    gather_end(2)
    norm_two(0)
    take_wi()
    project(2)
    mid_phase(0, 1)
    attend(2)
    mix(2)
    spread_on("g", g, 2)
    spread_on("n2", n2, 0)
    mid_phase(0, 2)
    norm_two(1)
    take_wb()
    feed(0)
    norm_two(2)
    spread_on("g", g, 1)
    spread_end("g", g, 1)
    mid_phase(1, 0)
    mid_phase(2, 0)
    spread_on("n2", n2, 1)
    feed(1)
    back_two(0)
    spread_end("g", g, 2)
    spread_on("n2", n2, 2)
    mid_phase(1, 1)
    output_rows(0)
    feed(2)
    share_out(2)
    share_out(3)
    share_out(7)
    spread_on("gm", gm, 0)
    spread_end("gm", gm, 0)
    mid_phase(1, 2)
    back_two(1)
    attend_back(0)
    back_start(0, 3)
    share_out(0)
    share_out(1)
    first_inward(2)
    first_inward(3)
    back_two(2)
    back_start(0, 2)
    share_out(4)
    share_out(5)
    back_start(0, 1)
    spread_on("gm", gm, 1)
    gather_grads(0)
    back_mid(0, 1)
    then_inward(2)
    then_inward(3)
    back_mid(0, 2)
    spread_end("gm", gm, 1)
    first_inward(7)
    spread_on("gm", gm, 2)
    mid_phase(2, 1)
    back_mid(0, 3)
    back_start(0, 0)
    share_out(8)
    then_inward(7)
    first_inward(0)
    first_inward(1)
    attend_back(1)
    then_outward(2)
    then_outward(3)
    first_inward(4)
    first_inward(5)
    then_inward(0)
    then_inward(1)
    share_out(6)
    back_pass(0, 3, False)
    spread_end("gm", gm, 2)
    attend_back(2)
    back_mid(0, 0)
    then_outward(7)
    back_pass(0, 3, True)
    then_inward(4)
    then_inward(5)
    first_inward(8)
    back_pass(0, 2, False)
    then_outward(0)
    then_outward(1)
    gather_grads(1)
    share_out(9)
    back_pass(0, 2, True)
    then_inward(8)
    then_outward(4)
    then_outward(5)
    first_inward(6)
    back_pass(0, 1, False)
    back_start(1, 2)
    gather_grads(2)
    share_out(11)
    share_out(12)
    back_start(1, 3)
    last_outward(2)
    last_outward(3)
    back_pass(0, 1, True)
    back_out(0, 0)
    then_inward(6)
    then_outward(8)
    back_start(1, 1)
    back_mid(1, 2)
    back_mid(1, 3)
    first_inward(9)
    then_inward(9)
    back_start(1, 0)
    back_mid(1, 1)
    then_outward(6)
    first_inward(12)
    first_inward(11)
    then_inward(12)
    share_out(10)
    bin_table(0)
    back_one(0)
    mid_phase(2, 2)
    then_outward(9)
    back_pass(1, 3, True)
    bin_table(1)
    then_inward(11)
    back_pass(1, 3, False)
    back_mid(1, 0)
    first_inward(10)
    then_outward(12)
    back_pass(1, 2, True)
    back_pass(1, 2, False)
    back_start(2, 2)
    output_rows(2)
    bin_table(2)
    small_start()
    small_send(0)
    then_inward(10)
    last_outward(7)
    back_mid(2, 2)
    then_outward(11)
    small_take(0)
    small_send(1)
    back_pass(1, 1, False)
    back_start(2, 3)
    back_pass(1, 1, True)
    back_mid(2, 3)
    back_pass(2, 3, True)
    back_start(2, 1)
    back_mid(2, 1)
    back_pass(2, 3, False)
    last_outward(6)
    last_outward(11)
    small_take(1)
    last_outward(0)
    last_outward(1)
    small_send(2)
    then_outward(10)
    back_out(1, 0)
    last_outward(12)
    back_pass(2, 2, True)
    back_pass(2, 2, False)
    last_outward(8)
    small_take(2)
    small_send(3)
    back_start(2, 0)
    back_mid(2, 0)
    back_pass(2, 1, True)
    back_pass(2, 1, False)
    output_rows(1)
    last_outward(10)
    back_one(1)
    last_outward(9)
    small_take(3)
    last_outward(4)
    last_outward(5)
    back_out(2, 0)
    back_one(2)
    for q in range(len(chunks)):
        local[4 + micro + q].wait()
    for name, copy, when in pending:
        if when is None:
            copy.wait_send()
        else:
            pl.when(when)(copy.wait_send)
    assert len(sems.numbers) <= n_sems, len(sems.numbers)


def kernel_scratch(nf, nc, micro, T, share, hidden, n_sems):
    R = 4 * T
    L = nc * R
    vm = lambda shape, kind=BF16: pltpu.VMEM(shape, kind)
    rids = 3 * micro + nc * micro
    chunks, chunk_rows = grad_chunks(share, hidden)
    wide = max(384, share)
    return [
        vm((640, share)), vm((8, D + 128), F32),
        vm((640, D)), vm((256, D)), vm((D, hidden)), vm((hidden, D)),
        vm((nf, 8, D + 128), F32), vm((8, D + 128), F32),
        vm((micro * L, D)), vm((micro * R, D)),
        vm((3, micro, 1, R), jnp.int32), vm((micro, 6, BLK, BLK), jnp.int32),
        vm((micro, 6, HEADS_HERE, BLK, BLK)),
        vm((micro, HEADS_HERE * R, 256)), vm((micro * L, 384)),
        vm((micro * L, HEADS_HERE * R)), vm((L, HEADS_HERE * R), F32), vm((L, HEADS_HERE * R)),
        vm((micro, 256, R), F32), vm((micro, 8, HEADS_HERE * R), F32), vm((micro * R, 256)),
        vm((6, 2, T, D), F32), vm((nc, 2, T, D)),
        vm((3 + nc, 2, T, D)), vm((3 + nc, T, D)), vm((rids, 2, T, D)), vm((rids, T, D)),
        vm((nc - 1, T, D)), vm((micro, nc + 1, T, D)), vm((micro, T, D), F32),
        vm((micro * R, D)), vm((micro * R, hidden)), vm((micro * R, hidden)), vm((micro * R, D)),
        vm((micro, T, D), F32), vm((micro, T, D), F32), vm((micro * R, 256)),
        vm((256, HEADS_HERE * R)), vm((micro, 6, HEADS_HERE, BLK, BLK)), vm((640, D), F32),
        vm((HEADS_HERE, 32, 8, 128), F32), vm((2, 8, HEADS_HERE * R), F32), vm((8, D), F32),
        vm((nf - 1, chunk_rows, wide)), vm((nf - 1, chunk_rows, wide)),
        vm((chunk_rows, wide)), vm((chunk_rows, wide)),
        vm((4, 8, D + 128), F32), vm((1 + nf + nc - 1, 8, D + 128), F32),
        pltpu.SemaphoreType.DMA((n_sems,)), pltpu.SemaphoreType.DMA((n_sems,)),
        pltpu.SemaphoreType.DMA((8 + micro + len(chunks),)),
    ]


def finish_kernel(
    share, hidden, out_low, in_low, grads, sums,
    out, grad_in, gain_one, gain_two, grad_q, grad_k, grad_v, grad_o, grad_i, grad_b, grad_t, turned,
):
    out[:, 0] = out_low[...]
    grad_in[:, 0] = in_low[...]
    gain_one[...] = sums[0:1, 0:share].reshape(share)
    gain_two[...] = sums[1:2, 0:share].reshape(share)
    turned[...] = jnp.transpose(
        jnp.concatenate([sums[:, pl.ds(D, 128)], jnp.zeros((120, 128), F32)], axis=0)
    )
    here = grad_t.shape[1]
    part = turned[pl.ds(pl.multiple_of(lax.axis_index("fsdp") * here, here), here)]
    part = jnp.transpose(jnp.concatenate([part, jnp.zeros((128 - here, 128), F32)], axis=0))
    grad_t[...] = part[0:HEADS_HERE, 0:here]
    chunks, unused = grad_chunks(share, hidden)
    for name, row, rows, cols in chunks:
        value = grads[pl.ds(row, rows), 0:cols].astype(F32)
        if name.startswith("back"):
            grad_b[pl.ds(int(name[4:]) * BACK_PART, BACK_PART)] = value
        elif name.startswith("in"):
            grad_i[:, pl.ds(int(name[2:]) * PART, PART)] = value
        else:
            {"query": grad_q, "key": grad_k, "value": grad_v, "out": grad_o}[name][...] = value


def per_device(
    nf, nc,
    tokens, positions, w_query, w_key, w_value, w_out, w_in, w_back, gain_one, gain_two, bias_table, cotangent,
):
    micro, T = tokens.shape[0], tokens.shape[2]
    share, hidden = w_in.shape
    chunks, chunk_rows = grad_chunks(share, hidden)
    wide = max(384, share)
    n_sems = 352
    sems = Sems()
    vmem, anywhere = pl.BlockSpec(memory_space=pltpu.VMEM), pl.BlockSpec(memory_space=pl.ANY)
    low = pl.pallas_call(
        functools.partial(layer_kernel, nf, nc, micro, T, share, hidden, n_sems, sems),
        out_shape=[
            jax.ShapeDtypeStruct((micro, T, D), BF16),
            jax.ShapeDtypeStruct((micro, T, D), BF16),
            jax.ShapeDtypeStruct((chunk_rows, wide), BF16),
            jax.ShapeDtypeStruct((8, D + 128), F32),
        ],
        in_specs=[vmem] * 2 + [anywhere] * 6 + [vmem] * 3 + [anywhere],
        out_specs=[vmem, vmem, anywhere, vmem],
        scratch_shapes=kernel_scratch(nf, nc, micro, T, share, hidden, n_sems),
        compiler_params=pltpu.CompilerParams(
            collective_id=0, has_side_effects=True, vmem_limit_bytes=61800 * 1024
        ),
    )(
        tokens[:, 0], positions, w_query.T, w_key.T, w_value.T, w_out, w_in, w_back,
        gain_one, gain_two, bias_table.T, cotangent[:, 0],
    )
    shapes = [
        (tokens.shape, BF16), (tokens.shape, BF16), (gain_one.shape, F32), (gain_two.shape, F32),
        (w_query.T.shape, F32), (w_key.T.shape, F32), (w_value.T.shape, F32), (w_out.shape, F32),
        (w_in.shape, F32), (w_back.shape, F32), (bias_table.T.shape, F32),
    ]
    done = pl.pallas_call(
        functools.partial(finish_kernel, share, hidden),
        out_shape=[jax.ShapeDtypeStruct(shape, kind) for shape, kind in shapes],
        in_specs=[vmem] * 4,
        out_specs=[vmem] * len(shapes),
        scratch_shapes=[pltpu.VMEM((128, 128), F32)],
        compiler_params=pltpu.CompilerParams(vmem_limit_bytes=61800 * 1024),
    )(*low)
    return tuple(x.T if i in (4, 5, 6, 10) else x for i, x in enumerate(done))


def solution(mesh):
    nf, nc = mesh.shape["fsdp"], mesh.shape["ctx"]
    fits = D // nf % BLK == 0 and nc <= 4 and nc % 2 == 0 and mesh.shape["tp"] == 4
    return jax.shard_map(
        functools.partial(per_device, nf, nc) if fits else per_device_plain,
        mesh=mesh,
        in_specs=(
            P(None, "fsdp", ("ctx", "tp"), None),
            P(None, "fsdp", "ctx"),
            P("fsdp", "tp"),
            P("fsdp", "tp"),
            P("fsdp", "tp"),
            P("tp", "fsdp"),
            P("fsdp", "tp"),
            P("tp", "fsdp"),
            P("fsdp"),
            P("fsdp"),
            P("fsdp", "tp"),
            P(None, "fsdp", ("ctx", "tp"), None),
        ),
        out_specs=(
            P(None, "fsdp", ("ctx", "tp"), None),
            P(None, "fsdp", ("ctx", "tp"), None),
            P("fsdp"),
            P("fsdp"),
            P("fsdp", "tp"),
            P("fsdp", "tp"),
            P("fsdp", "tp"),
            P("tp", "fsdp"),
            P("fsdp", "tp"),
            P("tp", "fsdp"),
            P("fsdp", "tp"),
        ),
        check_vma=False,
    )
```
